256 devices in a mesh: lon: 32 (over z, x_lo, core), lat: 8 (over y, x_hi).
Axes of the slice: x: 4 (x_hi: 2, x_lo: 2; x = x_hi * 2 + x_lo), y: 4, z: 8, core: 2. Of those that a mesh axis runs over, the one named last changes fastest.
Arguments:
- ocean_state: bfloat16 [256, 64, 4096], P(None, 'lat', 'lon'), may hold values from -6 to 6
- land_mask: int32 [64, 4096], P('lat', 'lon'), may hold values from 0 to 1, as said below
- kernel: bfloat16 [49, 256], replicated, may hold values from -2 to 2
- w_in: bfloat16 [256, 1024], replicated, may hold values from -0.375 to 0.375
- w_out: bfloat16 [1024, 256], replicated, may hold values from -0.1875 to 0.1875
- cotangent: bfloat16 [256, 64, 4096], P(None, 'lat', 'lon'), may hold values from -6 to 6
Outputs:
- stepped: bfloat16 [256, 64, 4096], P(None, 'lat', 'lon')
- grad_state: bfloat16 [256, 64, 4096], P(None, 'lat', 'lon')
- grad_kernel: float32 [49, 256], replicated
- grad_w_in: float32 [256, 1024], replicated
- grad_w_out: float32 [1024, 256], replicated
The draws below stay inside these ranges and needn't reach their ends.
Inputs may be any that keep to these rules, and one draw needn't show every extreme that they name: `land_mask`: 1 marks an ocean cell, 0 a land cell.
All inputs are finite; a program needn't handle non-finite values.
Results may differ from the reference program's by a relative error of at most 0.0058.
Values may be sent and summed in bfloat16 or wider, within the bound.
A program may use at most 128 MiB of HBM per device.

```python
import jax
import jax.numpy as jnp
from jax import lax

C = 256
HID = 1024
TAPS = 49
CLON = 128
NLAT = 64
NLON = 4096


def draw_land_mask(key, part):
    key = jax.random.fold_in(key, 11)
    level_key, roll_key, cell_key = jax.random.split(key, 3)
    blocks = NLON // CLON
    land_level = jax.random.randint(level_key, (1, blocks), 0, 5)
    tile_roll = jax.random.randint(roll_key, (NLAT, blocks), 0, 8)
    cell_bits = jax.random.randint(cell_key, (NLAT, blocks, CLON), 0, 2)
    all_land = (tile_roll < land_level)[..., None]
    all_ocean = (tile_roll >= land_level + 2)[..., None]
    mask_out = jnp.where(all_land, 0, jnp.where(all_ocean, 1, cell_bits))
    return mask_out.reshape(NLAT, NLON).astype(jnp.int32)


def draw_kernel(key, part):
    key = jax.random.fold_in(key, 7)
    tap_key, scale_key = jax.random.split(key)
    tap_values = jnp.clip(jax.random.normal(tap_key, (TAPS, C), jnp.float32), -4.0, 4.0)
    chan_scale = jnp.exp(jax.random.uniform(scale_key, (1, C), jnp.float32, -1.15, 1.15))
    return (tap_values * chan_scale / 7.0).astype(jnp.bfloat16)


def shard_levels(own_key, extent, cuts, least, top_value):
    level = 1.0
    for dim, blocks in cuts:
        steps = jax.random.uniform(jax.random.fold_in(jax.random.fold_in(own_key, 6), dim), (blocks,), jnp.float32, least / len(cuts), top_value / len(cuts))
        level = level * jnp.repeat(jnp.exp(steps), extent[dim] // blocks).reshape((-1,) + (1,) * (len(extent) - 1 - dim))
    return level


def gaussian(stream_key, dims, width, bound, shards=(), held_as=jnp.bfloat16):
    drawn = width * jax.random.normal(stream_key, dims, jnp.float32)
    if shards:
        drawn = drawn * shard_levels(stream_key, dims, shards, -0.22, 0.18)
    return jnp.clip(drawn, -bound, bound).astype(held_as)


def setup_inputs(seed: int = 0) -> dict:
    streams_of = jax.random.split(jax.random.key(seed), 7)
    ocean_state = gaussian(streams_of[0], (C, NLAT, NLON), 1.0, 6.0, ((1, 8), (2, 32)))
    land_mask = draw_land_mask(jax.random.fold_in(streams_of[6], 71), 0)
    kernel = draw_kernel(jax.random.fold_in(streams_of[6], 71), 0)
    w_in = gaussian(streams_of[3], (C, HID), C ** -0.5, 0.375)
    w_out = gaussian(streams_of[4], (HID, C), HID ** -0.5, 0.1875)
    cotangent = gaussian(streams_of[5], (C, NLAT, NLON), 1.0, 6.0, ((1, 8), (2, 32)))
    return dict(ocean_state=ocean_state, land_mask=land_mask, kernel=kernel, w_in=w_in, w_out=w_out, cotangent=cotangent)


tanh_slope = 0.7978845608028654
cubic_coef = 0.044715
norm_eps = 1e-06

def gelu_pair(inputs):
    inner_arg = tanh_slope * (inputs + cubic_coef * inputs * inputs * inputs)
    tanh_val = jnp.tanh(inner_arg)
    result = 0.5 * inputs * (1.0 + tanh_val)
    derivative = 0.5 * (1.0 + tanh_val) + 0.5 * inputs * (1.0 - tanh_val * tanh_val) * tanh_slope * (1.0 + 3.0 * cubic_coef * inputs * inputs)
    return (result, derivative)

def correlate(source, tap_weights):
    row_count = source.shape[1] - 6
    col_count = source.shape[2] - 6
    summed = jnp.zeros((source.shape[0], row_count, col_count), tap_weights.dtype)
    for tap_row in range(7):
        for tap_col in range(7):
            weight_col = tap_weights[tap_row * 7 + tap_col][:, None, None]
            window = source[:, tap_row:tap_row + row_count, tap_col:tap_col + col_count].astype(tap_weights.dtype)
            summed = summed + weight_col * window
    return summed

def kernel_grad(grad_field, source, float_type):
    row_count = grad_field.shape[1]
    col_count = grad_field.shape[2]
    grad_wide = grad_field.astype(float_type)
    tap_sums = []
    for tap_row in range(7):
        for tap_col in range(7):
            window = source[:, tap_row:tap_row + row_count, tap_col:tap_col + col_count].astype(float_type)
            tap_sums.append(lax.optimization_barrier(jnp.sum(grad_wide * window, axis=(1, 2))))
    return jnp.stack(tap_sums)

def spread_taps(grad_field, tap_weights):
    padded = jnp.pad(grad_field, ((0, 0), (6, 6), (6, 6)))
    return correlate(padded, tap_weights[::-1])

def cell_block(conv_out, state_cells, mask_cells, cot_cells, w_in, w_out):
    chan_mean = lax.optimization_barrier(jnp.mean(conv_out, axis=0, keepdims=True))
    centred = conv_out - chan_mean
    chan_var = lax.optimization_barrier(jnp.mean(centred * centred, axis=0, keepdims=True))
    inv_std = lax.rsqrt(chan_var + norm_eps)
    x_hat = centred * inv_std
    normed = x_hat.astype(jnp.bfloat16)
    pre_act = lax.dot_general(w_in, normed, (((0,), (0,)), ((), ())), preferred_element_type=jnp.float32)
    act_f32, derivative = gelu_pair(pre_act)
    activated = act_f32.astype(jnp.bfloat16)
    branch = lax.dot_general(w_out, activated, (((0,), (0,)), ((), ())), preferred_element_type=jnp.float32)
    ocean_f = mask_cells.astype(jnp.float32)
    stepped = (state_cells.astype(jnp.float32) + ocean_f * branch).astype(jnp.bfloat16)
    g_branch = (ocean_f * cot_cells.astype(jnp.float32)).astype(jnp.bfloat16)
    grad_out = lax.dot_general(activated, g_branch, (((1,), (1,)), ((), ())), preferred_element_type=jnp.float32)
    g_act = jnp.dot(w_out, g_branch, preferred_element_type=jnp.float32)
    g_pre = (g_act * derivative).astype(jnp.bfloat16)
    grad_in = lax.dot_general(normed, g_pre, (((1,), (1,)), ((), ())), preferred_element_type=jnp.float32)
    g_norm = jnp.dot(w_in, g_pre, preferred_element_type=jnp.float32)
    g_mean = lax.optimization_barrier(jnp.mean(g_norm, axis=0, keepdims=True))
    g_proj = lax.optimization_barrier(jnp.mean(g_norm * x_hat, axis=0, keepdims=True))
    g_conv = (inv_std * (g_norm - g_mean - x_hat * g_proj)).astype(jnp.bfloat16)
    return (stepped, g_conv, grad_in, grad_out)

def reference(ocean_state, land_mask, kernel, w_in, w_out, cotangent):
    channels, lat_rows, lon_cols = ocean_state.shape
    blocks = lon_cols // CLON
    partner = (blocks - 1 - jnp.arange(blocks)).astype(jnp.int32)
    tap_weights = kernel.astype(jnp.float32)
    lon_tiles = ocean_state.reshape(channels, lat_rows, blocks, CLON).transpose(2, 0, 1, 3)
    widened = jnp.concatenate([jnp.roll(lon_tiles, 1, axis=0)[..., CLON - 3:], lon_tiles, jnp.roll(lon_tiles, -1, axis=0)[..., :3]], axis=3)
    crown_rows = jnp.take(widened[:, :, lat_rows - 3:, :], partner, axis=0)[:, :, ::-1, ::-1]
    floor_rows = jnp.zeros((blocks, channels, 3, CLON + 6), jnp.bfloat16)
    extended = jnp.concatenate([floor_rows, widened, crown_rows], axis=2)
    mask_tiles = land_mask.reshape(lat_rows, blocks, CLON).transpose(1, 0, 2)
    cot_tiles = cotangent.reshape(channels, lat_rows, blocks, CLON).transpose(2, 0, 1, 3)
    cell_count = lat_rows * CLON

    def one_block(block_items):
        ext_b, state_b, mask_b, cot_b = block_items
        ext_f = ext_b.astype(jnp.float32)
        conv_out = correlate(ext_f, tap_weights)
        stepped, g_conv, grad_in, grad_out = cell_block(conv_out.reshape(channels, cell_count), state_b.reshape(channels, cell_count), mask_b.reshape(1, cell_count), cot_b.reshape(channels, cell_count), w_in, w_out)
        g_field = g_conv.reshape(channels, lat_rows, CLON).astype(jnp.float32)
        grad_k = kernel_grad(g_field, ext_f, jnp.float32)
        spread_b = spread_taps(g_field, tap_weights)
        return (stepped.reshape(channels, lat_rows, CLON), spread_b, grad_k, grad_in, grad_out)
    stepped_tiles, spread_tiles, kernel_parts, in_parts, out_parts = lax.map(one_block, (extended, lon_tiles, mask_tiles, cot_tiles))
    core_rows = spread_tiles[:, :, 3:lat_rows + 3, :]
    folded = lax.optimization_barrier(spread_tiles[:, :, lat_rows + 3:, :].astype(jnp.bfloat16)).astype(jnp.float32)[:, :, ::-1, ::-1]
    core_rows = core_rows.at[:, :, lat_rows - 3:, :].add(jnp.take(folded, partner, axis=0))
    middle = core_rows[..., 3:CLON + 3]
    middle = middle.at[..., :3].add(jnp.roll(core_rows, 1, axis=0)[..., CLON + 3:])
    middle = middle.at[..., CLON - 3:].add(jnp.roll(core_rows, -1, axis=0)[..., :3])
    middle = middle.transpose(1, 2, 0, 3).reshape(channels, lat_rows, lon_cols)
    grad_state = (cotangent.astype(jnp.float32) + middle).astype(jnp.bfloat16)
    stepped = stepped_tiles.transpose(1, 2, 0, 3).reshape(channels, lat_rows, lon_cols)
    return (stepped, grad_state, lax.optimization_barrier(jnp.sum(kernel_parts, axis=0)), lax.optimization_barrier(jnp.sum(in_parts, axis=0)), lax.optimization_barrier(jnp.sum(out_parts, axis=0)))
```

```python
import functools

import jax
import jax.numpy as jnp
from jax import lax
from jax.experimental import pallas as pl
from jax.experimental.pallas import tpu as pltpu
from jax.sharding import PartitionSpec as P

F32 = jnp.float32
BF16 = jnp.bfloat16
MESH = pl.DeviceIdType.MESH
TANH_SLOPE = 0.7978845608028654
CUBIC = 0.044715
EPS = 1e-06
C = 256
HID = 1024
ROWS = 8
COLS = 128
CELLS = ROWS * COLS
HALF = 2048
VMEM_LIMIT = 56 * 1024 * 1024
VSPEC = pl.BlockSpec(memory_space=pltpu.VMEM)


def al(value, multiple):
    return pl.multiple_of(value, multiple)


def lanes(rows):
    return lax.broadcasted_iota(jnp.int32, (rows, COLS), 1)


def pick(flag, yes, no):
    return flag * yes + (1 - flag) * no


class Place:
    def __init__(self, n_lon, n_lat):
        self.n_lon, self.n_lat = n_lon, n_lat
        self.lon = lax.axis_index("lon")
        self.lat = lax.axis_index("lat")
        self.crown = (self.lat == n_lat - 1).astype(jnp.int32)
        self.floor = (self.lat == 0).astype(jnp.int32)
        east = lax.rem(self.lon + 1, n_lon)
        west = lax.rem(self.lon + n_lon - 1, n_lon)
        north = pick(self.crown, self.lat, self.lat + 1)
        south = lax.rem(self.lat + n_lat - 1, n_lat)
        mirror = n_lon - 1 - self.lon
        self.west_id = {"lon": west, "lat": self.lat}
        self.east_id = {"lon": east, "lat": self.lat}
        self.north_id = {"lon": pick(self.crown, mirror, self.lon), "lat": north}
        self.south_id = {"lon": self.lon, "lat": south}
        nw = pick(self.crown, lax.rem(n_lon - self.lon, n_lon), west)
        ne = pick(self.crown, lax.rem(2 * n_lon - 2 - self.lon, n_lon), east)
        self.nw_self = (self.crown == 1) & (nw == self.lon)
        self.ne_self = (self.crown == 1) & (ne == self.lon)
        self.nw_id = {"lon": nw, "lat": north}
        self.ne_id = {"lon": ne, "lat": north}
        self.sw_id = {"lon": west, "lat": south}
        self.se_id = {"lon": east, "lat": south}
        self.core = lax.rem(self.lon, 2)
        self.xl = lax.rem(self.lon // 2, 2)
        self.zi = self.lon // 4
        self.n_xy, self.n_z = 2 * n_lat, n_lon // 4
        self.xy = self.lat * 2 + self.xl
        self.core_id = {"lon": self.lon + 1 - 2 * self.core, "lat": self.lat}

    def xy_peer(self, step):
        peer = lax.rem(self.xy + step, self.n_xy)
        return peer, {"lon": self.zi * 4 + lax.rem(peer, 2) * 2 + self.core, "lat": peer // 2}

    def z_peer(self, step):
        peer = lax.rem(self.zi + step, self.n_z)
        return peer, {"lon": peer * 4 + self.xl * 2 + self.core, "lat": self.lat}


def signal(barrier, device):
    pl.semaphore_signal(barrier, inc=1, device_id=device, device_id_type=MESH)


def greet_halo(place, barrier):
    for device in (place.west_id, place.east_id, place.north_id):
        signal(barrier, device)

    @pl.when(jnp.logical_not(place.nw_self))
    def _():
        signal(barrier, place.nw_id)

    @pl.when(jnp.logical_not(place.ne_self))
    def _():
        signal(barrier, place.ne_id)

    @pl.when(place.floor == 0)
    def _():
        for device in (place.south_id, place.sw_id, place.se_id):
            signal(barrier, device)

    return (
        5
        - place.nw_self.astype(jnp.int32)
        - place.ne_self.astype(jnp.int32)
        + 3 * (1 - place.floor)
    )


def halo_copies(place, rows_ref, t_ref, halo_ref, rt_ref, send_sem, recv_sem):
    crown = place.crown

    def remote(src, dst, index, slot, device):
        return pltpu.make_async_remote_copy(
            src_ref=src,
            dst_ref=dst,
            send_sem=send_sem.at[index],
            recv_sem=recv_sem.at[slot],
            device_id=device,
            device_id_type=MESH,
        )

    return [
        remote(t_ref, rt_ref.at[1, pl.ds(1, 2)], 0, 0, place.west_id),
        remote(t_ref, rt_ref.at[0, pl.ds(1, 2)], 1, 1, place.east_id),
        remote(rows_ref.at[pl.ds(5, 3)], halo_ref.at[crown], 2, 2 + crown, place.north_id),
        remote(rows_ref.at[pl.ds(0, 3)], halo_ref.at[1], 3, 3, place.south_id),
        remote(t_ref.at[1], rt_ref.at[1 - crown, 3 * crown], 4, 4 + 3 * crown, place.nw_id),
        remote(t_ref.at[1], rt_ref.at[crown, 3 * crown], 5, 5 + crown, place.ne_id),
        remote(t_ref.at[0], rt_ref.at[1, 3], 6, 6, place.sw_id),
        remote(t_ref.at[0], rt_ref.at[0, 3], 7, 7, place.se_id),
    ]


def halo_start(place, copies, t_ref, rt_ref, recv_sem):
    for index in (2, 0, 1):
        copies[index].start()

    @pl.when(place.floor == 0)
    def _():
        copies[3].start()
        copies[6].start()
        copies[7].start()

    for is_self, index, side, slot in ((place.nw_self, 4, 0, 7), (place.ne_self, 5, 1, 6)):

        @pl.when(is_self)
        def _(side=side, slot=slot):
            pltpu.make_async_copy(t_ref.at[1], rt_ref.at[side, 3], recv_sem.at[slot]).start()

        @pl.when(jnp.logical_not(is_self))
        def _(index=index):
            copies[index].start()


def wait_bytes(ref, sem):
    pltpu.make_async_copy(ref, ref, sem).wait()


def halo_wait(place, copies, t_ref, halo_ref, rt_ref, recv_sem):
    wait_bytes(rt_ref.at[1, pl.ds(1, 2)], recv_sem.at[0])
    wait_bytes(rt_ref.at[0, pl.ds(1, 2)], recv_sem.at[1])
    wait_bytes(halo_ref.at[1], recv_sem.at[3])
    wait_bytes(rt_ref.at[1, 3], recv_sem.at[6])
    wait_bytes(rt_ref.at[0, 3], recv_sem.at[7])

    @pl.when(place.floor == 0)
    def _():
        wait_bytes(halo_ref.at[0], recv_sem.at[2])
        wait_bytes(rt_ref.at[1, 0], recv_sem.at[4])
        wait_bytes(rt_ref.at[0, 0], recv_sem.at[5])


def halo_sent(place, copies):
    for index in (0, 1, 2):
        copies[index].wait_send()

    @pl.when(place.floor == 0)
    def _():
        for index in (3, 6, 7):
            copies[index].wait_send()

    for is_self, index in ((place.nw_self, 4), (place.ne_self, 5)):

        @pl.when(jnp.logical_not(is_self))
        def _(index=index):
            copies[index].wait_send()


def pack_group(values, group, rows_bf, edge_ref):
    lane = lanes(16)
    edge = (lane < 3) | (lane >= COLS - 3)
    packed = None
    at = pl.ds(al(group * 16, 16), 16)
    for r in range(ROWS):
        rows_bf[r, at, :] = values[r].astype(BF16)
        part = pltpu.roll(jnp.where(edge, values[r], 0.0), 8 * r + 4, 1)
        packed = part if packed is None else packed + part
    edge_ref[at, :] = packed


def pack_finish(edge_ref, t_ref):
    turned = edge_ref[...].T
    t_ref[0] = turned[:32].astype(BF16)
    t_ref[1] = turned[32:64].astype(BF16)


def unpack(place, halo_ref, rt_ref, ext_ref, rim_ref):
    crown = place.crown == 1
    source = lax.broadcasted_iota(jnp.int32, (COLS, COLS), 0)
    target = lax.broadcasted_iota(jnp.int32, (COLS, COLS), 1)
    turn = jnp.where(crown, COLS - 1 - source, source) == target
    turn = jnp.where(turn, 1.0, 0.0).astype(BF16)
    for k in range(3):
        ext_ref[k] = jnp.where(place.floor == 1, 0.0, halo_ref[0, k].astype(F32))
        row = halo_ref[1, pick(place.crown, 2 - k, k)]
        ext_ref[3 + k] = jnp.dot(row, turn, preferred_element_type=F32)
    blocks = []
    slot = lax.rem(lax.broadcasted_iota(jnp.int32, (32, C), 0), 8)
    for b in range(4):
        west, east = rt_ref[0, b].astype(F32), rt_ref[1, b].astype(F32)
        if b < 3:
            block = jnp.where(slot < 4, west, east)
        else:
            block = jnp.where((slot < 4) != crown, west, east)
        if b == 0:
            block = jnp.where(place.floor == 1, 0.0, block)
        blocks.append(block)
    rim = jnp.concatenate(blocks, axis=0).T.astype(BF16)
    last = jnp.where(crown & (source >= 96), 223 - source, source) == target
    last = jnp.where(last, 1.0, 0.0).astype(BF16)
    rim_ref[...] = jnp.dot(rim, last, preferred_element_type=F32)


def halo_kernel(n_lon, n_lat, x_ref, rows_ref, ext_ref, rim_ref, xf, rows_bf, edge, t_ref, halo, rt, send_sem, recv_sem):
    place = Place(n_lon, n_lat)
    barrier = pltpu.get_barrier_semaphore()
    count = greet_halo(place, barrier)

    def body(group, _):
        values = x_ref[pl.ds(group * 16, 16)].astype(F32).reshape(128, COLS)
        xf[pl.ds(al(group * 128, 128), 128), :] = values
        picked = [xf[pl.ds(group * 128 + r, 16, stride=8), :] for r in range(ROWS)]
        for r in range(ROWS):
            rows_ref[r, pl.ds(al(group * 16, 16), 16), :] = picked[r]
        pack_group(picked, group, rows_bf, edge)
        return 0

    lax.fori_loop(0, C // 16, body, 0)
    pack_finish(edge, t_ref)
    pl.semaphore_wait(barrier, count)
    copies = halo_copies(place, rows_bf, t_ref, halo, rt, send_sem, recv_sem)
    halo_start(place, copies, t_ref, rt, recv_sem)
    halo_wait(place, copies, t_ref, halo, rt, recv_sem)
    unpack(place, halo, rt, ext_ref, rim_ref)
    halo_sent(place, copies)


HALO_SCRATCH = [
    pltpu.VMEM((ROWS, C, COLS), BF16),
    pltpu.VMEM((C, COLS), F32),
    pltpu.VMEM((2, 32, C), BF16),
    pltpu.VMEM((2, 3, C, COLS), BF16),
    pltpu.VMEM((2, 4, 32, C), BF16),
    pltpu.SemaphoreType.DMA((8,)),
    pltpu.SemaphoreType.DMA((8,)),
]


def halo_call(x, n_lon, n_lat):
    return pl.pallas_call(
        functools.partial(halo_kernel, n_lon, n_lat),
        out_shape=(
            jax.ShapeDtypeStruct((ROWS, C, COLS), F32),
            jax.ShapeDtypeStruct((6, C, COLS), F32),
            jax.ShapeDtypeStruct((C, COLS), F32),
        ),
        in_specs=[VSPEC],
        out_specs=(VSPEC,) * 3,
        scratch_shapes=[pltpu.VMEM((C * ROWS, COLS), F32)] + HALO_SCRATCH,
        compiler_params=pltpu.CompilerParams(
            collective_id=0, has_side_effects=True, vmem_limit_bytes=VMEM_LIMIT
        ),
        name="halo_in",
    )(x)


def ext_row(rows_ref, ext_ref, r, at):
    if r < 3:
        return ext_ref[r, at, :]
    if r < 11:
        return rows_ref[r - 3, at, :]
    return ext_ref[r - 8, at, :]


def shifted(x, beside, d, lane):
    if d == 0:
        return x
    if d > 0:
        return pltpu.roll(jnp.where(lane < d, beside, x), COLS - d, 1)
    return pltpu.roll(jnp.where(lane >= COLS + d, beside, x), -d, 1)


def beside_row(rim, r):
    return pltpu.roll(rim, COLS - (8 * (r + 1) + 4) if r < 15 else 0, 1)


def conv_group(rows_ref, ext_ref, rim_ref, taps, north, group):
    at = pl.ds(al(group * 8, 8), 8)
    lane = lanes(8)
    rim = rim_ref[at, :]
    beside = [beside_row(rim, r) for r in range(14)]
    table = taps[at, :]
    table_n = table if north is None else north[at, :]
    total = [None] * ROWS
    for q in range(7):
        weight = [jnp.broadcast_to(table[:, 7 * a + q : 7 * a + q + 1], (8, COLS)) for a in range(7)]
        if north is None:
            weight_n = weight
        else:
            weight_n = [
                None if a < 4 else jnp.broadcast_to(table_n[:, 7 * a + q : 7 * a + q + 1], (8, COLS))
                for a in range(7)
            ]
        for r in range(14):
            moved = shifted(ext_row(rows_ref, ext_ref, r, at), beside[r], q - 3, lane)
            for a in range(7):
                i = r - a
                if 0 <= i < ROWS:
                    term = (weight_n if r >= 11 else weight)[a] * moved
                    total[i] = term if total[i] is None else total[i] + term
    return total


def tap_tables(taps_ref, pad_ref, fwd_ref, bwd_ref=None, north_ref=None, crown=None):
    pad_ref[...] = jnp.zeros_like(pad_ref)
    pad_ref[pl.ds(0, 49), :] = taps_ref[...].astype(F32)
    turned = pad_ref[...].T
    if fwd_ref is not None:
        fwd_ref[...] = turned
    if bwd_ref is not None:
        source = lax.broadcasted_iota(jnp.int32, (COLS, COLS), 0)
        target = lax.broadcasted_iota(jnp.int32, (COLS, COLS), 1)
        flip = jnp.where(source + target == 48, 1.0, 0.0).astype(BF16)
        flipped = jnp.dot(turned.astype(BF16), flip, preferred_element_type=F32)
        bwd_ref[...] = flipped
        north_ref[...] = jnp.where(crown, turned, flipped)


def block_kernel(
    rows_ref, ext_ref, rim_ref, mask_ref, taps_ref, w_in_ref, w_out_ref, cot_ref,
    stepped_ref, g_ref, grads_ref, gk_ref,
    pad, taps, w_in_t, w_out_t, conv, normed, gb, act, g_pre, g_norm, inv_ref, flat, gk_t,
):
    tap_tables(taps_ref, pad, taps)
    w_in_t[...] = w_in_ref[...].astype(F32).T.astype(BF16)
    w_out_t[...] = w_out_ref[...].astype(F32).T.astype(BF16)

    flat[...] = cot_ref[...].astype(F32).reshape(C * ROWS, COLS)
    for r in range(ROWS):
        ocean = mask_ref[pl.ds(r, 1), :].astype(F32)
        gb[:, r * COLS : (r + 1) * COLS] = (ocean * flat[pl.ds(r, C, stride=8), :]).astype(BF16)

    def conv_body(group, _):
        out = conv_group(rows_ref, ext_ref, rim_ref, taps, None, group)
        for i in range(ROWS):
            conv[pl.ds(al(group * 8, 8), 8), i * COLS : (i + 1) * COLS] = out[i]
        return 0

    lax.fori_loop(0, C // 8, conv_body, 0)

    for r in range(ROWS):
        at = slice(r * COLS, (r + 1) * COLS)
        value = conv[:, at]
        centred = value - jnp.sum(value, axis=0, keepdims=True) * (1.0 / C)
        var = jnp.sum(centred * centred, axis=0, keepdims=True) * (1.0 / C)
        inv = lax.rsqrt(var + EPS)
        inv_ref[pl.ds(r, 1), :] = inv
        x_hat = centred * inv
        conv[:, at] = x_hat
        normed[:, at] = x_hat.astype(BF16)

    def cells_body(n, _):
        at = pl.ds(al(n * 256, 256), 256)
        hat = normed[:, at]
        grad = gb[:, at]
        for h in range(4):
            hs = slice(h * 256, (h + 1) * 256)
            u = jnp.dot(w_in_t[hs, :], hat, preferred_element_type=F32)
            uu = u * u
            t = jnp.tanh(TANH_SLOPE * (u + CUBIC * (uu * u)))
            gate = 0.5 * (1.0 + t)
            act[hs, at] = (u * gate).astype(BF16)
            slope = gate + (0.5 * TANH_SLOPE) * u * (1.0 - t * t) * (1.0 + (3.0 * CUBIC) * uu)
            g_act = jnp.dot(w_out_ref[hs, :], grad, preferred_element_type=F32)
            g_pre[hs, at] = (g_act * slope).astype(BF16)
        g_norm[:, at] = jnp.dot(w_in_ref[...], g_pre[:, at], preferred_element_type=F32)
        branch = jnp.dot(w_out_t[...], act[:, at], preferred_element_type=F32)
        for k in range(2):
            r = 2 * n + k
            ocean = mask_ref[pl.ds(r, 1), :].astype(F32)
            flat[pl.ds(r, C, stride=8), :] = rows_ref[r] + ocean * branch[:, k * COLS : (k + 1) * COLS]
        return 0

    lax.fori_loop(0, CELLS // 256, cells_body, 0)

    def out_body(group, _):
        stepped_ref[pl.ds(group * 32, 32)] = flat[pl.ds(al(group * 256, 256), 256), :].reshape(32, ROWS, COLS).astype(BF16)
        return 0

    lax.fori_loop(0, C // 32, out_body, 0)

    nt = (((1,), (1,)), ((), ()))
    for h in range(4):
        hs = slice(h * 256, (h + 1) * 256)
        out = lax.dot_general(act[hs, :], gb[...], nt, preferred_element_type=F32).astype(BF16)
        grads_ref[h * 256 : (h + 1) * 256, :] = out[:, :COLS]
        grads_ref[1024 + h * 256 : 1024 + (h + 1) * 256, :] = out[:, COLS:]
    for h in range(4):
        hs = slice(h * 256, (h + 1) * 256)
        out = lax.dot_general(normed[...], g_pre[hs, :], nt, preferred_element_type=F32).astype(BF16)
        grads_ref[HALF + h * 512 : HALF + h * 512 + 256, :] = out[:, :COLS]
        grads_ref[HALF + h * 512 + 256 : HALF + (h + 1) * 512, :] = out[:, COLS:]

    for r in range(ROWS):
        at = slice(r * COLS, (r + 1) * COLS)
        grad, x_hat = g_norm[:, at], conv[:, at]
        mean = jnp.sum(grad, axis=0, keepdims=True) * (1.0 / C)
        proj = jnp.sum(grad * x_hat, axis=0, keepdims=True) * (1.0 / C)
        g_conv = inv_ref[pl.ds(r, 1), :] * (grad - mean - x_hat * proj)
        g_ref[r] = g_conv.astype(BF16).astype(F32)

    lane = lanes(8)

    def tap_body(group, _):
        at = pl.ds(al(group * 8, 8), 8)
        rim = rim_ref[at, :]
        beside = [beside_row(rim, r) for r in range(14)]
        grads = [g_ref[i, at, :] for i in range(ROWS)]
        out = jnp.zeros((8, COLS), F32)
        for q in range(7):
            total = [None] * 7
            for r in range(14):
                moved = shifted(ext_row(rows_ref, ext_ref, r, at), beside[r], q - 3, lane)
                for a in range(7):
                    i = r - a
                    if 0 <= i < ROWS:
                        term = grads[i] * moved
                        total[a] = term if total[a] is None else total[a] + term
            for a in range(7):
                out = jnp.where(lane == 7 * a + q, jnp.sum(total[a], axis=1, keepdims=True), out)
        gk_t[at, :] = out
        return 0

    lax.fori_loop(0, C // 8, tap_body, 0)
    turned = gk_t[...].T
    gk_ref[0] = turned[:64, :COLS].astype(BF16)
    gk_ref[1] = turned[:64, COLS:].astype(BF16)


def block_call(rows, ext, rim, mask, taps, w_in, w_out, cot):
    return pl.pallas_call(
        block_kernel,
        out_shape=(
            jax.ShapeDtypeStruct((C, ROWS, COLS), BF16),
            jax.ShapeDtypeStruct((ROWS, C, COLS), F32),
            jax.ShapeDtypeStruct((2 * HALF, COLS), BF16),
            jax.ShapeDtypeStruct((2, 64, COLS), BF16),
        ),
        in_specs=[VSPEC] * 8,
        out_specs=(VSPEC,) * 4,
        scratch_shapes=[
            pltpu.VMEM((COLS, C), F32),
            pltpu.VMEM((C, COLS), F32),
            pltpu.VMEM((HID, C), BF16),
            pltpu.VMEM((C, HID), BF16),
            pltpu.VMEM((C, CELLS), F32),
            pltpu.VMEM((C, CELLS), BF16),
            pltpu.VMEM((C, CELLS), BF16),
            pltpu.VMEM((HID, CELLS), BF16),
            pltpu.VMEM((HID, CELLS), BF16),
            pltpu.VMEM((C, CELLS), F32),
            pltpu.VMEM((ROWS, COLS), F32),
            pltpu.VMEM((C * ROWS, COLS), F32),
            pltpu.VMEM((C, COLS), F32),
        ],
        compiler_params=pltpu.CompilerParams(vmem_limit_bytes=VMEM_LIMIT),
        name="block",
    )(rows, ext, rim, mask, taps, w_in, w_out, cot)


def sum_kernel(
    n_lon, n_lat, g_ref, grads_ref, gk_ref, ext_ref, rim_ref, sums_ref, gk_out,
    rows_bf, edge, t_ref, halo, rt, send_sem, recv_sem,
    pair_in, mine, xy_in, part, z_in, done, gk_pair, gk_mine, gk_xy, gk_xy_mine, gk_z, gk_done, gk_last,
    core_sems, xy_sems, z_sems, zg_sems, xyg_sems, last_sems, gk_core, gk_xy_sems, gk_z_sems, gk_last_sems,
):
    place = Place(n_lon, n_lat)
    n_xy, n_z = place.n_xy, place.n_z
    rows_xy, rows_z = HALF // n_xy, HALF // n_xy // n_z
    barrier = pltpu.get_barrier_semaphore()
    count = greet_halo(place, barrier)
    signal(barrier, place.core_id)

    def greet_xy(step, _):
        signal(barrier, place.xy_peer(step)[1])
        return 0

    def greet_z(step, _):
        signal(barrier, place.z_peer(step)[1])
        return 0

    lax.fori_loop(1, n_xy, greet_xy, 0)
    lax.fori_loop(1, n_z, greet_z, 0)

    def body(group, _):
        at = pl.ds(al(group * 16, 16), 16)
        pack_group([g_ref[r, at, :] for r in range(ROWS)], group, rows_bf, edge)
        return 0

    lax.fori_loop(0, C // 16, body, 0)
    pack_finish(edge, t_ref)
    pl.semaphore_wait(barrier, count + n_xy + n_z - 1)

    def remote(src, dst, sems, index, device):
        return pltpu.make_async_remote_copy(
            src_ref=src, dst_ref=dst, send_sem=sems.at[0, index], recv_sem=sems.at[1, index],
            device_id=device, device_id_type=MESH,
        )

    copies = halo_copies(place, rows_bf, t_ref, halo, rt, send_sem, recv_sem)
    halo_start(place, copies, t_ref, rt, recv_sem)

    core, other = place.core, 1 - place.core
    first = remote(grads_ref.at[pl.ds(al(other * HALF, HALF), HALF)], pair_in, core_sems, 0, place.core_id)
    first_k = remote(gk_ref.at[other], gk_pair, gk_core, 0, place.core_id)
    first.start()
    first_k.start()
    first.wait()
    first_k.wait()

    def add_pair(i, _):
        at = pl.ds(al(i * 256, 256), 256)
        own = grads_ref[pl.ds(al(core * HALF + i * 256, 256), 256), :].astype(F32)
        mine[at, :] = (own + pair_in[at, :].astype(F32)).astype(BF16)
        return 0

    lax.fori_loop(0, HALF // 256, add_pair, 0)
    gk_mine[...] = (gk_ref[core].astype(F32) + gk_pair[...].astype(F32)).astype(BF16)

    def xy_copies(step):
        peer, device = place.xy_peer(step)
        return (
            remote(mine.at[pl.ds(al(peer * rows_xy, rows_xy), rows_xy)], xy_in.at[step], xy_sems, step, device),
            remote(gk_mine, gk_xy.at[step], gk_xy_sems, step, device),
        )

    def each(n, make, act):
        def run(step, _):
            for copy in make(step):
                act(copy)
            return 0

        lax.fori_loop(1, n, run, 0)

    def start(copy):
        copy.start()

    def wait(copy):
        copy.wait()

    each(n_xy, xy_copies, start)
    total = mine[pl.ds(al(place.xy * rows_xy, rows_xy), rows_xy), :].astype(F32)
    total_k = gk_mine[...].astype(F32)
    each(n_xy, xy_copies, wait)
    for step in range(1, n_xy):
        total = total + xy_in[step].astype(F32)
        total_k = total_k + gk_xy[step].astype(F32)
    part[...] = total.astype(BF16)
    gk_xy_mine[...] = total_k.astype(BF16)

    def z_copies(step):
        peer, device = place.z_peer(step)
        return (
            remote(part.at[pl.ds(al(peer * rows_z, rows_z), rows_z)], z_in.at[step], z_sems, step, device),
            remote(gk_xy_mine, gk_z.at[step], gk_z_sems, step, device),
        )

    each(n_z, z_copies, start)
    total = part[pl.ds(al(place.zi * rows_z, rows_z), rows_z), :].astype(F32)
    total_k = gk_xy_mine[...].astype(F32)
    each(n_z, z_copies, wait)
    for step in range(1, n_z):
        total = total + z_in[step].astype(F32)
        total_k = total_k + gk_z[step].astype(F32)
    done[place.xy, place.zi] = total.astype(BF16)
    gk_done[...] = total_k.astype(BF16)

    def zg_copies(step):
        _, device = place.z_peer(step)
        own = done.at[place.xy, place.zi]
        return (remote(own, own, zg_sems, step, device),)

    last_k = remote(gk_done, gk_last, gk_last_sems, 0, place.core_id)
    each(n_z, zg_copies, start)
    last_k.start()

    def zg_wait(step, _):
        sender = lax.rem(place.zi + n_z - step, n_z)
        wait_bytes(done.at[place.xy, sender], zg_sems.at[1, step])
        return 0

    lax.fori_loop(1, n_z, zg_wait, 0)

    def xyg_copies(step):
        _, device = place.xy_peer(step)
        own = done.at[place.xy]
        return (remote(own, own, xyg_sems, step, device),)

    def across(step, index):
        return remote(done.at[index], sums_ref.at[core, index], last_sems, step, place.core_id)

    each(n_xy, xyg_copies, start)
    across(0, place.xy).start()

    def xyg_wait(step, _):
        sender = lax.rem(place.xy + n_xy - step, n_xy)
        wait_bytes(done.at[sender], xyg_sems.at[1, step])
        across(step, sender).start()
        return 0

    lax.fori_loop(1, n_xy, xyg_wait, 0)
    sums_ref[core] = done[...]

    halo_wait(place, copies, t_ref, halo, rt, recv_sem)
    unpack(place, halo, rt, ext_ref, rim_ref)
    last_k.wait()
    gk_out[core] = gk_done[...]
    gk_out[other] = gk_last[...]

    def last_wait(step, _):
        sender = lax.rem(place.xy + n_xy - step, n_xy)
        wait_bytes(done.at[sender], last_sems.at[0, step])
        wait_bytes(sums_ref.at[other, sender], last_sems.at[1, step])
        return 0

    lax.fori_loop(0, n_xy, last_wait, 0)

    def sent(copy):
        copy.wait_send()

    each(n_z, zg_copies, sent)
    each(n_xy, xyg_copies, sent)
    halo_sent(place, copies)


def sum_call(g, grads, gk, n_lon, n_lat):
    n_xy, n_z = 2 * n_lat, n_lon // 4
    rows_xy, rows_z = HALF // n_xy, HALF // n_xy // n_z
    small = pltpu.VMEM((64, COLS), BF16)
    sems = lambda n: pltpu.SemaphoreType.DMA((2, n))
    return pl.pallas_call(
        functools.partial(sum_kernel, n_lon, n_lat),
        out_shape=(
            jax.ShapeDtypeStruct((6, C, COLS), F32),
            jax.ShapeDtypeStruct((C, COLS), F32),
            jax.ShapeDtypeStruct((2, n_xy, n_z, rows_z, COLS), BF16),
            jax.ShapeDtypeStruct((2, 64, COLS), BF16),
        ),
        in_specs=[VSPEC] * 3,
        out_specs=(VSPEC,) * 4,
        scratch_shapes=HALO_SCRATCH
        + [
            pltpu.VMEM((HALF, COLS), BF16),
            pltpu.VMEM((HALF, COLS), BF16),
            pltpu.VMEM((n_xy, rows_xy, COLS), BF16),
            pltpu.VMEM((rows_xy, COLS), BF16),
            pltpu.VMEM((n_z, rows_z, COLS), BF16),
            pltpu.VMEM((n_xy, n_z, rows_z, COLS), BF16),
            small,
            small,
            pltpu.VMEM((n_xy, 64, COLS), BF16),
            small,
            pltpu.VMEM((n_z, 64, COLS), BF16),
            small,
            small,
            sems(1),
            sems(n_xy),
            sems(n_z),
            sems(n_z),
            sems(n_xy),
            sems(n_xy),
            sems(1),
            sems(n_xy),
            sems(n_z),
            sems(1),
        ],
        compiler_params=pltpu.CompilerParams(
            collective_id=1, has_side_effects=True, vmem_limit_bytes=VMEM_LIMIT
        ),
        name="sums",
    )(g, grads, gk)


def finish_kernel(
    g_ref, ext_ref, rim_ref, taps_ref, cot_ref, sums_ref, gk_ref,
    state_ref, gk_out, gin_ref, gout_ref, pad, taps, north, flat,
    ):
    n_lat = lax.axis_size("lat")
    crown = lax.axis_index("lat") == n_lat - 1
    tap_tables(taps_ref, pad, None, taps, north, crown)
    flat[...] = cot_ref[...].astype(F32).reshape(C * ROWS, COLS)

    def body(group, _):
        out = conv_group(g_ref, ext_ref, rim_ref, taps, north, group)
        for i in range(ROWS):
            at = pl.ds(group * 64 + i, 8, stride=8)
            flat[at, :] = flat[at, :] + out[i]
        return 0

    lax.fori_loop(0, C // 8, body, 0)

    def out_body(group, _):
        state_ref[pl.ds(group * 32, 32)] = flat[pl.ds(al(group * 256, 256), 256), :].reshape(32, ROWS, COLS).astype(BF16)
        return 0

    lax.fori_loop(0, C // 32, out_body, 0)
    for b in range(2):
        gout_ref[:, b * COLS : (b + 1) * COLS] = sums_ref[b * 1024 : (b + 1) * 1024, :].astype(F32)
        gk_out[:, b * COLS : (b + 1) * COLS] = gk_ref[b].astype(F32)[:49]
    for b in range(8):
        gin_ref[:, b * COLS : (b + 1) * COLS] = sums_ref[HALF + b * 256 : HALF + (b + 1) * 256, :].astype(F32)


def finish_call(g, ext, rim, taps, cot, sums, gk):
    return pl.pallas_call(
        finish_kernel,
        out_shape=(
            jax.ShapeDtypeStruct((C, ROWS, COLS), BF16),
            jax.ShapeDtypeStruct((49, C), F32),
            jax.ShapeDtypeStruct((C, HID), F32),
            jax.ShapeDtypeStruct((HID, C), F32),
        ),
        in_specs=[VSPEC] * 7,
        out_specs=(VSPEC,) * 4,
        scratch_shapes=[
            pltpu.VMEM((COLS, C), F32),
            pltpu.VMEM((C, COLS), F32),
            pltpu.VMEM((C, COLS), F32),
            pltpu.VMEM((C * ROWS, COLS), F32),
        ],
        compiler_params=pltpu.CompilerParams(vmem_limit_bytes=VMEM_LIMIT),
        name="finish",
    )(g, ext, rim, taps, cot, sums, gk)


def per_device(n_lon, n_lat, ocean_state, land_mask, kernel, w_in, w_out, cotangent):
    rows, ext, rim = halo_call(ocean_state, n_lon, n_lat)
    stepped, g, grads, gk = block_call(rows, ext, rim, land_mask, kernel, w_in, w_out, cotangent)
    g_ext, g_rim, sums, gk = sum_call(g, grads, gk, n_lon, n_lat)
    state, grad_k, grad_in, grad_out = finish_call(
        g, g_ext, g_rim, kernel, cotangent, sums.reshape(2 * HALF, COLS), gk
    )
    return stepped, state, grad_k, grad_in, grad_out


def solution(mesh):
    return jax.shard_map(
        functools.partial(per_device, mesh.shape["lon"], mesh.shape["lat"]),
        mesh=mesh,
        in_specs=(P(None, "lat", "lon"), P("lat", "lon"), P(), P(), P(), P(None, "lat", "lon")),
        out_specs=(P(None, "lat", "lon"), P(None, "lat", "lon"), P(), P(), P()),
        check_vma=False,
    )
```

```python
import functools

import jax
import jax.numpy as jnp
from jax import lax
from jax.experimental import pallas as pl
from jax.experimental.pallas import tpu as pltpu
from jax.sharding import PartitionSpec as P

F32 = jnp.float32
BF16 = jnp.bfloat16
MESH = pl.DeviceIdType.MESH
TANH_SLOPE = 0.7978845608028654
CUBIC = 0.044715
EPS = 1e-06
C = 256
HID = 1024
ROWS = 8
COLS = 128
CELLS = ROWS * COLS
HALF = 2048
VMEM_LIMIT = 56 * 1024 * 1024
VSPEC = pl.BlockSpec(memory_space=pltpu.VMEM)


def al(value, multiple):
    return pl.multiple_of(value, multiple)


def pick(flag, yes, no):
    return flag * yes + (1 - flag) * no


class Place:
    def __init__(self, n_lon, n_lat):
        self.n_lon, self.n_lat = n_lon, n_lat
        self.lon = lax.axis_index("lon")
        self.lat = lax.axis_index("lat")
        self.crown = (self.lat == n_lat - 1).astype(jnp.int32)
        self.floor = (self.lat == 0).astype(jnp.int32)
        east = lax.rem(self.lon + 1, n_lon)
        west = lax.rem(self.lon + n_lon - 1, n_lon)
        north = pick(self.crown, self.lat, self.lat + 1)
        south = lax.rem(self.lat + n_lat - 1, n_lat)
        mirror = n_lon - 1 - self.lon
        self.west_id = {"lon": west, "lat": self.lat}
        self.east_id = {"lon": east, "lat": self.lat}
        self.north_id = {"lon": pick(self.crown, mirror, self.lon), "lat": north}
        self.south_id = {"lon": self.lon, "lat": south}
        nw = pick(self.crown, lax.rem(n_lon - self.lon, n_lon), west)
        ne = pick(self.crown, lax.rem(2 * n_lon - 2 - self.lon, n_lon), east)
        self.nw_self = (self.crown == 1) & (nw == self.lon)
        self.ne_self = (self.crown == 1) & (ne == self.lon)
        self.nw_id = {"lon": nw, "lat": north}
        self.ne_id = {"lon": ne, "lat": north}
        self.sw_id = {"lon": west, "lat": south}
        self.se_id = {"lon": east, "lat": south}
        self.core = lax.rem(self.lon, 2)
        self.xl = lax.rem(self.lon // 2, 2)
        self.zi = self.lon // 4
        self.n_xy, self.n_z = 2 * n_lat, n_lon // 4
        self.xy = self.lat * 2 + self.xl
        self.core_id = {"lon": self.lon + 1 - 2 * self.core, "lat": self.lat}

    def xy_peer(self, step):
        peer = lax.rem(self.xy + step, self.n_xy)
        return peer, {"lon": self.zi * 4 + lax.rem(peer, 2) * 2 + self.core, "lat": peer // 2}

    def z_peer(self, step):
        peer = lax.rem(self.zi + step, self.n_z)
        return peer, {"lon": peer * 4 + self.xl * 2 + self.core, "lat": self.lat}


def signal(barrier, device):
    pl.semaphore_signal(barrier, inc=1, device_id=device, device_id_type=MESH)


def greet_halo(place, barrier):
    for device in (place.west_id, place.east_id, place.north_id):
        signal(barrier, device)

    @pl.when(jnp.logical_not(place.nw_self))
    def _():
        signal(barrier, place.nw_id)

    @pl.when(jnp.logical_not(place.ne_self))
    def _():
        signal(barrier, place.ne_id)

    @pl.when(place.floor == 0)
    def _():
        for device in (place.south_id, place.sw_id, place.se_id):
            signal(barrier, device)

    return (
        5
        - place.nw_self.astype(jnp.int32)
        - place.ne_self.astype(jnp.int32)
        + 3 * (1 - place.floor)
    )


def halo_copies(place, rows_ref, edges, halo_ref, rt_ref, send_sem, recv_sem):
    crown = place.crown

    def remote(src, dst, index, slot, device):
        return pltpu.make_async_remote_copy(
            src_ref=src,
            dst_ref=dst,
            send_sem=send_sem.at[index],
            recv_sem=recv_sem.at[slot],
            device_id=device,
            device_id_type=MESH,
        )

    return [
        remote(edges.at[0], rt_ref.at[1, pl.ds(1, 2)], 0, 0, place.west_id),
        remote(edges.at[1], rt_ref.at[0, pl.ds(1, 2)], 1, 1, place.east_id),
        remote(rows_ref.at[pl.ds(5, 3)], halo_ref.at[crown], 2, 2 + crown, place.north_id),
        remote(rows_ref.at[pl.ds(0, 3)], halo_ref.at[1], 3, 3, place.south_id),
        remote(edges.at[0, 1], rt_ref.at[1 - crown, 3 * crown], 4, 4 + 3 * crown, place.nw_id),
        remote(edges.at[1, 1], rt_ref.at[crown, 3 * crown], 5, 5 + crown, place.ne_id),
        remote(edges.at[0, 0], rt_ref.at[1, 3], 6, 6, place.sw_id),
        remote(edges.at[1, 0], rt_ref.at[0, 3], 7, 7, place.se_id),
    ]


def halo_start(place, copies, edges, rt_ref, recv_sem):
    for index in (2, 0, 1):
        copies[index].start()

    @pl.when(place.floor == 0)
    def _():
        copies[3].start()
        copies[6].start()
        copies[7].start()

    for is_self, index, side, slot in ((place.nw_self, 4, 0, 7), (place.ne_self, 5, 1, 6)):

        @pl.when(is_self)
        def _(side=side, slot=slot):
            pltpu.make_async_copy(edges.at[side, 1], rt_ref.at[side, 3], recv_sem.at[slot]).start()

        @pl.when(jnp.logical_not(is_self))
        def _(index=index):
            copies[index].start()


def wait_bytes(ref, sem):
    pltpu.make_async_copy(ref, ref, sem).wait()


def halo_wait(place, halo_ref, rt_ref, recv_sem):
    wait_bytes(rt_ref.at[1, pl.ds(1, 2)], recv_sem.at[0])
    wait_bytes(rt_ref.at[0, pl.ds(1, 2)], recv_sem.at[1])
    wait_bytes(halo_ref.at[1], recv_sem.at[3])
    wait_bytes(rt_ref.at[1, 3], recv_sem.at[6])
    wait_bytes(rt_ref.at[0, 3], recv_sem.at[7])

    @pl.when(place.floor == 0)
    def _():
        wait_bytes(halo_ref.at[0], recv_sem.at[2])
        wait_bytes(rt_ref.at[1, 0], recv_sem.at[4])
        wait_bytes(rt_ref.at[0, 0], recv_sem.at[5])


def halo_sent(place, copies):
    for index in (0, 1, 2):
        copies[index].wait_send()

    @pl.when(place.floor == 0)
    def _():
        for index in (3, 6, 7):
            copies[index].wait_send()

    for is_self, index in ((place.nw_self, 4), (place.ne_self, 5)):

        @pl.when(jnp.logical_not(is_self))
        def _(index=index):
            copies[index].wait_send()


NT = (((1,), (1,)), ((), ()))


def square(n, rule):
    source = lax.broadcasted_iota(jnp.int32, (n, n), 0)
    target = lax.broadcasted_iota(jnp.int32, (n, n), 1)
    return jnp.where(rule(source, target), 1.0, 0.0).astype(BF16)


def lay_row(i, row, ident, wide, rows_t, edge_f):
    turned = lax.dot_general(ident, row, NT, preferred_element_type=F32)
    wide[0, 3 + i, 8:136, :] = turned[:, :COLS]
    wide[1, 3 + i, 8:136, :] = turned[:, COLS:]
    rows_t[i] = turned.astype(BF16)
    edge_f[0, 8 * i : 8 * i + 8, :] = turned[:8]
    edge_f[1, 8 * i : 8 * i + 8, :] = turned[120:]


def lay_edges(edge_f, edges):
    for side in range(2):
        for b in range(2):
            edges[side, b] = edge_f[side, 32 * b : 32 * b + 32, :].astype(BF16)


def unpack(place, halo_ref, rt_ref, wide):
    crown = place.crown == 1
    turn = square(COLS, lambda s, t: jnp.where(crown, COLS - 1 - s, s) == t)
    turn_small = square(32, lambda s, t: jnp.where(crown, 31 - s, s) == t)
    for k in range(3):
        south = jnp.where(place.floor == 1, 0.0, halo_ref[0, k].astype(F32))
        north = jnp.dot(turn, halo_ref[1, pick(place.crown, 2 - k, k)], preferred_element_type=F32)
        for h in range(2):
            wide[h, k, 8:136, :] = south[:, h * COLS : (h + 1) * COLS]
            wide[h, 11 + k, 8:136, :] = north[:, h * COLS : (h + 1) * COLS]
    for side in range(2):
        at = slice(136 * side, 136 * side + 8)
        for b in range(4):
            if b == 3:
                block = jnp.dot(turn_small, rt_ref[side, b], preferred_element_type=F32)
            else:
                block = rt_ref[side, b].astype(F32)
            if b == 0:
                block = jnp.where(place.floor == 1, 0.0, block)
            for s in range(4):
                r = 4 * b + s - 1
                if 0 <= r < 14:
                    for h in range(2):
                        wide[h, r, at, :] = block[8 * s : 8 * s + 8, h * COLS : (h + 1) * COLS]


LOCAL_ROWS = tuple(range(3, 11))
HALO_ROWS = (0, 1, 2, 11, 12, 13)


def conv_block(wide, weight, out_ref, h, j, rows, add):
    at = [pl.ds(al(i * COLS + j * 8, 8), 8) for i in range(ROWS)]
    total = [out_ref[h, at[i], :] if add else None for i in range(ROWS)]
    for q in range(7):
        for r in rows:
            moved = wide[h, r, pl.ds(j * 8 + (q + 5), 8), :]
            for a in range(7):
                i = r - a
                if 0 <= i < ROWS:
                    term = weight(h, a, q, r) * moved
                    total[i] = term if total[i] is None else total[i] + term
    for i in range(ROWS):
        out_ref[h, at[i], :] = total[i]


def conv_local(wide, weight, out_ref):
    def body(n, _):
        conv_block(wide, weight, out_ref, n // 14, 1 + lax.rem(n, 14), LOCAL_ROWS, False)
        return 0

    lax.fori_loop(0, 28, body, 0)


def conv_rest(wide, weight, out_ref):
    def inner(n, _):
        conv_block(wide, weight, out_ref, n // 14, 1 + lax.rem(n, 14), HALO_ROWS, True)
        return 0

    def rim(n, _):
        conv_block(wide, weight, out_ref, n // 2, 15 * lax.rem(n, 2), tuple(range(14)), False)
        return 0

    lax.fori_loop(0, 28, inner, 0)
    lax.fori_loop(0, 4, rim, 0)


def tap_sums(wide, g_wide, out_ref):
    row_id = lax.broadcasted_iota(jnp.int32, (8, COLS), 0)

    def body(n, _):
        h, q = n // 7, lax.rem(n, 7)
        total = [None] * 7
        for j in range(16):
            grads = [g_wide[h, 3 + i, 8 + 8 * j : 16 + 8 * j, :] for i in range(ROWS)]
            for r in range(14):
                moved = wide[h, r, pl.ds(q + (8 * j + 5), 8), :]
                for a in range(7):
                    i = r - a
                    if 0 <= i < ROWS:
                        term = grads[i] * moved
                        total[a] = term if total[a] is None else total[a] + term
        tile = jnp.zeros((8, COLS), F32)
        for a in range(7):
            tile = jnp.where(row_id == a, jnp.sum(total[a], axis=0, keepdims=True), tile)
        out_ref[h, q] = tile
        return 0

    lax.fori_loop(0, 14, body, 0)
    for h in range(2):
        out_ref[h, 7] = jnp.zeros((8, COLS), F32)


def whole_kernel(
    n_lon, n_lat,
    x_ref, mask_ref, taps_ref, w_in_ref, w_out_ref, cot_ref,
    stepped_ref, state_ref, gk_out, gin_ref, gout_ref,
    wide, rows_t, edge_f, edges, halo, rt, send_sem, recv_sem,
    g_wide, g_rows, g_edges, g_halo, g_rt, g_send, g_recv,
    taps, taps_n, w_in_t, w_out_t, flat, conv_t, x_hat_ref, normed, gb, act, g_pre, g_norm, inv_ref,
    grads, pair_in, mine, xy_in, part, z_in, done, sums,
    tap_acc, gk, gk_pair, gk_mine, gk_xy, gk_xy_mine, gk_z, gk_all,
    core_sems, xy_sems, z_sems, zg_sems, xyg_sems, last_sems, gk_core, gk_xy_sems, gk_z_sems, gk_last_sems,
):
    place = Place(n_lon, n_lat)
    n_xy, n_z = place.n_xy, place.n_z
    rows_xy, rows_z = HALF // n_xy, HALF // n_xy // n_z
    core, other = place.core, 1 - place.core

    barrier = pltpu.get_barrier_semaphore()
    count = greet_halo(place, barrier)
    signal(barrier, place.core_id)

    def greet_xy(step, _):
        signal(barrier, place.xy_peer(step)[1])
        return 0

    def greet_z(step, _):
        signal(barrier, place.z_peer(step)[1])
        return 0

    lax.fori_loop(1, n_xy, greet_xy, 0)
    lax.fori_loop(1, n_z, greet_z, 0)

    ident = square(COLS, lambda s, t: s == t)
    flat[...] = x_ref[...].astype(F32).reshape(C * ROWS, COLS)
    for i in range(ROWS):
        lay_row(i, flat[pl.ds(i, C, stride=8), :].astype(BF16), ident, wide, rows_t, edge_f)
    lay_edges(edge_f, edges)
    pl.semaphore_wait(barrier, count + n_xy + n_z - 1)
    copies = halo_copies(place, rows_t, edges, halo, rt, send_sem, recv_sem)
    halo_start(place, copies, edges, rt, recv_sem)

    crown = place.crown == 1
    table = taps_ref[...].astype(F32)
    for t in range(49):
        for h in range(2):
            taps[h, t] = jnp.broadcast_to(table[t : t + 1, h * COLS : (h + 1) * COLS], (8, COLS))
    for t in range(28, 49):
        for h in range(2):
            taps_n[h, t] = jnp.where(crown, taps[h, t], taps[h, 48 - t])

    def forward(h, a, q, r):
        return taps[h, 7 * a + q]

    def backward(h, a, q, r):
        return taps_n[h, 7 * a + q] if r >= 11 else taps[h, 48 - 7 * a - q]

    conv_local(wide, forward, conv_t)
    w_in_t[...] = w_in_ref[...].astype(F32).T.astype(BF16)
    w_out_t[...] = w_out_ref[...].astype(F32).T.astype(BF16)
    flat[...] = cot_ref[...].astype(F32).reshape(C * ROWS, COLS)
    for r in range(ROWS):
        ocean = mask_ref[pl.ds(r, 1), :].astype(F32)
        gb[:, r * COLS : (r + 1) * COLS] = (ocean * flat[pl.ds(r, C, stride=8), :]).astype(BF16)

    halo_wait(place, halo, rt, recv_sem)
    unpack(place, halo, rt, wide)
    conv_rest(wide, forward, conv_t)

    for r in range(ROWS):
        at = slice(r * COLS, (r + 1) * COLS)
        value = jnp.concatenate([conv_t[0, at, :].T, conv_t[1, at, :].T], axis=0)
        centred = value - jnp.sum(value, axis=0, keepdims=True) * (1.0 / C)
        var = jnp.sum(centred * centred, axis=0, keepdims=True) * (1.0 / C)
        inv = lax.rsqrt(var + EPS)
        inv_ref[pl.ds(r, 1), :] = inv
        x_hat = centred * inv
        x_hat_ref[:, at] = x_hat
        normed[:, at] = x_hat.astype(BF16)

    def cells_body(n, _):
        at = pl.ds(al(n * 256, 256), 256)
        hat = normed[:, at]
        grad = gb[:, at]
        for h in range(4):
            hs = slice(h * 256, (h + 1) * 256)
            u = jnp.dot(w_in_t[hs, :], hat, preferred_element_type=F32)
            uu = u * u
            t = jnp.tanh(TANH_SLOPE * (u + CUBIC * (uu * u)))
            gate = 0.5 * (1.0 + t)
            act[hs, at] = (u * gate).astype(BF16)
            slope = gate + (0.5 * TANH_SLOPE) * u * (1.0 - t * t) * (1.0 + (3.0 * CUBIC) * uu)
            g_act = jnp.dot(w_out_ref[hs, :], grad, preferred_element_type=F32)
            g_pre[hs, at] = (g_act * slope).astype(BF16)
        g_norm[:, at] = jnp.dot(w_in_ref[...], g_pre[:, at], preferred_element_type=F32)
        branch = jnp.dot(w_out_t[...], act[:, at], preferred_element_type=F32)
        for k in range(2):
            r = 2 * n + k
            ocean = mask_ref[pl.ds(r, 1), :].astype(F32)
            flat[pl.ds(r, C, stride=8), :] = ocean * branch[:, k * COLS : (k + 1) * COLS]
        return 0

    lax.fori_loop(0, CELLS // 256, cells_body, 0)

    for h in range(4):
        hs = slice(h * 256, (h + 1) * 256)
        out = lax.dot_general(act[hs, :], gb[...], NT, preferred_element_type=F32).astype(BF16)
        grads[h * 256 : (h + 1) * 256, :] = out[:, :COLS]
        grads[1024 + h * 256 : 1024 + (h + 1) * 256, :] = out[:, COLS:]
    for h in range(4):
        hs = slice(h * 256, (h + 1) * 256)
        out = lax.dot_general(normed[...], g_pre[hs, :], NT, preferred_element_type=F32).astype(BF16)
        grads[HALF + h * 512 : HALF + h * 512 + 256, :] = out[:, :COLS]
        grads[HALF + h * 512 + 256 : HALF + (h + 1) * 512, :] = out[:, COLS:]

    def remote(src, dst, sems, index, device):
        return pltpu.make_async_remote_copy(
            src_ref=src, dst_ref=dst, send_sem=sems.at[0, index], recv_sem=sems.at[1, index],
            device_id=device, device_id_type=MESH,
        )

    def each(n, make, act):
        def run(step, _):
            act(make(step))
            return 0

        lax.fori_loop(1, n, run, 0)

    def start(copy):
        copy.start()

    def wait(copy):
        copy.wait()

    def sent(copy):
        copy.wait_send()

    first = remote(grads.at[pl.ds(al(other * HALF, HALF), HALF)], pair_in, core_sems, 0, place.core_id)
    first.start()

    for r in range(ROWS):
        at = slice(r * COLS, (r + 1) * COLS)
        grad, x_hat = g_norm[:, at], x_hat_ref[:, at]
        mean = jnp.sum(grad, axis=0, keepdims=True) * (1.0 / C)
        proj = jnp.sum(grad * x_hat, axis=0, keepdims=True) * (1.0 / C)
        g_conv = inv_ref[pl.ds(r, 1), :] * (grad - mean - x_hat * proj)
        lay_row(r, g_conv.astype(BF16), ident, g_wide, g_rows, edge_f)
    lay_edges(edge_f, g_edges)

    first.wait()

    def add_pair(i, _):
        at = pl.ds(al(i * 256, 256), 256)
        own = grads[pl.ds(al(core * HALF + i * 256, 256), 256), :].astype(F32)
        mine[at, :] = (own + pair_in[at, :].astype(F32)).astype(BF16)
        return 0

    lax.fori_loop(0, HALF // 256, add_pair, 0)

    def xy_copy(step):
        peer, device = place.xy_peer(step)
        return remote(mine.at[pl.ds(al(peer * rows_xy, rows_xy), rows_xy)], xy_in.at[step], xy_sems, step, device)

    each(n_xy, xy_copy, start)
    g_copies = halo_copies(place, g_rows, g_edges, g_halo, g_rt, g_send, g_recv)
    halo_start(place, g_copies, g_edges, g_rt, g_recv)

    tap_sums(wide, g_wide, tap_acc)
    for h in range(2):
        gk[h] = tap_acc[h].reshape(64, COLS).astype(BF16)
    first_k = remote(gk.at[other], gk_pair, gk_core, 0, place.core_id)
    first_k.start()

    def step_body(group, _):
        at = pl.ds(group * 32, 32)
        moved = flat[pl.ds(al(group * 256, 256), 256), :].reshape(32, ROWS, COLS)
        stepped_ref[at] = (x_ref[at].astype(F32) + moved).astype(BF16)
        return 0

    lax.fori_loop(0, C // 32, step_body, 0)
    conv_local(g_wide, backward, conv_t)

    each(n_xy, xy_copy, wait)
    total = mine[pl.ds(al(place.xy * rows_xy, rows_xy), rows_xy), :].astype(F32)
    for step in range(1, n_xy):
        total = total + xy_in[step].astype(F32)
    part[...] = total.astype(BF16)

    def z_copy(step):
        peer, device = place.z_peer(step)
        return remote(part.at[pl.ds(al(peer * rows_z, rows_z), rows_z)], z_in.at[step], z_sems, step, device)

    each(n_z, z_copy, start)

    first_k.wait()
    gk_mine[...] = (gk[core].astype(F32) + gk_pair[...].astype(F32)).astype(BF16)

    def gk_xy_copy(step):
        _, device = place.xy_peer(step)
        return remote(gk_mine, gk_xy.at[step], gk_xy_sems, step, device)

    each(n_xy, gk_xy_copy, start)

    each(n_z, z_copy, wait)
    total = part[pl.ds(al(place.zi * rows_z, rows_z), rows_z), :].astype(F32)
    for step in range(1, n_z):
        total = total + z_in[step].astype(F32)
    done[place.xy, place.zi] = total.astype(BF16)

    def zg_copy(step):
        _, device = place.z_peer(step)
        own = done.at[place.xy, place.zi]
        return remote(own, own, zg_sems, step, device)

    each(n_z, zg_copy, start)

    halo_wait(place, g_halo, g_rt, g_recv)
    unpack(place, g_halo, g_rt, g_wide)

    def zg_wait(step, _):
        sender = lax.rem(place.zi + n_z - step, n_z)
        wait_bytes(done.at[place.xy, sender], zg_sems.at[1, step])
        return 0

    lax.fori_loop(1, n_z, zg_wait, 0)

    def xyg_copy(step):
        _, device = place.xy_peer(step)
        own = done.at[place.xy]
        return remote(own, own, xyg_sems, step, device)

    def across(step, index):
        return remote(done.at[index], sums.at[index], last_sems, step, place.core_id)

    each(n_xy, xyg_copy, start)
    across(0, place.xy).start()

    each(n_xy, gk_xy_copy, wait)
    total = gk_mine[...].astype(F32)
    for step in range(1, n_xy):
        total = total + gk_xy[step].astype(F32)
    gk_xy_mine[...] = total.astype(BF16)

    def gk_z_copy(step):
        _, device = place.z_peer(step)
        return remote(gk_xy_mine, gk_z.at[step], gk_z_sems, step, device)

    each(n_z, gk_z_copy, start)

    conv_rest(g_wide, backward, conv_t)
    for r in range(ROWS):
        at = slice(r * COLS, (r + 1) * COLS)
        flat[pl.ds(r, C, stride=8), :] = jnp.concatenate([conv_t[0, at, :].T, conv_t[1, at, :].T], axis=0)

    def state_body(group, _):
        at = pl.ds(group * 32, 32)
        moved = flat[pl.ds(al(group * 256, 256), 256), :].reshape(32, ROWS, COLS)
        state_ref[at] = (cot_ref[at].astype(F32) + moved).astype(BF16)
        return 0

    lax.fori_loop(0, C // 32, state_body, 0)

    each(n_z, gk_z_copy, wait)
    total = gk_xy_mine[...].astype(F32)
    for step in range(1, n_z):
        total = total + gk_z[step].astype(F32)
    gk_all[core] = total.astype(BF16)
    last_k = remote(gk_all.at[core], gk_all.at[core], gk_last_sems, 0, place.core_id)
    last_k.start()

    def xyg_wait(step, _):
        sender = lax.rem(place.xy + n_xy - step, n_xy)
        wait_bytes(done.at[sender], xyg_sems.at[1, step])
        across(step, sender).start()
        return 0

    lax.fori_loop(1, n_xy, xyg_wait, 0)

    def last_wait(step, _):
        sender = lax.rem(place.xy + n_xy - step, n_xy)
        wait_bytes(done.at[sender], last_sems.at[0, step])
        wait_bytes(sums.at[sender], last_sems.at[1, step])
        return 0

    lax.fori_loop(0, n_xy, last_wait, 0)

    def write(out_sums, in_sums):
        out_rows = out_sums[...].reshape(HALF, COLS)
        in_rows = in_sums[...].reshape(HALF, COLS)
        for b in range(2):
            gout_ref[:, b * COLS : (b + 1) * COLS] = out_rows[b * 1024 : (b + 1) * 1024].astype(F32)
        for b in range(8):
            gin_ref[:, b * COLS : (b + 1) * COLS] = in_rows[b * 256 : (b + 1) * 256].astype(F32)

    @pl.when(core == 0)
    def _():
        write(done, sums)

    @pl.when(core == 1)
    def _():
        write(sums, done)

    wait_bytes(gk_all.at[core], gk_last_sems.at[0, 0])
    wait_bytes(gk_all.at[other], gk_last_sems.at[1, 0])
    for h in range(2):
        total = gk_all[h].astype(F32)
        for t in range(49):
            a, q = t // 7, t % 7
            gk_out[t : t + 1, h * COLS : (h + 1) * COLS] = total[8 * q + a : 8 * q + a + 1]

    each(n_z, zg_copy, sent)
    each(n_xy, xyg_copy, sent)
    halo_sent(place, copies)
    halo_sent(place, g_copies)


def halo_scratch():
    return [
        pltpu.VMEM((2, 2, 32, C), BF16),
        pltpu.VMEM((2, 3, COLS, C), BF16),
        pltpu.VMEM((2, 4, 32, C), BF16),
        pltpu.SemaphoreType.DMA((8,)),
        pltpu.SemaphoreType.DMA((8,)),
    ]


def per_device(n_lon, n_lat, ocean_state, land_mask, kernel, w_in, w_out, cotangent):
    n_xy, n_z = 2 * n_lat, n_lon // 4
    rows_xy, rows_z = HALF // n_xy, HALF // n_xy // n_z
    wide = pltpu.VMEM((2, 14, 144, COLS), F32)
    turned_rows = pltpu.VMEM((ROWS, COLS, C), BF16)
    small = pltpu.VMEM((64, COLS), BF16)
    table = pltpu.VMEM((2, 49, 8, COLS), F32)
    sems = lambda n: pltpu.SemaphoreType.DMA((2, n))
    summed = pltpu.VMEM((n_xy, n_z, rows_z, COLS), BF16)
    return pl.pallas_call(
        functools.partial(whole_kernel, n_lon, n_lat),
        out_shape=(
            jax.ShapeDtypeStruct((C, ROWS, COLS), BF16),
            jax.ShapeDtypeStruct((C, ROWS, COLS), BF16),
            jax.ShapeDtypeStruct((49, C), F32),
            jax.ShapeDtypeStruct((C, HID), F32),
            jax.ShapeDtypeStruct((HID, C), F32),
        ),
        in_specs=[VSPEC] * 6,
        out_specs=(VSPEC,) * 5,
        scratch_shapes=[wide, turned_rows, pltpu.VMEM((2, 64, C), F32)]
        + halo_scratch()
        + [wide, turned_rows]
        + halo_scratch()
        + [
            table,
            table,
            pltpu.VMEM((HID, C), BF16),
            pltpu.VMEM((C, HID), BF16),
            pltpu.VMEM((C * ROWS, COLS), F32),
            pltpu.VMEM((2, CELLS, COLS), F32),
            pltpu.VMEM((C, CELLS), F32),
            pltpu.VMEM((C, CELLS), BF16),
            pltpu.VMEM((C, CELLS), BF16),
            pltpu.VMEM((HID, CELLS), BF16),
            pltpu.VMEM((HID, CELLS), BF16),
            pltpu.VMEM((C, CELLS), F32),
            pltpu.VMEM((ROWS, COLS), F32),
            pltpu.VMEM((2 * HALF, COLS), BF16),
            pltpu.VMEM((HALF, COLS), BF16),
            pltpu.VMEM((HALF, COLS), BF16),
            pltpu.VMEM((n_xy, rows_xy, COLS), BF16),
            pltpu.VMEM((rows_xy, COLS), BF16),
            pltpu.VMEM((n_z, rows_z, COLS), BF16),
            summed,
            summed,
            pltpu.VMEM((2, 8, 8, COLS), F32),
            pltpu.VMEM((2, 64, COLS), BF16),
            small,
            small,
            pltpu.VMEM((n_xy, 64, COLS), BF16),
            small,
            pltpu.VMEM((n_z, 64, COLS), BF16),
            pltpu.VMEM((2, 64, COLS), BF16),
            sems(1),
            sems(n_xy),
            sems(n_z),
            sems(n_z),
            sems(n_xy),
            sems(n_xy),
            sems(1),
            sems(n_xy),
            sems(n_z),
            sems(1),
        ],
        compiler_params=pltpu.CompilerParams(
            collective_id=0, has_side_effects=True, vmem_limit_bytes=VMEM_LIMIT
        ),
        name="convnext",
    )(ocean_state, land_mask, kernel, w_in, w_out, cotangent)


def solution(mesh):
    return jax.shard_map(
        functools.partial(per_device, mesh.shape["lon"], mesh.shape["lat"]),
        mesh=mesh,
        in_specs=(P(None, "lat", "lon"), P("lat", "lon"), P(), P(), P(), P(None, "lat", "lon")),
        out_specs=(P(None, "lat", "lon"), P(None, "lat", "lon"), P(), P(), P()),
        check_vma=False,
    )
```

```python
import functools

import jax
import jax.numpy as jnp
from jax import lax
from jax.experimental import pallas as pl
from jax.experimental.pallas import tpu as pltpu
from jax.sharding import PartitionSpec as P

F32 = jnp.float32
BF16 = jnp.bfloat16
MESH = pl.DeviceIdType.MESH
TANH_SLOPE = 0.7978845608028654
CUBIC = 0.044715
EPS = 1e-06
C = 256
HID = 1024
ROWS = 8
COLS = 128
CELLS = ROWS * COLS
HALF = 2048
VMEM_LIMIT = 56 * 1024 * 1024
VSPEC = pl.BlockSpec(memory_space=pltpu.VMEM)


def al(value, multiple):
    return pl.multiple_of(value, multiple)


def pick(flag, yes, no):
    return flag * yes + (1 - flag) * no


class Place:
    def __init__(self, n_lon, n_lat):
        self.n_lon, self.n_lat = n_lon, n_lat
        self.lon = lax.axis_index("lon")
        self.lat = lax.axis_index("lat")
        self.crown = (self.lat == n_lat - 1).astype(jnp.int32)
        self.floor = (self.lat == 0).astype(jnp.int32)
        east = lax.rem(self.lon + 1, n_lon)
        west = lax.rem(self.lon + n_lon - 1, n_lon)
        north = pick(self.crown, self.lat, self.lat + 1)
        south = lax.rem(self.lat + n_lat - 1, n_lat)
        mirror = n_lon - 1 - self.lon
        self.west_id = {"lon": west, "lat": self.lat}
        self.east_id = {"lon": east, "lat": self.lat}
        self.north_id = {"lon": pick(self.crown, mirror, self.lon), "lat": north}
        self.south_id = {"lon": self.lon, "lat": south}
        nw = pick(self.crown, lax.rem(n_lon - self.lon, n_lon), west)
        ne = pick(self.crown, lax.rem(2 * n_lon - 2 - self.lon, n_lon), east)
        self.nw_self = (self.crown == 1) & (nw == self.lon)
        self.ne_self = (self.crown == 1) & (ne == self.lon)
        self.nw_id = {"lon": nw, "lat": north}
        self.ne_id = {"lon": ne, "lat": north}
        self.sw_id = {"lon": west, "lat": south}
        self.se_id = {"lon": east, "lat": south}
        self.core = lax.rem(self.lon, 2)
        self.zi = self.lon // 4
        self.yi = self.lat // 2
        self.xi = lax.rem(self.lat, 2) * 2 + lax.rem(self.lon // 2, 2)
        self.n_y, self.n_z = n_lat // 2, n_lon // 4
        self.xz, self.n_xz = self.zi * 4 + self.xi, n_lon
        self.core_id = {"lon": self.lon + 1 - 2 * self.core, "lat": self.lat}

    def device(self, x, y, z):
        return {"lon": z * 4 + lax.rem(x, 2) * 2 + self.core, "lat": y * 2 + x // 2}

    def x_peer(self, step):
        return self.device(lax.rem(self.xi + step, 4), self.yi, self.zi)

    def z_peer(self, step):
        return self.device(self.xi, self.yi, lax.rem(self.zi + step, self.n_z))

    def y_peer(self, step):
        peer = lax.rem(self.yi + step, self.n_y)
        return peer, self.device(self.xi, peer, self.zi)

    def xz_peer(self, step):
        peer = lax.rem(self.xz + step, self.n_xz)
        return peer, self.device(lax.rem(peer, 4), self.yi, peer // 4)


def signal(barrier, device):
    pl.semaphore_signal(barrier, inc=1, device_id=device, device_id_type=MESH)


def greet_halo(place, barrier):
    for device in (place.west_id, place.east_id, place.north_id):
        signal(barrier, device)

    @pl.when(jnp.logical_not(place.nw_self))
    def _():
        signal(barrier, place.nw_id)

    @pl.when(jnp.logical_not(place.ne_self))
    def _():
        signal(barrier, place.ne_id)

    @pl.when(place.floor == 0)
    def _():
        for device in (place.south_id, place.sw_id, place.se_id):
            signal(barrier, device)

    return (
        5
        - place.nw_self.astype(jnp.int32)
        - place.ne_self.astype(jnp.int32)
        + 3 * (1 - place.floor)
    )


def halo_copies(place, rows_ref, edges, halo_ref, rt_ref, send_sem, recv_sem):
    crown = place.crown

    def remote(src, dst, index, slot, device):
        return pltpu.make_async_remote_copy(
            src_ref=src,
            dst_ref=dst,
            send_sem=send_sem.at[index],
            recv_sem=recv_sem.at[slot],
            device_id=device,
            device_id_type=MESH,
        )

    return [
        remote(edges.at[0], rt_ref.at[1, pl.ds(1, 2)], 0, 0, place.west_id),
        remote(edges.at[1], rt_ref.at[0, pl.ds(1, 2)], 1, 1, place.east_id),
        remote(edges.at[0, 1], rt_ref.at[1 - crown, 3 * crown], 2, 2 + 3 * crown, place.nw_id),
        remote(edges.at[1, 1], rt_ref.at[crown, 3 * crown], 3, 3 + crown, place.ne_id),
        remote(edges.at[0, 0], rt_ref.at[1, 3], 4, 4, place.sw_id),
        remote(edges.at[1, 0], rt_ref.at[0, 3], 5, 5, place.se_id),
    ] + [
        remote(rows_ref.at[7 - k], halo_ref.at[crown, k], 6 + k, 6 + k + 3 * crown, place.north_id)
        for k in range(3)
    ] + [
        remote(rows_ref.at[k], halo_ref.at[1, k], 9 + k, 9 + k, place.south_id) for k in range(3)
    ]


def halo_start(place, copies, edges, rt_ref, recv_sem):
    copies[0].start()
    copies[1].start()
    for is_self, index, side, slot in ((place.nw_self, 2, 0, 5), (place.ne_self, 3, 1, 4)):

        @pl.when(is_self)
        def _(side=side, slot=slot):
            pltpu.make_async_copy(edges.at[side, 1], rt_ref.at[side, 3], recv_sem.at[slot]).start()

        @pl.when(jnp.logical_not(is_self))
        def _(index=index):
            copies[index].start()

    @pl.when(place.floor == 0)
    def _():
        copies[4].start()
        copies[5].start()
        for k in range(3):
            copies[6 + k].start()
            copies[9 + k].start()

    @pl.when(place.floor == 1)
    def _():
        for k in range(3):
            copies[6 + k].start()


def wait_bytes(ref, sem):
    pltpu.make_async_copy(ref, ref, sem).wait()


def rim_wait(place, rt_ref, recv_sem):
    wait_bytes(rt_ref.at[1, pl.ds(1, 2)], recv_sem.at[0])
    wait_bytes(rt_ref.at[0, pl.ds(1, 2)], recv_sem.at[1])
    wait_bytes(rt_ref.at[1, 3], recv_sem.at[4])
    wait_bytes(rt_ref.at[0, 3], recv_sem.at[5])

    @pl.when(place.floor == 0)
    def _():
        wait_bytes(rt_ref.at[1, 0], recv_sem.at[2])
        wait_bytes(rt_ref.at[0, 0], recv_sem.at[3])


def row_wait(place, k, halo_ref, recv_sem):
    wait_bytes(halo_ref.at[1, k], recv_sem.at[9 + k])

    @pl.when(place.floor == 0)
    def _():
        wait_bytes(halo_ref.at[0, k], recv_sem.at[6 + k])


def halo_sent(place, copies):
    for index in (0, 1, 6, 7, 8):
        copies[index].wait_send()

    @pl.when(place.floor == 0)
    def _():
        for index in (4, 5, 9, 10, 11):
            copies[index].wait_send()

    for is_self, index in ((place.nw_self, 2), (place.ne_self, 3)):

        @pl.when(jnp.logical_not(is_self))
        def _(index=index):
            copies[index].wait_send()


NT = (((1,), (1,)), ((), ()))


def square(n, rule):
    source = lax.broadcasted_iota(jnp.int32, (n, n), 0)
    target = lax.broadcasted_iota(jnp.int32, (n, n), 1)
    return jnp.where(rule(source, target), 1.0, 0.0).astype(BF16)


def lay_row(i, row, ident, wide, rows_t, edge_f):
    turned = lax.dot_general(ident, row, NT, preferred_element_type=F32)
    wide[0, 3 + i, 8:136, :] = turned[:, :COLS]
    wide[1, 3 + i, 8:136, :] = turned[:, COLS:]
    rows_t[i] = turned.astype(BF16)
    edge_f[0, 8 * i : 8 * i + 8, :] = turned[:8]
    edge_f[1, 8 * i : 8 * i + 8, :] = turned[120:]


def lay_edges(edge_f, edges):
    for side in range(2):
        for b in range(2):
            edges[side, b] = edge_f[side, 32 * b : 32 * b + 32, :].astype(BF16)


def unpack_rim(place, rt_ref, wide):
    crown = place.crown == 1
    turn = square(32, lambda s, t: jnp.where(crown, 31 - s, s) == t)
    for side in range(2):
        at = slice(136 * side, 136 * side + 8)
        for b in range(4):
            if b == 3:
                block = jnp.dot(turn, rt_ref[side, b], preferred_element_type=F32)
            else:
                block = rt_ref[side, b].astype(F32)
            if b == 0:
                block = jnp.where(place.floor == 1, 0.0, block)
            for s in range(4):
                r = 4 * b + s - 1
                if 0 <= r < 14:
                    for h in range(2):
                        wide[h, r, at, :] = block[8 * s : 8 * s + 8, h * COLS : (h + 1) * COLS]


def unpack_row(place, k, halo_ref, wide):
    crown = place.crown == 1
    turn = square(COLS, lambda s, t: jnp.where(crown, COLS - 1 - s, s) == t)
    south = jnp.where(place.floor == 1, 0.0, halo_ref[0, k].astype(F32))
    north = jnp.dot(turn, halo_ref[1, k], preferred_element_type=F32)
    for h in range(2):
        wide[h, 2 - k, 8:136, :] = south[:, h * COLS : (h + 1) * COLS]
        wide[h, 11 + k, 8:136, :] = north[:, h * COLS : (h + 1) * COLS]


LOCAL_ROWS = tuple(range(3, 11))
HALO_ROWS = (0, 1, 2, 11, 12, 13)
PLACE = (6, 4, 2, 0, 1, 3, 5, 7)


def conv_block(wide, weight, out_ref, h, j, rows, add):
    at = [pl.ds(al(i * COLS + j * 8, 8), 8) for i in range(ROWS)]
    reached = [i for i in range(ROWS) if any(0 <= r - i < 7 for r in rows)]
    total = {i: out_ref[h, at[i], :] if add else None for i in reached}
    for q in range(7):
        for r in rows:
            moved = wide[h, r, pl.ds(j * 8 + (q + 5), 8), :]
            for a in range(7):
                i = r - a
                if 0 <= i < ROWS:
                    term = weight(h, a, q, r) * moved
                    total[i] = term if total[i] is None else total[i] + term
    for i in reached:
        out_ref[h, at[i], :] = total[i]


def conv_inner(wide, weight, out_ref):
    def body(n, _):
        conv_block(wide, weight, out_ref, n // 14, 1 + lax.rem(n, 14), LOCAL_ROWS, False)
        return 0

    lax.fori_loop(0, 28, body, 0)


def conv_rim(wide, weight, out_ref):
    def body(n, _):
        conv_block(wide, weight, out_ref, n // 2, 15 * lax.rem(n, 2), LOCAL_ROWS, False)
        return 0

    lax.fori_loop(0, 4, body, 0)


def conv_halo(wide, weight, out_ref, rows):
    def body(j, _):
        for h in range(2):
            conv_block(wide, weight, out_ref, h, j, rows, True)
        return 0

    lax.fori_loop(0, 16, body, 0)


def tap_sums(wide, g_wide, out_ref):
    row_id = lax.broadcasted_iota(jnp.int32, (8, COLS), 0)

    def body(n, _):
        h, q = n // 7, lax.rem(n, 7)
        total = [None] * 7
        for j in range(16):
            grads = [g_wide[h, 3 + i, 8 + 8 * j : 16 + 8 * j, :] for i in range(ROWS)]
            for r in range(14):
                moved = wide[h, r, pl.ds(q + (8 * j + 5), 8), :]
                for a in range(7):
                    i = r - a
                    if 0 <= i < ROWS:
                        term = grads[i] * moved
                        total[a] = term if total[a] is None else total[a] + term
        tile = jnp.zeros((8, COLS), F32)
        for a in range(7):
            tile = jnp.where(row_id == a, jnp.sum(total[a], axis=0, keepdims=True), tile)
        out_ref[h, q] = tile
        return 0

    lax.fori_loop(0, 14, body, 0)
    for h in range(2):
        out_ref[h, 7] = jnp.zeros((8, COLS), F32)


def whole_kernel(
    n_lon, n_lat,
    x_ref, mask_ref, taps_ref, w_in_ref, w_out_ref, cot_ref,
    stepped_ref, state_ref, sums_ref, gk_out,
    wide, rows_t, edge_f, edges, halo, rt, send_sem, recv_sem,
    g_wide, g_rows, g_edges, g_halo, g_rt, g_send, g_recv,
    taps, taps_n, w_in_t, w_out_t, flat, flat2, conv_t, x_hat_ref, normed, gb, act, g_pre, g_norm, inv_ref,
    grads, pair_in, mine, y_in, part, xz_in, done, sums,
    tap_acc, gk, gk_pair, gk_mine, gk_y, gk_x, gk_z, gk_all,
    core_sems, y_sems, xz_sems, xzg_sems, yg_sems, last_sems, gk_core, gk_y_sems, gk_x_sems, gk_z_sems, gk_last_sems,
):
    place = Place(n_lon, n_lat)
    n_y, n_z, n_xz = place.n_y, place.n_z, place.n_xz
    rows_y, rows_xz = HALF // n_y, HALF // n_y // n_xz
    core, other = place.core, 1 - place.core

    barrier = pltpu.get_barrier_semaphore()
    count = greet_halo(place, barrier)
    signal(barrier, place.core_id)

    def greet_y(step, _):
        signal(barrier, place.y_peer(step)[1])
        return 0

    def greet_xz(step, _):
        signal(barrier, place.xz_peer(step)[1])
        return 0

    lax.fori_loop(1, n_y, greet_y, 0)
    lax.fori_loop(1, n_xz, greet_xz, 0)

    ident = square(COLS, lambda s, t: s == t)
    flat[...] = x_ref[...].astype(F32).reshape(C * ROWS, COLS)
    for i in range(ROWS):
        lay_row(i, flat[pl.ds(i, C, stride=8), :].astype(BF16), ident, wide, rows_t, edge_f)
    lay_edges(edge_f, edges)
    pl.semaphore_wait(barrier, count + n_y + n_xz - 1)
    copies = halo_copies(place, rows_t, edges, halo, rt, send_sem, recv_sem)
    halo_start(place, copies, edges, rt, recv_sem)

    crown = place.crown == 1
    table = taps_ref[...].astype(F32)
    for t in range(49):
        for h in range(2):
            taps[h, t] = jnp.broadcast_to(table[t : t + 1, h * COLS : (h + 1) * COLS], (8, COLS))
    for t in range(28, 49):
        for h in range(2):
            taps_n[h, t] = jnp.where(crown, taps[h, t], taps[h, 48 - t])

    def forward(h, a, q, r):
        return taps[h, 7 * a + q]

    def backward(h, a, q, r):
        return taps_n[h, 7 * a + q] if r >= 11 else taps[h, 48 - 7 * a - q]

    conv_inner(wide, forward, conv_t)
    w_in_t[...] = w_in_ref[...].astype(F32).T.astype(BF16)
    w_out_t[...] = w_out_ref[...].astype(F32).T.astype(BF16)
    flat[...] = cot_ref[...].astype(F32).reshape(C * ROWS, COLS)
    for r in range(ROWS):
        ocean = mask_ref[pl.ds(r, 1), :].astype(F32)
        gb[:, PLACE[r] * COLS : (PLACE[r] + 1) * COLS] = (ocean * flat[pl.ds(r, C, stride=8), :]).astype(BF16)

    rim_wait(place, rt, recv_sem)
    unpack_rim(place, rt, wide)
    conv_rim(wide, forward, conv_t)

    def cells_body(n, _):
        for k in range(3):

            @pl.when(n == k + 1)
            def _(k=k):
                row_wait(place, k, halo, recv_sem)
                unpack_row(place, k, halo, wide)
                conv_halo(wide, forward, conv_t, (2 - k, 11 + k))

        at = pl.ds(al(n * 256, 256), 256)
        pair = (3 - n, 4 + n)
        for k, r in enumerate(pair):
            row_at = pl.ds(al(r * COLS, COLS), COLS)
            value = jnp.concatenate([conv_t[0, row_at, :].T, conv_t[1, row_at, :].T], axis=0)
            centred = value - jnp.sum(value, axis=0, keepdims=True) * (1.0 / C)
            var = jnp.sum(centred * centred, axis=0, keepdims=True) * (1.0 / C)
            inv = lax.rsqrt(var + EPS)
            inv_ref[pl.ds(r, 1), :] = inv
            x_hat = centred * inv
            x_hat_ref[:, pl.ds(al(n * 256 + k * COLS, COLS), COLS)] = x_hat
            normed[:, pl.ds(al(n * 256 + k * COLS, COLS), COLS)] = x_hat.astype(BF16)
        hat = normed[:, at]
        grad = gb[:, at]
        for h in range(4):
            hs = slice(h * 256, (h + 1) * 256)
            u = jnp.dot(w_in_t[hs, :], hat, preferred_element_type=F32)
            uu = u * u
            t = jnp.tanh(TANH_SLOPE * (u + CUBIC * (uu * u)))
            gate = 0.5 * (1.0 + t)
            act[hs, at] = (u * gate).astype(BF16)
            slope = gate + (0.5 * TANH_SLOPE) * u * (1.0 - t * t) * (1.0 + (3.0 * CUBIC) * uu)
            g_act = jnp.dot(w_out_ref[hs, :], grad, preferred_element_type=F32)
            g_pre[hs, at] = (g_act * slope).astype(BF16)
        g_norm[:, at] = jnp.dot(w_in_ref[...], g_pre[:, at], preferred_element_type=F32)
        branch = jnp.dot(w_out_t[...], act[:, at], preferred_element_type=F32)
        for k, r in enumerate(pair):
            ocean = mask_ref[pl.ds(r, 1), :].astype(F32)
            flat[pl.ds(r, C, stride=8), :] = ocean * branch[:, k * COLS : (k + 1) * COLS]
        return 0

    lax.fori_loop(0, ROWS // 2, cells_body, 0)

    for h in range(4):
        hs = slice(h * 256, (h + 1) * 256)
        out = lax.dot_general(act[hs, :], gb[...], NT, preferred_element_type=F32).astype(BF16)
        grads[h * 256 : (h + 1) * 256, :] = out[:, :COLS]
        grads[1024 + h * 256 : 1024 + (h + 1) * 256, :] = out[:, COLS:]
    for h in range(4):
        hs = slice(h * 256, (h + 1) * 256)
        out = lax.dot_general(normed[...], g_pre[hs, :], NT, preferred_element_type=F32).astype(BF16)
        grads[HALF + h * 512 : HALF + h * 512 + 256, :] = out[:, :COLS]
        grads[HALF + h * 512 + 256 : HALF + (h + 1) * 512, :] = out[:, COLS:]

    def remote(src, dst, sems, index, device):
        return pltpu.make_async_remote_copy(
            src_ref=src, dst_ref=dst, send_sem=sems.at[0, index], recv_sem=sems.at[1, index],
            device_id=device, device_id_type=MESH,
        )

    def each(n, make, act):
        def run(step, _):
            act(make(step))
            return 0

        lax.fori_loop(1, n, run, 0)

    def start(copy):
        copy.start()

    def wait(copy):
        copy.wait()

    def sent(copy):
        copy.wait_send()

    first = remote(grads.at[pl.ds(al(other * HALF, HALF), HALF)], pair_in, core_sems, 0, place.core_id)
    first.start()

    for r in range(ROWS):
        at = slice(PLACE[r] * COLS, (PLACE[r] + 1) * COLS)
        grad, x_hat = g_norm[:, at], x_hat_ref[:, at]
        mean = jnp.sum(grad, axis=0, keepdims=True) * (1.0 / C)
        proj = jnp.sum(grad * x_hat, axis=0, keepdims=True) * (1.0 / C)
        g_conv = inv_ref[pl.ds(r, 1), :] * (grad - mean - x_hat * proj)
        lay_row(r, g_conv.astype(BF16), ident, g_wide, g_rows, edge_f)
    lay_edges(edge_f, g_edges)
    g_copies = halo_copies(place, g_rows, g_edges, g_halo, g_rt, g_send, g_recv)
    halo_start(place, g_copies, g_edges, g_rt, g_recv)

    first.wait()

    def add_pair(i, _):
        at = pl.ds(al(i * 256, 256), 256)
        own = grads[pl.ds(al(core * HALF + i * 256, 256), 256), :].astype(F32)
        mine[at, :] = (own + pair_in[at, :].astype(F32)).astype(BF16)
        return 0

    lax.fori_loop(0, HALF // 256, add_pair, 0)

    def y_copy(step):
        peer, device = place.y_peer(step)
        return remote(mine.at[pl.ds(al(peer * rows_y, rows_y), rows_y)], y_in.at[step], y_sems, step, device)

    each(n_y, y_copy, start)

    tap_sums(wide, g_wide, tap_acc)
    for h in range(2):
        gk[h] = tap_acc[h].reshape(64, COLS)
    first_k = remote(gk.at[other], gk_pair, gk_core, 0, place.core_id)
    first_k.start()
    conv_inner(g_wide, backward, conv_t)

    each(n_y, y_copy, wait)

    def add_y(i, _):
        at = pl.ds(al(i * 128, 128), 128)
        total = mine[pl.ds(al(place.yi * rows_y + i * 128, 128), 128), :].astype(F32)
        for step in range(1, n_y):
            total = total + y_in[step, at, :].astype(F32)
        part[at, :] = total.astype(BF16)
        return 0

    lax.fori_loop(0, rows_y // 128, add_y, 0)

    def xz_copy(step):
        peer, device = place.xz_peer(step)
        return remote(part.at[pl.ds(al(peer * rows_xz, rows_xz), rows_xz)], xz_in.at[step], xz_sems, step, device)

    each(n_xz, xz_copy, start)

    first_k.wait()
    gk_mine[0] = (gk[core] + gk_pair[...]).astype(BF16)

    def gk_round(k, n, peer_of, slots, sems):
        def copy(step):
            return remote(gk_mine.at[k], slots.at[step], sems, step, peer_of(step))

        def finish():
            each(n, copy, wait)
            total = gk_mine[k].astype(F32)
            for step in range(1, n):
                total = total + slots[step].astype(F32)
            gk_mine[k + 1] = total.astype(BF16)

        each(n, copy, start)
        return finish

    gk_finish = gk_round(0, n_y, lambda step: place.y_peer(step)[1], gk_y, gk_y_sems)
    rim_wait(place, g_rt, g_recv)
    unpack_rim(place, g_rt, g_wide)
    conv_rim(g_wide, backward, conv_t)

    each(n_xz, xz_copy, wait)
    total = part[pl.ds(al(place.xz * rows_xz, rows_xz), rows_xz), :].astype(F32)
    for step in range(1, n_xz):
        total = total + xz_in[step].astype(F32)
    done[place.yi, place.xz] = total.astype(BF16)

    def xzg_copy(step):
        _, device = place.xz_peer(step)
        own = done.at[place.yi, place.xz]
        return remote(own, own, xzg_sems, step, device)

    each(n_xz, xzg_copy, start)
    gk_finish()
    gk_finish = gk_round(1, 4, place.x_peer, gk_x, gk_x_sems)

    for k in range(3):
        row_wait(place, k, g_halo, g_recv)
        unpack_row(place, k, g_halo, g_wide)

    def xzg_wait(step, _):
        sender = lax.rem(place.xz + n_xz - step, n_xz)
        wait_bytes(done.at[place.yi, sender], xzg_sems.at[1, step])
        return 0

    lax.fori_loop(1, n_xz, xzg_wait, 0)

    def yg_copy(step):
        _, device = place.y_peer(step)
        own = done.at[place.yi]
        return remote(own, own, yg_sems, step, device)

    def across(step, index):
        return remote(done.at[index], sums.at[index], last_sems, step, place.core_id)

    each(n_y, yg_copy, start)
    across(0, place.yi).start()

    gk_finish()
    gk_finish = gk_round(2, n_z, place.z_peer, gk_z, gk_z_sems)

    conv_halo(g_wide, backward, conv_t, HALO_ROWS)
    for r in range(ROWS):
        at = slice(r * COLS, (r + 1) * COLS)
        flat2[pl.ds(r, C, stride=8), :] = jnp.concatenate([conv_t[0, at, :].T, conv_t[1, at, :].T], axis=0)

    gk_finish()
    gk_all[core] = gk_mine[3]
    last_k = remote(gk_all.at[core], gk_all.at[core], gk_last_sems, 0, place.core_id)
    last_k.start()

    def out_body(group, _):
        at = pl.ds(group * 32, 32)
        rows_at = pl.ds(al(group * 256, 256), 256)
        moved = flat[rows_at, :].reshape(32, ROWS, COLS)
        stepped_ref[at] = (x_ref[at].astype(F32) + moved).astype(BF16)
        moved = flat2[rows_at, :].reshape(32, ROWS, COLS)
        state_ref[at] = (cot_ref[at].astype(F32) + moved).astype(BF16)
        return 0

    lax.fori_loop(0, C // 32, out_body, 0)

    def yg_wait(step, _):
        sender = lax.rem(place.yi + n_y - step, n_y)
        wait_bytes(done.at[sender], yg_sems.at[1, step])
        across(step, sender).start()
        return 0

    lax.fori_loop(1, n_y, yg_wait, 0)

    wait_bytes(gk_all.at[core], gk_last_sems.at[0, 0])
    wait_bytes(gk_all.at[other], gk_last_sems.at[1, 0])
    gk_out[...] = gk_all[...]
    sums_ref[core] = done[...]

    def last_wait(step, _):
        sender = lax.rem(place.yi + n_y - step, n_y)
        wait_bytes(done.at[sender], last_sems.at[0, step])
        wait_bytes(sums.at[sender], last_sems.at[1, step])
        return 0

    lax.fori_loop(0, n_y, last_wait, 0)
    sums_ref[other] = sums[...]

    each(n_xz, xzg_copy, sent)
    each(n_y, yg_copy, sent)
    halo_sent(place, copies)
    halo_sent(place, g_copies)


def finish_kernel(stepped_in, state_in, sums_ref, gk_ref, stepped_ref, state_ref, gk_out, gin_ref, gout_ref):
    stepped_ref[...] = stepped_in[...]
    state_ref[...] = state_in[...]
    for b in range(2):
        gout_ref[:, b * COLS : (b + 1) * COLS] = sums_ref[0, b * 1024 : (b + 1) * 1024, :].astype(F32)
    for b in range(8):
        gin_ref[:, b * COLS : (b + 1) * COLS] = sums_ref[1, b * 256 : (b + 1) * 256, :].astype(F32)
    for h in range(2):
        total = gk_ref[h].astype(F32)
        for t in range(49):
            a, q = t // 7, t % 7
            gk_out[t : t + 1, h * COLS : (h + 1) * COLS] = total[8 * q + a : 8 * q + a + 1]


def halo_scratch():
    return [
        pltpu.VMEM((2, 2, 32, C), BF16),
        pltpu.VMEM((2, 3, COLS, C), BF16),
        pltpu.VMEM((2, 4, 32, C), BF16),
        pltpu.SemaphoreType.DMA((12,)),
        pltpu.SemaphoreType.DMA((12,)),
    ]


def per_device(n_lon, n_lat, ocean_state, land_mask, kernel, w_in, w_out, cotangent):
    n_y, n_z, n_xz = n_lat // 2, n_lon // 4, n_lon
    rows_y, rows_xz = HALF // n_y, HALF // n_y // n_xz
    wide = pltpu.VMEM((2, 14, 144, COLS), F32)
    turned_rows = pltpu.VMEM((ROWS, COLS, C), BF16)
    table = pltpu.VMEM((2, 49, 8, COLS), F32)
    sems = lambda n: pltpu.SemaphoreType.DMA((2, n))
    summed = pltpu.VMEM((n_y, n_xz, rows_xz, COLS), BF16)
    flat = pltpu.VMEM((C * ROWS, COLS), F32)
    field = jax.ShapeDtypeStruct((C, ROWS, COLS), BF16)
    stepped, state, sums, gk = pl.pallas_call(
        functools.partial(whole_kernel, n_lon, n_lat),
        out_shape=(
            field,
            field,
            jax.ShapeDtypeStruct((2, n_y, n_xz, rows_xz, COLS), BF16),
            jax.ShapeDtypeStruct((2, 64, COLS), BF16),
        ),
        in_specs=[VSPEC] * 6,
        out_specs=(VSPEC,) * 4,
        scratch_shapes=[wide, turned_rows, pltpu.VMEM((2, 64, C), F32)]
        + halo_scratch()
        + [wide, turned_rows]
        + halo_scratch()
        + [
            table,
            table,
            pltpu.VMEM((HID, C), BF16),
            pltpu.VMEM((C, HID), BF16),
            flat,
            flat,
            pltpu.VMEM((2, CELLS, COLS), F32),
            pltpu.VMEM((C, CELLS), F32),
            pltpu.VMEM((C, CELLS), BF16),
            pltpu.VMEM((C, CELLS), BF16),
            pltpu.VMEM((HID, CELLS), BF16),
            pltpu.VMEM((HID, CELLS), BF16),
            pltpu.VMEM((C, CELLS), F32),
            pltpu.VMEM((ROWS, COLS), F32),
            pltpu.VMEM((2 * HALF, COLS), BF16),
            pltpu.VMEM((HALF, COLS), BF16),
            pltpu.VMEM((HALF, COLS), BF16),
            pltpu.VMEM((n_y, rows_y, COLS), BF16),
            pltpu.VMEM((rows_y, COLS), BF16),
            pltpu.VMEM((n_xz, rows_xz, COLS), BF16),
            summed,
            summed,
            pltpu.VMEM((2, 8, 8, COLS), F32),
            pltpu.VMEM((2, 64, COLS), F32),
            pltpu.VMEM((64, COLS), F32),
            pltpu.VMEM((4, 64, COLS), BF16),
            pltpu.VMEM((n_y, 64, COLS), BF16),
            pltpu.VMEM((4, 64, COLS), BF16),
            pltpu.VMEM((n_z, 64, COLS), BF16),
            pltpu.VMEM((2, 64, COLS), BF16),
            sems(1),
            sems(n_y),
            sems(n_xz),
            sems(n_xz),
            sems(n_y),
            sems(n_y),
            sems(1),
            sems(n_y),
            sems(4),
            sems(n_z),
            sems(1),
        ],
        compiler_params=pltpu.CompilerParams(
            collective_id=0, has_side_effects=True, vmem_limit_bytes=VMEM_LIMIT
        ),
        name="convnext",
    )(ocean_state, land_mask, kernel, w_in, w_out, cotangent)
    return pl.pallas_call(
        finish_kernel,
        out_shape=(
            field,
            field,
            jax.ShapeDtypeStruct((49, C), F32),
            jax.ShapeDtypeStruct((C, HID), F32),
            jax.ShapeDtypeStruct((HID, C), F32),
        ),
        in_specs=[VSPEC] * 4,
        out_specs=(VSPEC,) * 5,
        compiler_params=pltpu.CompilerParams(vmem_limit_bytes=VMEM_LIMIT),
        name="finish",
    )(stepped, state, sums.reshape(2, HALF, COLS), gk)


def solution(mesh):
    return jax.shard_map(
        functools.partial(per_device, mesh.shape["lon"], mesh.shape["lat"]),
        mesh=mesh,
        in_specs=(P(None, "lat", "lon"), P("lat", "lon"), P(), P(), P(), P(None, "lat", "lon")),
        out_specs=(P(None, "lat", "lon"), P(None, "lat", "lon"), P(), P(), P()),
        check_vma=False,
    )
```

```python
import functools

import jax
import jax.numpy as jnp
from jax import lax
from jax.experimental import pallas as pl
from jax.experimental.pallas import tpu as pltpu
from jax.sharding import PartitionSpec as P

F32 = jnp.float32
BF16 = jnp.bfloat16
MESH = pl.DeviceIdType.MESH
TANH_SLOPE = 0.7978845608028654
CUBIC = 0.044715
EPS = 1e-06
C = 256
HID = 1024
ROWS = 8
COLS = 128
CELLS = ROWS * COLS
HALF = 2048
VMEM_LIMIT = 56 * 1024 * 1024
VSPEC = pl.BlockSpec(memory_space=pltpu.VMEM)


def al(value, multiple):
    return pl.multiple_of(value, multiple)


def pick(flag, yes, no):
    return flag * yes + (1 - flag) * no


class Place:
    def __init__(self, n_lon, n_lat):
        self.n_lon, self.n_lat = n_lon, n_lat
        self.lon = lax.axis_index("lon")
        self.lat = lax.axis_index("lat")
        self.crown = (self.lat == n_lat - 1).astype(jnp.int32)
        self.floor = (self.lat == 0).astype(jnp.int32)
        east = lax.rem(self.lon + 1, n_lon)
        west = lax.rem(self.lon + n_lon - 1, n_lon)
        north = pick(self.crown, self.lat, self.lat + 1)
        south = lax.rem(self.lat + n_lat - 1, n_lat)
        mirror = n_lon - 1 - self.lon
        self.west_id = {"lon": west, "lat": self.lat}
        self.east_id = {"lon": east, "lat": self.lat}
        self.north_id = {"lon": pick(self.crown, mirror, self.lon), "lat": north}
        self.south_id = {"lon": self.lon, "lat": south}
        nw = pick(self.crown, lax.rem(n_lon - self.lon, n_lon), west)
        ne = pick(self.crown, lax.rem(2 * n_lon - 2 - self.lon, n_lon), east)
        self.nw_self = (self.crown == 1) & (nw == self.lon)
        self.ne_self = (self.crown == 1) & (ne == self.lon)
        self.nw_id = {"lon": nw, "lat": north}
        self.ne_id = {"lon": ne, "lat": north}
        self.sw_id = {"lon": west, "lat": south}
        self.se_id = {"lon": east, "lat": south}
        self.core = lax.rem(self.lon, 2)
        self.zi = self.lon // 4
        self.yi = self.lat // 2
        self.xi = lax.rem(self.lat, 2) * 2 + lax.rem(self.lon // 2, 2)
        self.n_y, self.n_z = n_lat // 2, n_lon // 4
        self.core_id = {"lon": self.lon + 1 - 2 * self.core, "lat": self.lat}

    def device(self, x, y, z):
        return {"lon": z * 4 + lax.rem(x, 2) * 2 + self.core, "lat": y * 2 + x // 2}

    def x_peer(self, step):
        return self.device(lax.rem(self.xi + step, 4), self.yi, self.zi)

    def z_peer(self, step):
        return self.device(self.xi, self.yi, lax.rem(self.zi + step, self.n_z))

    def y_peer(self, step):
        peer = lax.rem(self.yi + step, self.n_y)
        return peer, self.device(self.xi, peer, self.zi)

    def plane(self, ahead):
        return lax.rem(self.zi + ahead, self.n_z)

    def xz_peer(self, ahead, step):
        x = lax.rem(self.xi + step, 4)
        return x, self.device(x, self.yi, self.plane(ahead))


def signal(barrier, device):
    pl.semaphore_signal(barrier, inc=1, device_id=device, device_id_type=MESH)


def greet_halo(place, barrier):
    for device in (place.west_id, place.east_id, place.north_id):
        signal(barrier, device)

    @pl.when(jnp.logical_not(place.nw_self))
    def _():
        signal(barrier, place.nw_id)

    @pl.when(jnp.logical_not(place.ne_self))
    def _():
        signal(barrier, place.ne_id)

    @pl.when(place.floor == 0)
    def _():
        for device in (place.south_id, place.sw_id, place.se_id):
            signal(barrier, device)

    return (
        5
        - place.nw_self.astype(jnp.int32)
        - place.ne_self.astype(jnp.int32)
        + 3 * (1 - place.floor)
    )


def halo_copies(place, rows_ref, edges, halo_ref, rt_ref, send_sem, recv_sem):
    crown = place.crown

    def remote(src, dst, index, slot, device):
        return pltpu.make_async_remote_copy(
            src_ref=src,
            dst_ref=dst,
            send_sem=send_sem.at[index],
            recv_sem=recv_sem.at[slot],
            device_id=device,
            device_id_type=MESH,
        )

    return [
        remote(edges.at[0], rt_ref.at[1, pl.ds(1, 2)], 0, 0, place.west_id),
        remote(edges.at[1], rt_ref.at[0, pl.ds(1, 2)], 1, 1, place.east_id),
        remote(edges.at[0, 1], rt_ref.at[1 - crown, 3 * crown], 2, 2 + 3 * crown, place.nw_id),
        remote(edges.at[1, 1], rt_ref.at[crown, 3 * crown], 3, 3 + crown, place.ne_id),
        remote(edges.at[0, 0], rt_ref.at[1, 3], 4, 4, place.sw_id),
        remote(edges.at[1, 0], rt_ref.at[0, 3], 5, 5, place.se_id),
    ] + [
        remote(rows_ref.at[7 - k], halo_ref.at[crown, k], 6 + k, 6 + k + 3 * crown, place.north_id)
        for k in range(3)
    ] + [
        remote(rows_ref.at[k], halo_ref.at[1, k], 9 + k, 9 + k, place.south_id) for k in range(3)
    ]


def halo_start(place, copies, edges, rt_ref, recv_sem):
    copies[0].start()
    copies[1].start()
    for is_self, index, side, slot in ((place.nw_self, 2, 0, 5), (place.ne_self, 3, 1, 4)):

        @pl.when(is_self)
        def _(side=side, slot=slot):
            pltpu.make_async_copy(edges.at[side, 1], rt_ref.at[side, 3], recv_sem.at[slot]).start()

        @pl.when(jnp.logical_not(is_self))
        def _(index=index):
            copies[index].start()

    @pl.when(place.floor == 0)
    def _():
        copies[4].start()
        copies[5].start()


def row_start(place, copies, k):
    copies[6 + k].start()

    @pl.when(place.floor == 0)
    def _():
        copies[9 + k].start()


def wait_bytes(ref, sem):
    pltpu.make_async_copy(ref, ref, sem).wait()


def rim_wait(place, rt_ref, recv_sem):
    wait_bytes(rt_ref.at[1, pl.ds(1, 2)], recv_sem.at[0])
    wait_bytes(rt_ref.at[0, pl.ds(1, 2)], recv_sem.at[1])
    wait_bytes(rt_ref.at[1, 3], recv_sem.at[4])
    wait_bytes(rt_ref.at[0, 3], recv_sem.at[5])

    @pl.when(place.floor == 0)
    def _():
        wait_bytes(rt_ref.at[1, 0], recv_sem.at[2])
        wait_bytes(rt_ref.at[0, 0], recv_sem.at[3])


def row_wait(place, k, halo_ref, recv_sem):
    wait_bytes(halo_ref.at[1, k], recv_sem.at[9 + k])

    @pl.when(place.floor == 0)
    def _():
        wait_bytes(halo_ref.at[0, k], recv_sem.at[6 + k])


def halo_sent(place, copies):
    for index in (0, 1, 6, 7, 8):
        copies[index].wait_send()

    @pl.when(place.floor == 0)
    def _():
        for index in (4, 5, 9, 10, 11):
            copies[index].wait_send()

    for is_self, index in ((place.nw_self, 2), (place.ne_self, 3)):

        @pl.when(jnp.logical_not(is_self))
        def _(index=index):
            copies[index].wait_send()


NT = (((1,), (1,)), ((), ()))


def square(n, rule):
    source = lax.broadcasted_iota(jnp.int32, (n, n), 0)
    target = lax.broadcasted_iota(jnp.int32, (n, n), 1)
    return jnp.where(rule(source, target), 1.0, 0.0).astype(BF16)


def lay_row(i, row, ident, wide, rows_t, edge_f):
    turned = lax.dot_general(ident, row, NT, preferred_element_type=F32)
    wide[0, 3 + i, 8:136, :] = turned[:, :COLS]
    wide[1, 3 + i, 8:136, :] = turned[:, COLS:]
    rows_t[i] = turned.astype(BF16)
    edge_f[0, 8 * i : 8 * i + 8, :] = turned[:8]
    edge_f[1, 8 * i : 8 * i + 8, :] = turned[120:]


def lay_edges(edge_f, edges):
    for side in range(2):
        for b in range(2):
            edges[side, b] = edge_f[side, 32 * b : 32 * b + 32, :].astype(BF16)


def unpack_rim(place, rt_ref, wide):
    crown = place.crown == 1
    turn = square(32, lambda s, t: jnp.where(crown, 31 - s, s) == t)
    for side in range(2):
        at = slice(136 * side, 136 * side + 8)
        for b in range(4):
            if b == 3:
                block = jnp.dot(turn, rt_ref[side, b], preferred_element_type=F32)
            else:
                block = rt_ref[side, b].astype(F32)
            if b == 0:
                block = jnp.where(place.floor == 1, 0.0, block)
            for s in range(4):
                r = 4 * b + s - 1
                if 0 <= r < 14:
                    for h in range(2):
                        wide[h, r, at, :] = block[8 * s : 8 * s + 8, h * COLS : (h + 1) * COLS]


def unpack_row(place, k, halo_ref, wide):
    crown = place.crown == 1
    turn = square(COLS, lambda s, t: jnp.where(crown, COLS - 1 - s, s) == t)
    south = jnp.where(place.floor == 1, 0.0, halo_ref[0, k].astype(F32))
    north = jnp.dot(turn, halo_ref[1, k], preferred_element_type=F32)
    for h in range(2):
        wide[h, 2 - k, 8:136, :] = south[:, h * COLS : (h + 1) * COLS]
        wide[h, 11 + k, 8:136, :] = north[:, h * COLS : (h + 1) * COLS]


LOCAL_ROWS = tuple(range(3, 11))
HALO_ROWS = (0, 1, 2, 11, 12, 13)
PLACE = (6, 4, 2, 0, 1, 3, 5, 7)


def conv_block(wide, weight, out_ref, h, j, rows, add):
    at = [pl.ds(al(i * COLS + j * 8, 8), 8) for i in range(ROWS)]
    reached = [i for i in range(ROWS) if any(0 <= r - i < 7 for r in rows)]
    total = {i: out_ref[h, at[i], :] if add else None for i in reached}
    for q in range(7):
        for r in rows:
            moved = wide[h, r, pl.ds(j * 8 + (q + 5), 8), :]
            for a in range(7):
                i = r - a
                if 0 <= i < ROWS:
                    term = weight(h, a, q, r) * moved
                    total[i] = term if total[i] is None else total[i] + term
    for i in reached:
        out_ref[h, at[i], :] = total[i]


def conv_inner(wide, weight, out_ref, h):
    def body(n, _):
        conv_block(wide, weight, out_ref, h, n + 1, LOCAL_ROWS, False)
        return 0

    lax.fori_loop(0, 14, body, 0)


def conv_rim(wide, weight, out_ref):
    def body(n, _):
        conv_block(wide, weight, out_ref, n // 2, 15 * lax.rem(n, 2), LOCAL_ROWS, False)
        return 0

    lax.fori_loop(0, 4, body, 0)


def conv_halo(wide, weight, out_ref, rows):
    def body(j, _):
        for h in range(2):
            conv_block(wide, weight, out_ref, h, j, rows, True)
        return 0

    lax.fori_loop(0, 16, body, 0)


def tap_sums(wide, g_wide, out_ref):
    row_id = lax.broadcasted_iota(jnp.int32, (8, COLS), 0)

    def body(n, _):
        h, q = n // 7, lax.rem(n, 7)
        total = [None] * 7
        for j in range(16):
            grads = [g_wide[h, 3 + i, 8 + 8 * j : 16 + 8 * j, :] for i in range(ROWS)]
            for r in range(14):
                moved = wide[h, r, pl.ds(q + (8 * j + 5), 8), :]
                for a in range(7):
                    i = r - a
                    if 0 <= i < ROWS:
                        term = grads[i] * moved
                        total[a] = term if total[a] is None else total[a] + term
        tile = jnp.zeros((8, COLS), F32)
        for a in range(7):
            tile = jnp.where(row_id == a, jnp.sum(total[a], axis=0, keepdims=True), tile)
        out_ref[h, q] = tile
        return 0

    lax.fori_loop(0, 14, body, 0)
    for h in range(2):
        out_ref[h, 7] = jnp.zeros((8, COLS), F32)


def whole_kernel(
    n_lon, n_lat,
    x_ref, mask_ref, taps_ref, w_in_ref, w_out_ref, cot_ref,
    stepped_ref, state_ref, sums_ref, gk_out,
    wide, rows_t, edge_f, edges, halo, rt, send_sem, recv_sem,
    g_wide, g_rows, g_edges, g_halo, g_rt, g_send, g_recv,
    taps, taps_n, w_in_t, w_out_t, flat, flat2, conv_t, x_hat_ref, normed, gb, act, g_pre, g_norm, inv_ref,
    grads, pair_in, mine, y_in, part, xz_in, done, sums,
    tap_acc, gk, gk_pair, gk_mine, gk_y, gk_x, gk_z, gk_all,
    core_sems, y_sems, xz_sems, xzg_sems, yg_sems, last_sems, gk_core, gk_y_sems, gk_x_sems, gk_z_sems, gk_last_sems,
):
    place = Place(n_lon, n_lat)
    n_y, n_z = place.n_y, place.n_z
    rows_p = HALF // n_y // n_z
    rows_x = rows_p // 4
    near = sorted(range(n_z), key=lambda ahead: min(ahead, n_z - ahead))
    far = near[::-1]
    core, other = place.core, 1 - place.core

    barrier = pltpu.get_barrier_semaphore()
    count = greet_halo(place, barrier)
    signal(barrier, place.core_id)

    def greet_y(step, _):
        signal(barrier, place.y_peer(step)[1])
        return 0

    def greet_xz(n, _):
        signal(barrier, place.xz_peer(n // 4, lax.rem(n, 4))[1])
        return 0

    lax.fori_loop(1, n_y, greet_y, 0)
    lax.fori_loop(1, 4 * n_z, greet_xz, 0)

    ident = square(COLS, lambda s, t: s == t)
    flat[...] = x_ref[...].astype(F32).reshape(C * ROWS, COLS)
    for i in range(ROWS):
        lay_row(i, flat[pl.ds(i, C, stride=8), :].astype(BF16), ident, wide, rows_t, edge_f)
    lay_edges(edge_f, edges)
    crown = place.crown == 1
    table = taps_ref[...].astype(F32)
    for t in range(49):
        for h in range(2):
            taps[h, t] = jnp.broadcast_to(table[t : t + 1, h * COLS : (h + 1) * COLS], (8, COLS))
    for t in range(28, 49):
        for h in range(2):
            taps_n[h, t] = jnp.where(crown, taps[h, t], taps[h, 48 - t])

    def forward(h, a, q, r):
        return taps[h, 7 * a + q]

    def backward(h, a, q, r):
        return taps_n[h, 7 * a + q] if r >= 11 else taps[h, 48 - 7 * a - q]

    conv_inner(wide, forward, conv_t, 0)
    w_in_t[...] = w_in_ref[...].astype(F32).T.astype(BF16)
    w_out_t[...] = w_out_ref[...].astype(F32).T.astype(BF16)
    flat[...] = cot_ref[...].astype(F32).reshape(C * ROWS, COLS)
    for r in range(ROWS):
        ocean = mask_ref[pl.ds(r, 1), :].astype(F32)
        gb[:, PLACE[r] * COLS : (PLACE[r] + 1) * COLS] = (ocean * flat[pl.ds(r, C, stride=8), :]).astype(BF16)

    pl.semaphore_wait(barrier, count + n_y + 4 * n_z - 1)
    copies = halo_copies(place, rows_t, edges, halo, rt, send_sem, recv_sem)
    halo_start(place, copies, edges, rt, recv_sem)
    row_start(place, copies, 0)
    conv_inner(wide, forward, conv_t, 1)
    row_start(place, copies, 1)
    rim_wait(place, rt, recv_sem)
    unpack_rim(place, rt, wide)
    conv_rim(wide, forward, conv_t)
    row_start(place, copies, 2)

    def cells_body(n, _):
        for k in range(3):

            @pl.when(n == k + 1)
            def _(k=k):
                row_wait(place, k, halo, recv_sem)
                unpack_row(place, k, halo, wide)
                conv_halo(wide, forward, conv_t, (2 - k, 11 + k))

        at = pl.ds(al(n * 256, 256), 256)
        pair = (3 - n, 4 + n)
        for k, r in enumerate(pair):
            row_at = pl.ds(al(r * COLS, COLS), COLS)
            value = jnp.concatenate([conv_t[0, row_at, :].T, conv_t[1, row_at, :].T], axis=0)
            centred = value - jnp.sum(value, axis=0, keepdims=True) * (1.0 / C)
            var = jnp.sum(centred * centred, axis=0, keepdims=True) * (1.0 / C)
            inv = lax.rsqrt(var + EPS)
            inv_ref[pl.ds(r, 1), :] = inv
            x_hat = centred * inv
            x_hat_ref[:, pl.ds(al(n * 256 + k * COLS, COLS), COLS)] = x_hat
            normed[:, pl.ds(al(n * 256 + k * COLS, COLS), COLS)] = x_hat.astype(BF16)
        hat = normed[:, at]
        grad = gb[:, at]
        for h in range(4):
            hs = slice(h * 256, (h + 1) * 256)
            u = jnp.dot(w_in_t[hs, :], hat, preferred_element_type=F32)
            uu = u * u
            t = jnp.tanh(TANH_SLOPE * (u + CUBIC * (uu * u)))
            gate = 0.5 * (1.0 + t)
            act[hs, at] = (u * gate).astype(BF16)
            slope = gate + (0.5 * TANH_SLOPE) * u * (1.0 - t * t) * (1.0 + (3.0 * CUBIC) * uu)
            g_act = jnp.dot(w_out_ref[hs, :], grad, preferred_element_type=F32)
            g_pre[hs, at] = (g_act * slope).astype(BF16)
        return 0

    lax.fori_loop(0, ROWS // 2, cells_body, 0)

    for h in range(4):
        hs = slice(h * 256, (h + 1) * 256)
        out = lax.dot_general(act[hs, :], gb[...], NT, preferred_element_type=F32).astype(BF16)
        grads[h * 256 : (h + 1) * 256, :] = out[:, :COLS]
        grads[1024 + h * 256 : 1024 + (h + 1) * 256, :] = out[:, COLS:]
    for h in range(4):
        hs = slice(h * 256, (h + 1) * 256)
        out = lax.dot_general(normed[...], g_pre[hs, :], NT, preferred_element_type=F32).astype(BF16)
        grads[HALF + h * 512 : HALF + h * 512 + 256, :] = out[:, :COLS]
        grads[HALF + h * 512 + 256 : HALF + (h + 1) * 512, :] = out[:, COLS:]

    def remote(src, dst, sems, index, device):
        return pltpu.make_async_remote_copy(
            src_ref=src, dst_ref=dst, send_sem=sems.at[0, index], recv_sem=sems.at[1, index],
            device_id=device, device_id_type=MESH,
        )

    def each(n, make, act):
        def run(step, _):
            act(make(step))
            return 0

        lax.fori_loop(1, n, run, 0)

    def start(copy):
        copy.start()

    def wait(copy):
        copy.wait()

    def sent(copy):
        copy.wait_send()

    first = remote(grads.at[pl.ds(al(other * HALF, HALF), HALF)], pair_in, core_sems, 0, place.core_id)
    first.start()

    def norm_body(n, _):
        at = pl.ds(al(n * 256, 256), 256)
        g_norm[:, at] = jnp.dot(w_in_ref[...], g_pre[:, at], preferred_element_type=F32)
        return 0

    lax.fori_loop(0, ROWS // 2, norm_body, 0)
    for r in range(ROWS):
        at = slice(PLACE[r] * COLS, (PLACE[r] + 1) * COLS)
        grad, x_hat = g_norm[:, at], x_hat_ref[:, at]
        mean = jnp.sum(grad, axis=0, keepdims=True) * (1.0 / C)
        proj = jnp.sum(grad * x_hat, axis=0, keepdims=True) * (1.0 / C)
        g_conv = inv_ref[pl.ds(r, 1), :] * (grad - mean - x_hat * proj)
        lay_row(r, g_conv.astype(BF16), ident, g_wide, g_rows, edge_f)
    lay_edges(edge_f, g_edges)
    g_copies = halo_copies(place, g_rows, g_edges, g_halo, g_rt, g_send, g_recv)
    halo_start(place, g_copies, g_edges, g_rt, g_recv)
    for k in range(3):
        row_start(place, g_copies, k)

    first.wait()

    def add_pair(i, _):
        at = pl.ds(al(i * 256, 256), 256)
        own = grads[pl.ds(al(core * HALF + i * 256, 256), 256), :].astype(F32)
        mine[at, :] = (own + pair_in[at, :].astype(F32)).astype(BF16)
        return 0

    lax.fori_loop(0, HALF // 256, add_pair, 0)

    def y_copy(ahead, step):
        peer, device = place.y_peer(step)
        row = (peer * n_z + place.plane(ahead)) * rows_p
        return remote(mine.at[pl.ds(al(row, rows_p), rows_p)], y_in.at[ahead, step], y_sems, ahead * n_y + step, device)

    def plane_steps(ahead):
        return range(1 if ahead == 0 else 0, 4)

    for ahead in far:
        for step in range(1, n_y):
            y_copy(ahead, step).start()

    tap_sums(wide, g_wide, tap_acc)
    for h in range(2):
        gk[h] = tap_acc[h].reshape(64, COLS)
    first_k = remote(gk.at[other], gk_pair, gk_core, 0, place.core_id)
    first_k.start()

    def xz_copy(ahead, step):
        x, device = place.xz_peer(ahead, step)
        src = part.at[ahead, pl.ds(al(x * rows_x, rows_x), rows_x)]
        return remote(src, xz_in.at[ahead, step], xz_sems, ahead * 4 + step, device)

    for ahead in far:
        for step in range(1, n_y):
            y_copy(ahead, step).wait()
        own = pl.ds(al((place.yi * n_z + place.plane(ahead)) * rows_p, rows_p), rows_p)
        total = mine[own, :].astype(F32)
        for step in range(1, n_y):
            total = total + y_in[ahead, step].astype(F32)
        part[ahead] = total.astype(BF16)
        for step in plane_steps(ahead):
            xz_copy(ahead, step).start()

    for h in range(2):
        conv_inner(g_wide, backward, conv_t, h)

    def branch_body(n, _):
        branch = jnp.dot(w_out_t[...], act[:, pl.ds(al(n * 256, 256), 256)], preferred_element_type=F32)
        for k, r in enumerate((3 - n, 4 + n)):
            ocean = mask_ref[pl.ds(r, 1), :].astype(F32)
            flat[pl.ds(r, C, stride=8), :] = ocean * branch[:, k * COLS : (k + 1) * COLS]
        return 0

    lax.fori_loop(0, ROWS // 2, branch_body, 0)

    first_k.wait()
    gk_mine[0] = (gk[core] + gk_pair[...]).astype(BF16)

    def gk_round(k, n, peer_of, slots, sems):
        def copy(step):
            return remote(gk_mine.at[k], slots.at[step], sems, step, peer_of(step))

        def finish():
            each(n, copy, wait)
            total = gk_mine[k].astype(F32)
            for step in range(1, n):
                total = total + slots[step].astype(F32)
            gk_mine[k + 1] = total.astype(BF16)

        each(n, copy, start)
        return finish

    gk_finish = gk_round(0, n_y, lambda step: place.y_peer(step)[1], gk_y, gk_y_sems)
    rim_wait(place, g_rt, g_recv)
    unpack_rim(place, g_rt, g_wide)
    conv_rim(g_wide, backward, conv_t)

    for ahead in near:
        for step in plane_steps(ahead):
            xz_copy(ahead, step).wait()
    total = part[0, pl.ds(al(place.xi * rows_x, rows_x), rows_x), :].astype(F32)
    for ahead in near:
        for step in plane_steps(ahead):
            total = total + xz_in[ahead, step].astype(F32)
    done[place.yi, place.zi, place.xi] = total.astype(BF16)

    def xzg_copy(ahead, step):
        _, device = place.xz_peer(ahead, step)
        own = done.at[place.yi, place.zi, place.xi]
        return remote(own, own, xzg_sems, ahead * 4 + step, device)

    for ahead in far:
        for step in plane_steps(ahead):
            xzg_copy(ahead, step).start()
    gk_finish()
    gk_finish = gk_round(1, 4, place.x_peer, gk_x, gk_x_sems)

    for k in range(3):
        row_wait(place, k, g_halo, g_recv)
        unpack_row(place, k, g_halo, g_wide)
    conv_halo(g_wide, backward, conv_t, HALO_ROWS)
    for r in range(ROWS):
        at = slice(r * COLS, (r + 1) * COLS)
        flat2[pl.ds(r, C, stride=8), :] = jnp.concatenate([conv_t[0, at, :].T, conv_t[1, at, :].T], axis=0)

    def out_body(group, _):
        at = pl.ds(group * 32, 32)
        rows_at = pl.ds(al(group * 256, 256), 256)
        moved = flat[rows_at, :].reshape(32, ROWS, COLS)
        stepped_ref[at] = (x_ref[at].astype(F32) + moved).astype(BF16)
        moved = flat2[rows_at, :].reshape(32, ROWS, COLS)
        state_ref[at] = (cot_ref[at].astype(F32) + moved).astype(BF16)
        return 0

    lax.fori_loop(0, C // 32, out_body, 0)

    gk_finish()
    gk_finish = gk_round(2, n_z, place.z_peer, gk_z, gk_z_sems)

    def behind(ahead):
        return lax.rem(place.zi + n_z - ahead, n_z)

    def yg_copy(ahead, step):
        _, device = place.y_peer(step)
        own = done.at[place.yi, behind(ahead)]
        return remote(own, own, yg_sems, ahead * n_y + step, device)

    def across(ahead, step, y):
        whole = done.at[y, behind(ahead)], sums.at[y, behind(ahead)]
        return remote(*whole, last_sems, ahead * n_y + step, place.core_id)

    for ahead in near:
        for step in plane_steps(ahead):
            x = lax.rem(place.xi + 4 - step, 4)
            wait_bytes(done.at[place.yi, behind(ahead), x], xzg_sems.at[1, ahead * 4 + step])
        for step in range(1, n_y):
            yg_copy(ahead, step).start()
        across(ahead, 0, place.yi).start()

    for ahead in near:
        for step in range(1, n_y):
            y = lax.rem(place.yi + n_y - step, n_y)
            wait_bytes(done.at[y, behind(ahead)], yg_sems.at[1, ahead * n_y + step])
            across(ahead, step, y).start()

    gk_finish()
    gk_all[core] = gk_mine[3]
    last_k = remote(gk_all.at[core], gk_all.at[core], gk_last_sems, 0, place.core_id)
    last_k.start()

    wait_bytes(gk_all.at[core], gk_last_sems.at[0, 0])
    wait_bytes(gk_all.at[other], gk_last_sems.at[1, 0])
    gk_out[...] = gk_all[...]
    sums_ref[core] = done[...]

    for ahead in near:
        for step in range(n_y):
            y = lax.rem(place.yi + n_y - step, n_y)
            wait_bytes(done.at[y, behind(ahead)], last_sems.at[0, ahead * n_y + step])
            wait_bytes(sums.at[y, behind(ahead)], last_sems.at[1, ahead * n_y + step])
    sums_ref[other] = sums[...]

    for ahead in near:
        for step in plane_steps(ahead):
            xzg_copy(ahead, step).wait_send()
        for step in range(1, n_y):
            yg_copy(ahead, step).wait_send()
    halo_sent(place, copies)
    halo_sent(place, g_copies)


def finish_kernel(stepped_in, state_in, sums_ref, gk_ref, stepped_ref, state_ref, gk_out, gin_ref, gout_ref):
    stepped_ref[...] = stepped_in[...]
    state_ref[...] = state_in[...]
    for b in range(2):
        gout_ref[:, b * COLS : (b + 1) * COLS] = sums_ref[0, b * 1024 : (b + 1) * 1024, :].astype(F32)
    for b in range(8):
        gin_ref[:, b * COLS : (b + 1) * COLS] = sums_ref[1, b * 256 : (b + 1) * 256, :].astype(F32)
    for h in range(2):
        total = gk_ref[h].astype(F32)
        for t in range(49):
            a, q = t // 7, t % 7
            gk_out[t : t + 1, h * COLS : (h + 1) * COLS] = total[8 * q + a : 8 * q + a + 1]


def halo_scratch():
    return [
        pltpu.VMEM((2, 2, 32, C), BF16),
        pltpu.VMEM((2, 3, COLS, C), BF16),
        pltpu.VMEM((2, 4, 32, C), BF16),
        pltpu.SemaphoreType.DMA((12,)),
        pltpu.SemaphoreType.DMA((12,)),
    ]


def per_device(n_lon, n_lat, ocean_state, land_mask, kernel, w_in, w_out, cotangent):
    n_y, n_z = n_lat // 2, n_lon // 4
    rows_p = HALF // n_y // n_z
    wide = pltpu.VMEM((2, 14, 144, COLS), F32)
    turned_rows = pltpu.VMEM((ROWS, COLS, C), BF16)
    table = pltpu.VMEM((2, 49, 8, COLS), F32)
    sems = lambda n: pltpu.SemaphoreType.DMA((2, n))
    summed = pltpu.VMEM((n_y, n_z, 4, rows_p // 4, COLS), BF16)
    flat = pltpu.VMEM((C * ROWS, COLS), F32)
    field = jax.ShapeDtypeStruct((C, ROWS, COLS), BF16)
    stepped, state, sums, gk = pl.pallas_call(
        functools.partial(whole_kernel, n_lon, n_lat),
        out_shape=(
            field,
            field,
            jax.ShapeDtypeStruct((2, n_y, n_z, 4, rows_p // 4, COLS), BF16),
            jax.ShapeDtypeStruct((2, 64, COLS), BF16),
        ),
        in_specs=[VSPEC] * 6,
        out_specs=(VSPEC,) * 4,
        scratch_shapes=[wide, turned_rows, pltpu.VMEM((2, 64, C), F32)]
        + halo_scratch()
        + [wide, turned_rows]
        + halo_scratch()
        + [
            table,
            table,
            pltpu.VMEM((HID, C), BF16),
            pltpu.VMEM((C, HID), BF16),
            flat,
            flat,
            pltpu.VMEM((2, CELLS, COLS), F32),
            pltpu.VMEM((C, CELLS), F32),
            pltpu.VMEM((C, CELLS), BF16),
            pltpu.VMEM((C, CELLS), BF16),
            pltpu.VMEM((HID, CELLS), BF16),
            pltpu.VMEM((HID, CELLS), BF16),
            pltpu.VMEM((C, CELLS), F32),
            pltpu.VMEM((ROWS, COLS), F32),
            pltpu.VMEM((2 * HALF, COLS), BF16),
            pltpu.VMEM((HALF, COLS), BF16),
            pltpu.VMEM((HALF, COLS), BF16),
            pltpu.VMEM((n_z, n_y, rows_p, COLS), BF16),
            pltpu.VMEM((n_z, rows_p, COLS), BF16),
            pltpu.VMEM((n_z, 4, rows_p // 4, COLS), BF16),
            summed,
            summed,
            pltpu.VMEM((2, 8, 8, COLS), F32),
            pltpu.VMEM((2, 64, COLS), F32),
            pltpu.VMEM((64, COLS), F32),
            pltpu.VMEM((4, 64, COLS), BF16),
            pltpu.VMEM((n_y, 64, COLS), BF16),
            pltpu.VMEM((4, 64, COLS), BF16),
            pltpu.VMEM((n_z, 64, COLS), BF16),
            pltpu.VMEM((2, 64, COLS), BF16),
            sems(1),
            sems(n_z * n_y),
            sems(n_z * 4),
            sems(n_z * 4),
            sems(n_z * n_y),
            sems(n_z * n_y),
            sems(1),
            sems(n_y),
            sems(4),
            sems(n_z),
            sems(1),
        ],
        compiler_params=pltpu.CompilerParams(
            collective_id=0, has_side_effects=True, vmem_limit_bytes=VMEM_LIMIT
        ),
        name="convnext",
    )(ocean_state, land_mask, kernel, w_in, w_out, cotangent)
    return pl.pallas_call(
        finish_kernel,
        out_shape=(
            field,
            field,
            jax.ShapeDtypeStruct((49, C), F32),
            jax.ShapeDtypeStruct((C, HID), F32),
            jax.ShapeDtypeStruct((HID, C), F32),
        ),
        in_specs=[VSPEC] * 4,
        out_specs=(VSPEC,) * 5,
        compiler_params=pltpu.CompilerParams(vmem_limit_bytes=VMEM_LIMIT),
        name="finish",
    )(stepped, state, sums.reshape(2, HALF, COLS), gk)


def solution(mesh):
    return jax.shard_map(
        functools.partial(per_device, mesh.shape["lon"], mesh.shape["lat"]),
        mesh=mesh,
        in_specs=(P(None, "lat", "lon"), P("lat", "lon"), P(), P(), P(), P(None, "lat", "lon")),
        out_specs=(P(None, "lat", "lon"), P(None, "lat", "lon"), P(), P(), P()),
        check_vma=False,
    )
```

```python
import functools

import jax
import jax.numpy as jnp
from jax import lax
from jax.experimental import pallas as pl
from jax.experimental.pallas import tpu as pltpu
from jax.sharding import PartitionSpec as P

F32 = jnp.float32
BF16 = jnp.bfloat16
MESH = pl.DeviceIdType.MESH
TANH_SLOPE = 0.7978845608028654
CUBIC = 0.044715
EPS = 1e-06
C = 256
HID = 1024
ROWS = 8
COLS = 128
CELLS = ROWS * COLS
HALF = 2048
VMEM_LIMIT = 56 * 1024 * 1024
VSPEC = pl.BlockSpec(memory_space=pltpu.VMEM)


def al(value, multiple):
    return pl.multiple_of(value, multiple)


def pick(flag, yes, no):
    return flag * yes + (1 - flag) * no


class Place:
    def __init__(self, n_lon, n_lat):
        self.n_lon, self.n_lat = n_lon, n_lat
        self.lon = lax.axis_index("lon")
        self.lat = lax.axis_index("lat")
        self.crown = (self.lat == n_lat - 1).astype(jnp.int32)
        self.floor = (self.lat == 0).astype(jnp.int32)
        east = lax.rem(self.lon + 1, n_lon)
        west = lax.rem(self.lon + n_lon - 1, n_lon)
        north = pick(self.crown, self.lat, self.lat + 1)
        south = lax.rem(self.lat + n_lat - 1, n_lat)
        mirror = n_lon - 1 - self.lon
        self.west_id = {"lon": west, "lat": self.lat}
        self.east_id = {"lon": east, "lat": self.lat}
        self.north_id = {"lon": pick(self.crown, mirror, self.lon), "lat": north}
        self.south_id = {"lon": self.lon, "lat": south}
        nw = pick(self.crown, lax.rem(n_lon - self.lon, n_lon), west)
        ne = pick(self.crown, lax.rem(2 * n_lon - 2 - self.lon, n_lon), east)
        self.nw_self = (self.crown == 1) & (nw == self.lon)
        self.ne_self = (self.crown == 1) & (ne == self.lon)
        self.nw_id = {"lon": nw, "lat": north}
        self.ne_id = {"lon": ne, "lat": north}
        self.sw_id = {"lon": west, "lat": south}
        self.se_id = {"lon": east, "lat": south}
        self.core = lax.rem(self.lon, 2)
        self.zi = self.lon // 4
        self.yi = self.lat // 2
        self.xi = lax.rem(self.lat, 2) * 2 + lax.rem(self.lon // 2, 2)
        self.n_y, self.n_z = n_lat // 2, n_lon // 4
        self.core_id = {"lon": self.lon + 1 - 2 * self.core, "lat": self.lat}

    def device(self, x, y, z):
        return {"lon": z * 4 + lax.rem(x, 2) * 2 + self.core, "lat": y * 2 + x // 2}

    def x_peer(self, step):
        return self.device(lax.rem(self.xi + step, 4), self.yi, self.zi)

    def z_peer(self, step):
        return self.device(self.xi, self.yi, lax.rem(self.zi + step, self.n_z))

    def y_peer(self, step):
        peer = lax.rem(self.yi + step, self.n_y)
        return peer, self.device(self.xi, peer, self.zi)

    def plane(self, ahead):
        return lax.rem(self.zi + ahead, self.n_z)

    def xz_peer(self, ahead, step):
        x = lax.rem(self.xi + step, 4)
        return x, self.device(x, self.yi, self.plane(ahead))


def signal(barrier, device):
    pl.semaphore_signal(barrier, inc=1, device_id=device, device_id_type=MESH)


def greet_halo(place, barrier):
    for device in (place.west_id, place.east_id, place.north_id):
        signal(barrier, device)

    @pl.when(jnp.logical_not(place.nw_self))
    def _():
        signal(barrier, place.nw_id)

    @pl.when(jnp.logical_not(place.ne_self))
    def _():
        signal(barrier, place.ne_id)

    @pl.when(place.floor == 0)
    def _():
        for device in (place.south_id, place.sw_id, place.se_id):
            signal(barrier, device)

    return (
        5
        - place.nw_self.astype(jnp.int32)
        - place.ne_self.astype(jnp.int32)
        + 3 * (1 - place.floor)
    )


def halo_copies(place, rows_ref, edges, halo_ref, rt_ref, send_sem, recv_sem):
    crown = place.crown

    def remote(src, dst, index, slot, device):
        return pltpu.make_async_remote_copy(
            src_ref=src,
            dst_ref=dst,
            send_sem=send_sem.at[index],
            recv_sem=recv_sem.at[slot],
            device_id=device,
            device_id_type=MESH,
        )

    return [
        remote(edges.at[0], rt_ref.at[1, pl.ds(1, 2)], 0, 0, place.west_id),
        remote(edges.at[1], rt_ref.at[0, pl.ds(1, 2)], 1, 1, place.east_id),
        remote(edges.at[0, 1], rt_ref.at[1 - crown, 3 * crown], 2, 2 + 3 * crown, place.nw_id),
        remote(edges.at[1, 1], rt_ref.at[crown, 3 * crown], 3, 3 + crown, place.ne_id),
        remote(edges.at[0, 0], rt_ref.at[1, 3], 4, 4, place.sw_id),
        remote(edges.at[1, 0], rt_ref.at[0, 3], 5, 5, place.se_id),
    ] + [
        remote(rows_ref.at[7 - k], halo_ref.at[crown, k], 6 + k, 6 + k + 3 * crown, place.north_id)
        for k in range(3)
    ] + [
        remote(rows_ref.at[k], halo_ref.at[1, k], 9 + k, 9 + k, place.south_id) for k in range(3)
    ]


def halo_start(place, copies, edges, rt_ref, recv_sem):
    copies[0].start()
    copies[1].start()
    for is_self, index, side, slot in ((place.nw_self, 2, 0, 5), (place.ne_self, 3, 1, 4)):

        @pl.when(is_self)
        def _(side=side, slot=slot):
            pltpu.make_async_copy(edges.at[side, 1], rt_ref.at[side, 3], recv_sem.at[slot]).start()

        @pl.when(jnp.logical_not(is_self))
        def _(index=index):
            copies[index].start()

    @pl.when(place.floor == 0)
    def _():
        copies[4].start()
        copies[5].start()


def row_start(place, copies, k):
    copies[6 + k].start()

    @pl.when(place.floor == 0)
    def _():
        copies[9 + k].start()


def wait_bytes(ref, sem):
    pltpu.make_async_copy(ref, ref, sem).wait()


def rim_wait(place, rt_ref, recv_sem):
    wait_bytes(rt_ref.at[1, pl.ds(1, 2)], recv_sem.at[0])
    wait_bytes(rt_ref.at[0, pl.ds(1, 2)], recv_sem.at[1])
    wait_bytes(rt_ref.at[1, 3], recv_sem.at[4])
    wait_bytes(rt_ref.at[0, 3], recv_sem.at[5])

    @pl.when(place.floor == 0)
    def _():
        wait_bytes(rt_ref.at[1, 0], recv_sem.at[2])
        wait_bytes(rt_ref.at[0, 0], recv_sem.at[3])


def row_wait(place, k, halo_ref, recv_sem):
    wait_bytes(halo_ref.at[1, k], recv_sem.at[9 + k])

    @pl.when(place.floor == 0)
    def _():
        wait_bytes(halo_ref.at[0, k], recv_sem.at[6 + k])


def halo_sent(place, copies):
    for index in (0, 1, 6, 7, 8):
        copies[index].wait_send()

    @pl.when(place.floor == 0)
    def _():
        for index in (4, 5, 9, 10, 11):
            copies[index].wait_send()

    for is_self, index in ((place.nw_self, 2), (place.ne_self, 3)):

        @pl.when(jnp.logical_not(is_self))
        def _(index=index):
            copies[index].wait_send()


NT = (((1,), (1,)), ((), ()))


def square(n, rule):
    source = lax.broadcasted_iota(jnp.int32, (n, n), 0)
    target = lax.broadcasted_iota(jnp.int32, (n, n), 1)
    return jnp.where(rule(source, target), 1.0, 0.0).astype(BF16)


def lay_row(i, row, ident, wide, rows_t, edge_f):
    turned = lax.dot_general(ident, row, NT, preferred_element_type=F32)
    wide[0, 3 + i, 8:136, :] = turned[:, :COLS]
    wide[1, 3 + i, 8:136, :] = turned[:, COLS:]
    rows_t[i] = turned.astype(BF16)
    edge_f[0, 8 * i : 8 * i + 8, :] = turned[:8]
    edge_f[1, 8 * i : 8 * i + 8, :] = turned[120:]


def lay_edges(edge_f, edges):
    for side in range(2):
        for b in range(2):
            edges[side, b] = edge_f[side, 32 * b : 32 * b + 32, :].astype(BF16)


def unpack_rim(place, rt_ref, wide):
    crown = place.crown == 1
    turn = square(32, lambda s, t: jnp.where(crown, 31 - s, s) == t)
    for side in range(2):
        at = slice(136 * side, 136 * side + 8)
        for b in range(4):
            if b == 3:
                block = jnp.dot(turn, rt_ref[side, b], preferred_element_type=F32)
            else:
                block = rt_ref[side, b].astype(F32)
            if b == 0:
                block = jnp.where(place.floor == 1, 0.0, block)
            for s in range(4):
                r = 4 * b + s - 1
                if 0 <= r < 14:
                    for h in range(2):
                        wide[h, r, at, :] = block[8 * s : 8 * s + 8, h * COLS : (h + 1) * COLS]


def unpack_row(place, k, halo_ref, wide):
    crown = place.crown == 1
    turn = square(COLS, lambda s, t: jnp.where(crown, COLS - 1 - s, s) == t)
    south = jnp.where(place.floor == 1, 0.0, halo_ref[0, k].astype(F32))
    north = jnp.dot(turn, halo_ref[1, k], preferred_element_type=F32)
    for h in range(2):
        wide[h, 2 - k, 8:136, :] = south[:, h * COLS : (h + 1) * COLS]
        wide[h, 11 + k, 8:136, :] = north[:, h * COLS : (h + 1) * COLS]


LOCAL_ROWS = tuple(range(3, 11))
HALO_ROWS = (0, 1, 2, 11, 12, 13)
PLACE = (6, 4, 2, 0, 1, 3, 5, 7)


def conv_block(wide, weight, out_ref, h, j, rows, add):
    at = [pl.ds(al(i * COLS + j * 8, 8), 8) for i in range(ROWS)]
    reached = [i for i in range(ROWS) if any(0 <= r - i < 7 for r in rows)]
    total = {i: out_ref[h, at[i], :] if add else None for i in reached}
    for q in range(7):
        for r in rows:
            moved = wide[h, r, pl.ds(j * 8 + (q + 5), 8), :]
            for a in range(7):
                i = r - a
                if 0 <= i < ROWS:
                    term = weight(h, a, q, r) * moved
                    total[i] = term if total[i] is None else total[i] + term
    for i in reached:
        out_ref[h, at[i], :] = total[i]


def conv_inner(wide, weight, out_ref, h):
    def body(n, _):
        conv_block(wide, weight, out_ref, h, n + 1, LOCAL_ROWS, False)
        return 0

    lax.fori_loop(0, 14, body, 0)


def conv_rim(wide, weight, out_ref):
    def body(n, _):
        conv_block(wide, weight, out_ref, n // 2, 15 * lax.rem(n, 2), LOCAL_ROWS, False)
        return 0

    lax.fori_loop(0, 4, body, 0)


def conv_halo(wide, weight, out_ref, rows):
    def body(j, _):
        for h in range(2):
            conv_block(wide, weight, out_ref, h, j, rows, True)
        return 0

    lax.fori_loop(0, 16, body, 0)


def tap_sums(wide, g_wide, out_ref):
    row_id = lax.broadcasted_iota(jnp.int32, (8, COLS), 0)

    def body(n, _):
        h, q = n // 7, lax.rem(n, 7)
        total = [None] * 7
        for j in range(16):
            grads = [g_wide[h, 3 + i, 8 + 8 * j : 16 + 8 * j, :] for i in range(ROWS)]
            for r in range(14):
                moved = wide[h, r, pl.ds(q + (8 * j + 5), 8), :]
                for a in range(7):
                    i = r - a
                    if 0 <= i < ROWS:
                        term = grads[i] * moved
                        total[a] = term if total[a] is None else total[a] + term
        tile = jnp.zeros((8, COLS), F32)
        for a in range(7):
            tile = jnp.where(row_id == a, jnp.sum(total[a], axis=0, keepdims=True), tile)
        out_ref[h, q] = tile
        return 0

    lax.fori_loop(0, 14, body, 0)
    for h in range(2):
        out_ref[h, 7] = jnp.zeros((8, COLS), F32)


def whole_kernel(
    n_lon, n_lat,
    x_ref, mask_ref, taps_ref, w_in_ref, w_out_ref, cot_ref,
    stepped_ref, state_ref, sums_ref, gk_out,
    wide, rows_t, edge_f, edges, halo, rt, send_sem, recv_sem,
    g_wide, g_rows, g_edges, g_halo, g_rt, g_send, g_recv,
    taps, taps_n, w_in_t, w_out_t, flat, flat2, conv_t, x_hat_ref, normed, gb, act, g_pre, g_norm, inv_ref,
    grads, pair_in, mine, y_in, part, xz_in, done, sums,
    tap_acc, gk, gk_pair, gk_mine, gk_y, gk_x, gk_z, gk_all,
    core_sems, y_sems, xz_sems, xzg_sems, yg_sems, last_sems, gk_core, gk_y_sems, gk_x_sems, gk_z_sems, gk_last_sems,
):
    place = Place(n_lon, n_lat)
    n_y, n_z = place.n_y, place.n_z
    rows_p = HALF // n_y // n_z
    rows_x = rows_p // 4
    near = sorted(range(n_z), key=lambda ahead: min(ahead, n_z - ahead))
    far = near[::-1]
    core, other = place.core, 1 - place.core

    barrier = pltpu.get_barrier_semaphore()
    count = greet_halo(place, barrier)
    signal(barrier, place.core_id)

    def greet_y(step, _):
        signal(barrier, place.y_peer(step)[1])
        return 0

    def greet_xz(n, _):
        signal(barrier, place.xz_peer(n // 4, lax.rem(n, 4))[1])
        return 0

    lax.fori_loop(1, n_y, greet_y, 0)
    lax.fori_loop(1, 4 * n_z, greet_xz, 0)

    ident = square(COLS, lambda s, t: s == t)
    flat[...] = x_ref[...].astype(F32).reshape(C * ROWS, COLS)
    for i in range(ROWS):
        lay_row(i, flat[pl.ds(i, C, stride=8), :].astype(BF16), ident, wide, rows_t, edge_f)
    lay_edges(edge_f, edges)
    w_in_t[...] = w_in_ref[...].astype(F32).T.astype(BF16)
    w_out_t[...] = w_out_ref[...].astype(F32).T.astype(BF16)
    pl.semaphore_wait(barrier, count + n_y + 4 * n_z - 1)
    copies = halo_copies(place, rows_t, edges, halo, rt, send_sem, recv_sem)
    halo_start(place, copies, edges, rt, recv_sem)
    for k in range(3):
        row_start(place, copies, k)

    crown = place.crown == 1
    table = taps_ref[...].astype(F32)
    for t in range(49):
        for h in range(2):
            taps[h, t] = jnp.broadcast_to(table[t : t + 1, h * COLS : (h + 1) * COLS], (8, COLS))
    for t in range(28, 49):
        for h in range(2):
            taps_n[h, t] = jnp.where(crown, taps[h, t], taps[h, 48 - t])

    def forward(h, a, q, r):
        return taps[h, 7 * a + q]

    def backward(h, a, q, r):
        return taps_n[h, 7 * a + q] if r >= 11 else taps[h, 48 - 7 * a - q]

    for h in range(2):
        conv_inner(wide, forward, conv_t, h)
    flat[...] = cot_ref[...].astype(F32).reshape(C * ROWS, COLS)
    for r in range(ROWS):
        ocean = mask_ref[pl.ds(r, 1), :].astype(F32)
        gb[:, PLACE[r] * COLS : (PLACE[r] + 1) * COLS] = (ocean * flat[pl.ds(r, C, stride=8), :]).astype(BF16)

    rim_wait(place, rt, recv_sem)
    unpack_rim(place, rt, wide)
    conv_rim(wide, forward, conv_t)

    def cells_body(n, _):
        for k in range(3):

            @pl.when(n == k + 1)
            def _(k=k):
                row_wait(place, k, halo, recv_sem)
                unpack_row(place, k, halo, wide)
                conv_halo(wide, forward, conv_t, (2 - k, 11 + k))

        at = pl.ds(al(n * 256, 256), 256)
        pair = (3 - n, 4 + n)
        for k, r in enumerate(pair):
            row_at = pl.ds(al(r * COLS, COLS), COLS)
            value = jnp.concatenate([conv_t[0, row_at, :].T, conv_t[1, row_at, :].T], axis=0)
            centred = value - jnp.sum(value, axis=0, keepdims=True) * (1.0 / C)
            var = jnp.sum(centred * centred, axis=0, keepdims=True) * (1.0 / C)
            inv = lax.rsqrt(var + EPS)
            inv_ref[pl.ds(r, 1), :] = inv
            x_hat = centred * inv
            x_hat_ref[:, pl.ds(al(n * 256 + k * COLS, COLS), COLS)] = x_hat
            normed[:, pl.ds(al(n * 256 + k * COLS, COLS), COLS)] = x_hat.astype(BF16)
        hat = normed[:, at]
        grad = gb[:, at]
        for h in range(4):
            hs = slice(h * 256, (h + 1) * 256)
            u = jnp.dot(w_in_t[hs, :], hat, preferred_element_type=F32)
            uu = u * u
            t = jnp.tanh(TANH_SLOPE * (u + CUBIC * (uu * u)))
            gate = 0.5 * (1.0 + t)
            act[hs, at] = (u * gate).astype(BF16)
            slope = gate + (0.5 * TANH_SLOPE) * u * (1.0 - t * t) * (1.0 + (3.0 * CUBIC) * uu)
            g_act = jnp.dot(w_out_ref[hs, :], grad, preferred_element_type=F32)
            g_pre[hs, at] = (g_act * slope).astype(BF16)
        return 0

    lax.fori_loop(0, ROWS // 2, cells_body, 0)

    for h in range(4):
        hs = slice(h * 256, (h + 1) * 256)
        out = lax.dot_general(act[hs, :], gb[...], NT, preferred_element_type=F32).astype(BF16)
        grads[h * 256 : (h + 1) * 256, :] = out[:, :COLS]
        grads[1024 + h * 256 : 1024 + (h + 1) * 256, :] = out[:, COLS:]
    for h in range(4):
        hs = slice(h * 256, (h + 1) * 256)
        out = lax.dot_general(normed[...], g_pre[hs, :], NT, preferred_element_type=F32).astype(BF16)
        grads[HALF + h * 512 : HALF + h * 512 + 256, :] = out[:, :COLS]
        grads[HALF + h * 512 + 256 : HALF + (h + 1) * 512, :] = out[:, COLS:]

    def remote(src, dst, sems, index, device):
        return pltpu.make_async_remote_copy(
            src_ref=src, dst_ref=dst, send_sem=sems.at[0, index], recv_sem=sems.at[1, index],
            device_id=device, device_id_type=MESH,
        )

    def each(n, make, act):
        def run(step, _):
            act(make(step))
            return 0

        lax.fori_loop(1, n, run, 0)

    def start(copy):
        copy.start()

    def wait(copy):
        copy.wait()

    def sent(copy):
        copy.wait_send()

    first = remote(grads.at[pl.ds(al(other * HALF, HALF), HALF)], pair_in, core_sems, 0, place.core_id)
    first.start()

    def norm_body(n, _):
        at = pl.ds(al(n * 256, 256), 256)
        g_norm[:, at] = jnp.dot(w_in_ref[...], g_pre[:, at], preferred_element_type=F32)
        return 0

    lax.fori_loop(0, ROWS // 2, norm_body, 0)
    for r in range(ROWS):
        at = slice(PLACE[r] * COLS, (PLACE[r] + 1) * COLS)
        grad, x_hat = g_norm[:, at], x_hat_ref[:, at]
        mean = jnp.sum(grad, axis=0, keepdims=True) * (1.0 / C)
        proj = jnp.sum(grad * x_hat, axis=0, keepdims=True) * (1.0 / C)
        g_conv = inv_ref[pl.ds(r, 1), :] * (grad - mean - x_hat * proj)
        lay_row(r, g_conv.astype(BF16), ident, g_wide, g_rows, edge_f)
    lay_edges(edge_f, g_edges)
    g_copies = halo_copies(place, g_rows, g_edges, g_halo, g_rt, g_send, g_recv)

    first.wait()

    def add_pair(i, _):
        at = pl.ds(al(i * 256, 256), 256)
        own = grads[pl.ds(al(core * HALF + i * 256, 256), 256), :].astype(F32)
        mine[at, :] = (own + pair_in[at, :].astype(F32)).astype(BF16)
        return 0

    lax.fori_loop(0, HALF // 256, add_pair, 0)

    def y_copy(ahead, step):
        peer, device = place.y_peer(step)
        row = (peer * n_z + place.plane(ahead)) * rows_p
        return remote(mine.at[pl.ds(al(row, rows_p), rows_p)], y_in.at[ahead, step], y_sems, ahead * n_y + step, device)

    def plane_steps(ahead):
        return range(1 if ahead == 0 else 0, 4)

    for ahead in far:
        for step in range(1, n_y):
            y_copy(ahead, step).start()

    tap_sums(wide, g_wide, tap_acc)
    for h in range(2):
        gk[h] = tap_acc[h].reshape(64, COLS)
    first_k = remote(gk.at[other], gk_pair, gk_core, 0, place.core_id)
    first_k.start()

    def xz_copy(ahead, step):
        x, device = place.xz_peer(ahead, step)
        src = part.at[ahead, pl.ds(al(x * rows_x, rows_x), rows_x)]
        return remote(src, xz_in.at[ahead, step], xz_sems, ahead * 4 + step, device)

    for ahead in far:
        for step in range(1, n_y):
            y_copy(ahead, step).wait()
        own = pl.ds(al((place.yi * n_z + place.plane(ahead)) * rows_p, rows_p), rows_p)
        total = mine[own, :].astype(F32)
        for step in range(1, n_y):
            total = total + y_in[ahead, step].astype(F32)
        part[ahead] = total.astype(BF16)
        for step in plane_steps(ahead):
            xz_copy(ahead, step).start()
    halo_start(place, g_copies, g_edges, g_rt, g_recv)
    for k in range(3):
        row_start(place, g_copies, k)

    for h in range(2):
        conv_inner(g_wide, backward, conv_t, h)

    def branch_body(n, _):
        branch = jnp.dot(w_out_t[...], act[:, pl.ds(al(n * 256, 256), 256)], preferred_element_type=F32)
        for k, r in enumerate((3 - n, 4 + n)):
            ocean = mask_ref[pl.ds(r, 1), :].astype(F32)
            flat[pl.ds(r, C, stride=8), :] = ocean * branch[:, k * COLS : (k + 1) * COLS]
        return 0

    lax.fori_loop(0, ROWS // 2, branch_body, 0)

    first_k.wait()
    gk_mine[0] = (gk[core] + gk_pair[...]).astype(BF16)

    def gk_round(k, n, peer_of, slots, sems):
        def copy(step):
            return remote(gk_mine.at[k], slots.at[step], sems, step, peer_of(step))

        def finish():
            each(n, copy, wait)
            total = gk_mine[k].astype(F32)
            for step in range(1, n):
                total = total + slots[step].astype(F32)
            gk_mine[k + 1] = total.astype(BF16)

        each(n, copy, start)
        return finish

    gk_finish = gk_round(0, n_y, lambda step: place.y_peer(step)[1], gk_y, gk_y_sems)

    for ahead in near:
        for step in plane_steps(ahead):
            xz_copy(ahead, step).wait()
    total = part[0, pl.ds(al(place.xi * rows_x, rows_x), rows_x), :].astype(F32)
    for ahead in near:
        for step in plane_steps(ahead):
            total = total + xz_in[ahead, step].astype(F32)
    done[place.yi, place.zi, place.xi] = total.astype(BF16)

    def xzg_copy(ahead, step):
        _, device = place.xz_peer(ahead, step)
        own = done.at[place.yi, place.zi, place.xi]
        return remote(own, own, xzg_sems, ahead * 4 + step, device)

    for ahead in far:
        for step in plane_steps(ahead):
            xzg_copy(ahead, step).start()
    gk_finish()
    gk_finish = gk_round(1, 4, place.x_peer, gk_x, gk_x_sems)

    rim_wait(place, g_rt, g_recv)
    unpack_rim(place, g_rt, g_wide)
    conv_rim(g_wide, backward, conv_t)

    def behind(ahead):
        return lax.rem(place.zi + n_z - ahead, n_z)

    def yg_copy(ahead, step):
        _, device = place.y_peer(step)
        own = done.at[place.yi, behind(ahead)]
        return remote(own, own, yg_sems, ahead * n_y + step, device)

    def across(ahead, step, y):
        whole = done.at[y, behind(ahead)], sums.at[y, behind(ahead)]
        return remote(*whole, last_sems, ahead * n_y + step, place.core_id)

    for ahead in near:
        for step in plane_steps(ahead):
            x = lax.rem(place.xi + 4 - step, 4)
            wait_bytes(done.at[place.yi, behind(ahead), x], xzg_sems.at[1, ahead * 4 + step])
        for step in range(1, n_y):
            yg_copy(ahead, step).start()
        across(ahead, 0, place.yi).start()

    gk_finish()
    gk_finish = gk_round(2, n_z, place.z_peer, gk_z, gk_z_sems)
    for k in range(3):
        row_wait(place, k, g_halo, g_recv)
        unpack_row(place, k, g_halo, g_wide)
    conv_halo(g_wide, backward, conv_t, HALO_ROWS)
    for r in range(ROWS):
        at = slice(r * COLS, (r + 1) * COLS)
        flat2[pl.ds(r, C, stride=8), :] = jnp.concatenate([conv_t[0, at, :].T, conv_t[1, at, :].T], axis=0)

    def out_body(group, _):
        at = pl.ds(group * 32, 32)
        rows_at = pl.ds(al(group * 256, 256), 256)
        moved = flat[rows_at, :].reshape(32, ROWS, COLS)
        stepped_ref[at] = (x_ref[at].astype(F32) + moved).astype(BF16)
        moved = flat2[rows_at, :].reshape(32, ROWS, COLS)
        state_ref[at] = (cot_ref[at].astype(F32) + moved).astype(BF16)
        return 0

    lax.fori_loop(0, C // 32, out_body, 0)

    for ahead in near:
        for step in range(1, n_y):
            y = lax.rem(place.yi + n_y - step, n_y)
            wait_bytes(done.at[y, behind(ahead)], yg_sems.at[1, ahead * n_y + step])
            across(ahead, step, y).start()

    gk_finish()
    gk_all[core] = gk_mine[3]
    last_k = remote(gk_all.at[core], gk_all.at[core], gk_last_sems, 0, place.core_id)
    last_k.start()

    wait_bytes(gk_all.at[core], gk_last_sems.at[0, 0])
    wait_bytes(gk_all.at[other], gk_last_sems.at[1, 0])
    gk_out[...] = gk_all[...]
    sums_ref[core] = done[...]

    for ahead in near:
        for step in range(n_y):
            y = lax.rem(place.yi + n_y - step, n_y)
            wait_bytes(done.at[y, behind(ahead)], last_sems.at[0, ahead * n_y + step])
            wait_bytes(sums.at[y, behind(ahead)], last_sems.at[1, ahead * n_y + step])
    sums_ref[other] = sums[...]

    for ahead in near:
        for step in plane_steps(ahead):
            xzg_copy(ahead, step).wait_send()
        for step in range(1, n_y):
            yg_copy(ahead, step).wait_send()
    halo_sent(place, copies)
    halo_sent(place, g_copies)


def finish_kernel(stepped_in, state_in, sums_ref, gk_ref, stepped_ref, state_ref, gk_out, gin_ref, gout_ref):
    stepped_ref[...] = stepped_in[...]
    state_ref[...] = state_in[...]
    for b in range(2):
        gout_ref[:, b * COLS : (b + 1) * COLS] = sums_ref[0, b * 1024 : (b + 1) * 1024, :].astype(F32)
    for b in range(8):
        gin_ref[:, b * COLS : (b + 1) * COLS] = sums_ref[1, b * 256 : (b + 1) * 256, :].astype(F32)
    for h in range(2):
        total = gk_ref[h].astype(F32)
        for t in range(49):
            a, q = t // 7, t % 7
            gk_out[t : t + 1, h * COLS : (h + 1) * COLS] = total[8 * q + a : 8 * q + a + 1]


def halo_scratch():
    return [
        pltpu.VMEM((2, 2, 32, C), BF16),
        pltpu.VMEM((2, 3, COLS, C), BF16),
        pltpu.VMEM((2, 4, 32, C), BF16),
        pltpu.SemaphoreType.DMA((12,)),
        pltpu.SemaphoreType.DMA((12,)),
    ]


def per_device(n_lon, n_lat, ocean_state, land_mask, kernel, w_in, w_out, cotangent):
    n_y, n_z = n_lat // 2, n_lon // 4
    rows_p = HALF // n_y // n_z
    wide = pltpu.VMEM((2, 14, 144, COLS), F32)
    turned_rows = pltpu.VMEM((ROWS, COLS, C), BF16)
    table = pltpu.VMEM((2, 49, 8, COLS), F32)
    sems = lambda n: pltpu.SemaphoreType.DMA((2, n))
    summed = pltpu.VMEM((n_y, n_z, 4, rows_p // 4, COLS), BF16)
    flat = pltpu.VMEM((C * ROWS, COLS), F32)
    field = jax.ShapeDtypeStruct((C, ROWS, COLS), BF16)
    stepped, state, sums, gk = pl.pallas_call(
        functools.partial(whole_kernel, n_lon, n_lat),
        out_shape=(
            field,
            field,
            jax.ShapeDtypeStruct((2, n_y, n_z, 4, rows_p // 4, COLS), BF16),
            jax.ShapeDtypeStruct((2, 64, COLS), BF16),
        ),
        in_specs=[VSPEC] * 6,
        out_specs=(VSPEC,) * 4,
        scratch_shapes=[wide, turned_rows, pltpu.VMEM((2, 64, C), F32)]
        + halo_scratch()
        + [wide, turned_rows]
        + halo_scratch()
        + [
            table,
            table,
            pltpu.VMEM((HID, C), BF16),
            pltpu.VMEM((C, HID), BF16),
            flat,
            flat,
            pltpu.VMEM((2, CELLS, COLS), F32),
            pltpu.VMEM((C, CELLS), F32),
            pltpu.VMEM((C, CELLS), BF16),
            pltpu.VMEM((C, CELLS), BF16),
            pltpu.VMEM((HID, CELLS), BF16),
            pltpu.VMEM((HID, CELLS), BF16),
            pltpu.VMEM((C, CELLS), F32),
            pltpu.VMEM((ROWS, COLS), F32),
            pltpu.VMEM((2 * HALF, COLS), BF16),
            pltpu.VMEM((HALF, COLS), BF16),
            pltpu.VMEM((HALF, COLS), BF16),
            pltpu.VMEM((n_z, n_y, rows_p, COLS), BF16),
            pltpu.VMEM((n_z, rows_p, COLS), BF16),
            pltpu.VMEM((n_z, 4, rows_p // 4, COLS), BF16),
            summed,
            summed,
            pltpu.VMEM((2, 8, 8, COLS), F32),
            pltpu.VMEM((2, 64, COLS), F32),
            pltpu.VMEM((64, COLS), F32),
            pltpu.VMEM((4, 64, COLS), BF16),
            pltpu.VMEM((n_y, 64, COLS), BF16),
            pltpu.VMEM((4, 64, COLS), BF16),
            pltpu.VMEM((n_z, 64, COLS), BF16),
            pltpu.VMEM((2, 64, COLS), BF16),
            sems(1),
            sems(n_z * n_y),
            sems(n_z * 4),
            sems(n_z * 4),
            sems(n_z * n_y),
            sems(n_z * n_y),
            sems(1),
            sems(n_y),
            sems(4),
            sems(n_z),
            sems(1),
        ],
        compiler_params=pltpu.CompilerParams(
            collective_id=0, has_side_effects=True, vmem_limit_bytes=VMEM_LIMIT
        ),
        name="convnext",
    )(ocean_state, land_mask, kernel, w_in, w_out, cotangent)
    return pl.pallas_call(
        finish_kernel,
        out_shape=(
            field,
            field,
            jax.ShapeDtypeStruct((49, C), F32),
            jax.ShapeDtypeStruct((C, HID), F32),
            jax.ShapeDtypeStruct((HID, C), F32),
        ),
        in_specs=[VSPEC] * 4,
        out_specs=(VSPEC,) * 5,
        compiler_params=pltpu.CompilerParams(vmem_limit_bytes=VMEM_LIMIT),
        name="finish",
    )(stepped, state, sums.reshape(2, HALF, COLS), gk)


def solution(mesh):
    return jax.shard_map(
        functools.partial(per_device, mesh.shape["lon"], mesh.shape["lat"]),
        mesh=mesh,
        in_specs=(P(None, "lat", "lon"), P("lat", "lon"), P(), P(), P(), P(None, "lat", "lon")),
        out_specs=(P(None, "lat", "lon"), P(None, "lat", "lon"), P(), P(), P()),
        check_vma=False,
    )
```

```python
import functools

import jax
import jax.numpy as jnp
from jax import lax
from jax.experimental import pallas as pl
from jax.experimental.pallas import tpu as pltpu
from jax.sharding import PartitionSpec as P

F32 = jnp.float32
BF16 = jnp.bfloat16
MESH = pl.DeviceIdType.MESH
TANH_SLOPE = 0.7978845608028654
CUBIC = 0.044715
EPS = 1e-06
C = 256
HID = 1024
ROWS = 8
COLS = 128
CELLS = ROWS * COLS
HALF = 2048
VMEM_LIMIT = 56 * 1024 * 1024
VSPEC = pl.BlockSpec(memory_space=pltpu.VMEM)


def al(value, multiple):
    return pl.multiple_of(value, multiple)


def pick(flag, yes, no):
    return flag * yes + (1 - flag) * no


class Place:
    def __init__(self, n_lon, n_lat):
        self.n_lon, self.n_lat = n_lon, n_lat
        self.lon = lax.axis_index("lon")
        self.lat = lax.axis_index("lat")
        self.crown = (self.lat == n_lat - 1).astype(jnp.int32)
        self.floor = (self.lat == 0).astype(jnp.int32)
        east = lax.rem(self.lon + 1, n_lon)
        west = lax.rem(self.lon + n_lon - 1, n_lon)
        north = pick(self.crown, self.lat, self.lat + 1)
        south = lax.rem(self.lat + n_lat - 1, n_lat)
        mirror = n_lon - 1 - self.lon
        self.west_id = {"lon": west, "lat": self.lat}
        self.east_id = {"lon": east, "lat": self.lat}
        self.north_id = {"lon": pick(self.crown, mirror, self.lon), "lat": north}
        self.south_id = {"lon": self.lon, "lat": south}
        nw = pick(self.crown, lax.rem(n_lon - self.lon, n_lon), west)
        ne = pick(self.crown, lax.rem(2 * n_lon - 2 - self.lon, n_lon), east)
        self.nw_self = (self.crown == 1) & (nw == self.lon)
        self.ne_self = (self.crown == 1) & (ne == self.lon)
        self.nw_id = {"lon": nw, "lat": north}
        self.ne_id = {"lon": ne, "lat": north}
        self.sw_id = {"lon": west, "lat": south}
        self.se_id = {"lon": east, "lat": south}
        self.core = lax.rem(self.lon, 2)
        self.zi = self.lon // 4
        self.yi = self.lat // 2
        self.xi = lax.rem(self.lat, 2) * 2 + lax.rem(self.lon // 2, 2)
        self.n_y, self.n_z = n_lat // 2, n_lon // 4
        self.core_id = {"lon": self.lon + 1 - 2 * self.core, "lat": self.lat}

    def device(self, x, y, z):
        return {"lon": z * 4 + lax.rem(x, 2) * 2 + self.core, "lat": y * 2 + x // 2}

    def x_peer(self, step):
        return self.device(lax.rem(self.xi + step, 4), self.yi, self.zi)

    def z_peer(self, step):
        return self.device(self.xi, self.yi, lax.rem(self.zi + step, self.n_z))

    def y_peer(self, step):
        peer = lax.rem(self.yi + step, self.n_y)
        return peer, self.device(self.xi, peer, self.zi)

    def plane(self, ahead):
        return lax.rem(self.zi + ahead, self.n_z)

    def xz_peer(self, ahead, step):
        x = lax.rem(self.xi + step, 4)
        return x, self.device(x, self.yi, self.plane(ahead))


def signal(barrier, device):
    pl.semaphore_signal(barrier, inc=1, device_id=device, device_id_type=MESH)


def greet_halo(place, barrier):
    for device in (place.west_id, place.east_id, place.north_id):
        signal(barrier, device)

    @pl.when(jnp.logical_not(place.nw_self))
    def _():
        signal(barrier, place.nw_id)

    @pl.when(jnp.logical_not(place.ne_self))
    def _():
        signal(barrier, place.ne_id)

    @pl.when(place.floor == 0)
    def _():
        for device in (place.south_id, place.sw_id, place.se_id):
            signal(barrier, device)

    return (
        5
        - place.nw_self.astype(jnp.int32)
        - place.ne_self.astype(jnp.int32)
        + 3 * (1 - place.floor)
    )


def halo_copies(place, rows_ref, edges, halo_ref, rt_ref, send_sem, recv_sem):
    crown = place.crown

    def remote(src, dst, index, slot, device):
        return pltpu.make_async_remote_copy(
            src_ref=src,
            dst_ref=dst,
            send_sem=send_sem.at[index],
            recv_sem=recv_sem.at[slot],
            device_id=device,
            device_id_type=MESH,
        )

    return [
        remote(edges.at[0], rt_ref.at[1, pl.ds(1, 2)], 0, 0, place.west_id),
        remote(edges.at[1], rt_ref.at[0, pl.ds(1, 2)], 1, 1, place.east_id),
        remote(edges.at[0, 1], rt_ref.at[1 - crown, 3 * crown], 2, 2 + 3 * crown, place.nw_id),
        remote(edges.at[1, 1], rt_ref.at[crown, 3 * crown], 3, 3 + crown, place.ne_id),
        remote(edges.at[0, 0], rt_ref.at[1, 3], 4, 4, place.sw_id),
        remote(edges.at[1, 0], rt_ref.at[0, 3], 5, 5, place.se_id),
    ] + [
        remote(rows_ref.at[7 - k], halo_ref.at[crown, k], 6 + k, 6 + k + 3 * crown, place.north_id)
        for k in range(3)
    ] + [
        remote(rows_ref.at[k], halo_ref.at[1, k], 9 + k, 9 + k, place.south_id) for k in range(3)
    ]


def halo_start(place, copies, edges, rt_ref, recv_sem):
    copies[0].start()
    copies[1].start()
    for is_self, index, side, slot in ((place.nw_self, 2, 0, 5), (place.ne_self, 3, 1, 4)):

        @pl.when(is_self)
        def _(side=side, slot=slot):
            pltpu.make_async_copy(edges.at[side, 1], rt_ref.at[side, 3], recv_sem.at[slot]).start()

        @pl.when(jnp.logical_not(is_self))
        def _(index=index):
            copies[index].start()

    @pl.when(place.floor == 0)
    def _():
        copies[4].start()
        copies[5].start()


def row_start(place, copies, k):
    copies[6 + k].start()

    @pl.when(place.floor == 0)
    def _():
        copies[9 + k].start()


def wait_bytes(ref, sem):
    pltpu.make_async_copy(ref, ref, sem).wait()


def rim_wait(place, rt_ref, recv_sem):
    wait_bytes(rt_ref.at[1, pl.ds(1, 2)], recv_sem.at[0])
    wait_bytes(rt_ref.at[0, pl.ds(1, 2)], recv_sem.at[1])
    wait_bytes(rt_ref.at[1, 3], recv_sem.at[4])
    wait_bytes(rt_ref.at[0, 3], recv_sem.at[5])

    @pl.when(place.floor == 0)
    def _():
        wait_bytes(rt_ref.at[1, 0], recv_sem.at[2])
        wait_bytes(rt_ref.at[0, 0], recv_sem.at[3])


def row_wait(place, k, halo_ref, recv_sem):
    wait_bytes(halo_ref.at[1, k], recv_sem.at[9 + k])

    @pl.when(place.floor == 0)
    def _():
        wait_bytes(halo_ref.at[0, k], recv_sem.at[6 + k])


def halo_sent(place, copies):
    for index in (0, 1, 6, 7, 8):
        copies[index].wait_send()

    @pl.when(place.floor == 0)
    def _():
        for index in (4, 5, 9, 10, 11):
            copies[index].wait_send()

    for is_self, index in ((place.nw_self, 2), (place.ne_self, 3)):

        @pl.when(jnp.logical_not(is_self))
        def _(index=index):
            copies[index].wait_send()


NT = (((1,), (1,)), ((), ()))


def square(n, rule):
    source = lax.broadcasted_iota(jnp.int32, (n, n), 0)
    target = lax.broadcasted_iota(jnp.int32, (n, n), 1)
    return jnp.where(rule(source, target), 1.0, 0.0).astype(BF16)


def lay_row(i, row, ident, wide, rows_t, edge_f):
    turned = lax.dot_general(ident, row, NT, preferred_element_type=F32)
    wide[0, 3 + i, 8:136, :] = turned[:, :COLS]
    wide[1, 3 + i, 8:136, :] = turned[:, COLS:]
    rows_t[i] = turned.astype(BF16)
    edge_f[0, 8 * i : 8 * i + 8, :] = turned[:8]
    edge_f[1, 8 * i : 8 * i + 8, :] = turned[120:]


def lay_edges(edge_f, edges):
    for side in range(2):
        for b in range(2):
            edges[side, b] = edge_f[side, 32 * b : 32 * b + 32, :].astype(BF16)


def unpack_rim(place, rt_ref, wide):
    crown = place.crown == 1
    turn = square(32, lambda s, t: jnp.where(crown, 31 - s, s) == t)
    for side in range(2):
        at = slice(136 * side, 136 * side + 8)
        for b in range(4):
            if b == 3:
                block = jnp.dot(turn, rt_ref[side, b], preferred_element_type=F32)
            else:
                block = rt_ref[side, b].astype(F32)
            if b == 0:
                block = jnp.where(place.floor == 1, 0.0, block)
            for s in range(4):
                r = 4 * b + s - 1
                if 0 <= r < 14:
                    for h in range(2):
                        wide[h, r, at, :] = block[8 * s : 8 * s + 8, h * COLS : (h + 1) * COLS]


def unpack_row(place, k, halo_ref, wide):
    crown = place.crown == 1
    turn = square(COLS, lambda s, t: jnp.where(crown, COLS - 1 - s, s) == t)
    south = jnp.where(place.floor == 1, 0.0, halo_ref[0, k].astype(F32))
    north = jnp.dot(turn, halo_ref[1, k], preferred_element_type=F32)
    for h in range(2):
        wide[h, 2 - k, 8:136, :] = south[:, h * COLS : (h + 1) * COLS]
        wide[h, 11 + k, 8:136, :] = north[:, h * COLS : (h + 1) * COLS]


LOCAL_ROWS = tuple(range(3, 11))
HALO_ROWS = (0, 1, 2, 11, 12, 13)
PLACE = (6, 4, 2, 0, 1, 3, 5, 7)


def conv_block(wide, weight, out_ref, h, j, rows, add):
    at = [pl.ds(al(i * COLS + j * 8, 8), 8) for i in range(ROWS)]
    reached = [i for i in range(ROWS) if any(0 <= r - i < 7 for r in rows)]
    total = {i: out_ref[h, at[i], :] if add else None for i in reached}
    for q in range(7):
        for r in rows:
            moved = wide[h, r, pl.ds(j * 8 + (q + 5), 8), :]
            for a in range(7):
                i = r - a
                if 0 <= i < ROWS:
                    term = weight(h, a, q, r) * moved
                    total[i] = term if total[i] is None else total[i] + term
    for i in reached:
        out_ref[h, at[i], :] = total[i]


def conv_inner(wide, weight, out_ref, h):
    def body(n, _):
        conv_block(wide, weight, out_ref, h, n + 1, LOCAL_ROWS, False)
        return 0

    lax.fori_loop(0, 14, body, 0)


def conv_rim(wide, weight, out_ref):
    def body(n, _):
        conv_block(wide, weight, out_ref, n // 2, 15 * lax.rem(n, 2), LOCAL_ROWS, False)
        return 0

    lax.fori_loop(0, 4, body, 0)


def conv_halo(wide, weight, out_ref, rows):
    def body(j, _):
        for h in range(2):
            conv_block(wide, weight, out_ref, h, j, rows, True)
        return 0

    lax.fori_loop(0, 16, body, 0)


def tap_sums(wide, g_wide, out_ref):
    row_id = lax.broadcasted_iota(jnp.int32, (8, COLS), 0)

    def body(n, _):
        h, q = n // 7, lax.rem(n, 7)
        total = [None] * 7
        for j in range(16):
            grads = [g_wide[h, 3 + i, 8 + 8 * j : 16 + 8 * j, :] for i in range(ROWS)]
            for r in range(14):
                moved = wide[h, r, pl.ds(q + (8 * j + 5), 8), :]
                for a in range(7):
                    i = r - a
                    if 0 <= i < ROWS:
                        term = grads[i] * moved
                        total[a] = term if total[a] is None else total[a] + term
        tile = jnp.zeros((8, COLS), F32)
        for a in range(7):
            tile = jnp.where(row_id == a, jnp.sum(total[a], axis=0, keepdims=True), tile)
        out_ref[h, q] = tile
        return 0

    lax.fori_loop(0, 14, body, 0)
    for h in range(2):
        out_ref[h, 7] = jnp.zeros((8, COLS), F32)


def whole_kernel(
    n_lon, n_lat,
    x_ref, mask_ref, taps_ref, w_in_ref, w_out_ref, cot_ref,
    stepped_ref, state_ref, sums_ref, gk_out,
    wide, rows_t, edge_f, edges, halo, rt, send_sem, recv_sem,
    g_wide, g_rows, g_edges, g_halo, g_rt, g_send, g_recv,
    taps, taps_n, w_in_t, w_out_t, flat, flat2, conv_t, x_hat_ref, normed, gb, act, g_pre, g_norm, inv_ref,
    grads, pair_in, mine, y_in, part, xz_in, done, sums,
    tap_acc, gk, gk_pair, gk_mine, gk_y, gk_x, gk_z, gk_all,
    core_sems, y_sems, xz_sems, xzg_sems, yg_sems, last_sems, gk_core, gk_y_sems, gk_x_sems, gk_z_sems, gk_last_sems,
):
    place = Place(n_lon, n_lat)
    n_y, n_z = place.n_y, place.n_z
    rows_p = HALF // n_y // n_z
    rows_x = rows_p // 4
    near = sorted(range(n_z), key=lambda ahead: min(ahead, n_z - ahead))
    far = near[::-1]
    core, other = place.core, 1 - place.core

    barrier = pltpu.get_barrier_semaphore()
    def greet_y(step, _):
        signal(barrier, place.y_peer(step)[1])
        return 0

    def greet_xz(n, _):
        signal(barrier, place.xz_peer(n // 4, lax.rem(n, 4))[1])
        return 0

    lax.fori_loop(1, 4 * n_z, greet_xz, 0)
    lax.fori_loop(1, n_y, greet_y, 0)
    count = greet_halo(place, barrier)
    signal(barrier, place.core_id)

    ident = square(COLS, lambda s, t: s == t)
    flat[...] = x_ref[...].astype(F32).reshape(C * ROWS, COLS)
    for i in range(ROWS):
        lay_row(i, flat[pl.ds(i, C, stride=8), :].astype(BF16), ident, wide, rows_t, edge_f)
    lay_edges(edge_f, edges)
    w_in_t[...] = w_in_ref[...].astype(F32).T.astype(BF16)
    w_out_t[...] = w_out_ref[...].astype(F32).T.astype(BF16)
    pl.semaphore_wait(barrier, count + n_y + 4 * n_z - 1)
    copies = halo_copies(place, rows_t, edges, halo, rt, send_sem, recv_sem)
    halo_start(place, copies, edges, rt, recv_sem)
    row_start(place, copies, 0)

    crown = place.crown == 1
    table = taps_ref[...].astype(F32)
    for t in range(49):
        for h in range(2):
            taps[h, t] = jnp.broadcast_to(table[t : t + 1, h * COLS : (h + 1) * COLS], (8, COLS))
    for t in range(28, 49):
        for h in range(2):
            taps_n[h, t] = jnp.where(crown, taps[h, t], taps[h, 48 - t])

    def forward(h, a, q, r):
        return taps[h, 7 * a + q]

    def backward(h, a, q, r):
        return taps_n[h, 7 * a + q] if r >= 11 else taps[h, 48 - 7 * a - q]

    for h in range(2):
        conv_inner(wide, forward, conv_t, h)
        row_start(place, copies, 1 + h)
    flat[...] = cot_ref[...].astype(F32).reshape(C * ROWS, COLS)
    for r in range(ROWS):
        ocean = mask_ref[pl.ds(r, 1), :].astype(F32)
        gb[:, PLACE[r] * COLS : (PLACE[r] + 1) * COLS] = (ocean * flat[pl.ds(r, C, stride=8), :]).astype(BF16)

    rim_wait(place, rt, recv_sem)
    unpack_rim(place, rt, wide)
    conv_rim(wide, forward, conv_t)

    def cells_body(n, _):
        for k in range(3):

            @pl.when(n == k + 1)
            def _(k=k):
                row_wait(place, k, halo, recv_sem)
                unpack_row(place, k, halo, wide)
                conv_halo(wide, forward, conv_t, (2 - k, 11 + k))

        at = pl.ds(al(n * 256, 256), 256)
        pair = (3 - n, 4 + n)
        for k, r in enumerate(pair):
            row_at = pl.ds(al(r * COLS, COLS), COLS)
            value = jnp.concatenate([conv_t[0, row_at, :].T, conv_t[1, row_at, :].T], axis=0)
            centred = value - jnp.sum(value, axis=0, keepdims=True) * (1.0 / C)
            var = jnp.sum(centred * centred, axis=0, keepdims=True) * (1.0 / C)
            inv = lax.rsqrt(var + EPS)
            inv_ref[pl.ds(r, 1), :] = inv
            x_hat = centred * inv
            x_hat_ref[:, pl.ds(al(n * 256 + k * COLS, COLS), COLS)] = x_hat
            normed[:, pl.ds(al(n * 256 + k * COLS, COLS), COLS)] = x_hat.astype(BF16)
        hat = normed[:, at]
        grad = gb[:, at]
        for h in range(4):
            hs = slice(h * 256, (h + 1) * 256)
            u = jnp.dot(w_in_t[hs, :], hat, preferred_element_type=F32)
            uu = u * u
            t = jnp.tanh(TANH_SLOPE * (u + CUBIC * (uu * u)))
            gate = 0.5 * (1.0 + t)
            act[hs, at] = (u * gate).astype(BF16)
            slope = gate + (0.5 * TANH_SLOPE) * u * (1.0 - t * t) * (1.0 + (3.0 * CUBIC) * uu)
            g_act = jnp.dot(w_out_ref[hs, :], grad, preferred_element_type=F32)
            g_pre[hs, at] = (g_act * slope).astype(BF16)
        return 0

    lax.fori_loop(0, ROWS // 2, cells_body, 0)

    for h in range(4):
        hs = slice(h * 256, (h + 1) * 256)
        out = lax.dot_general(act[hs, :], gb[...], NT, preferred_element_type=F32).astype(BF16)
        grads[h * 256 : (h + 1) * 256, :] = out[:, :COLS]
        grads[1024 + h * 256 : 1024 + (h + 1) * 256, :] = out[:, COLS:]
    for h in range(4):
        hs = slice(h * 256, (h + 1) * 256)
        out = lax.dot_general(normed[...], g_pre[hs, :], NT, preferred_element_type=F32).astype(BF16)
        grads[HALF + h * 512 : HALF + h * 512 + 256, :] = out[:, :COLS]
        grads[HALF + h * 512 + 256 : HALF + (h + 1) * 512, :] = out[:, COLS:]

    def remote(src, dst, sems, index, device):
        return pltpu.make_async_remote_copy(
            src_ref=src, dst_ref=dst, send_sem=sems.at[0, index], recv_sem=sems.at[1, index],
            device_id=device, device_id_type=MESH,
        )

    def each(n, make, act):
        def run(step, _):
            act(make(step))
            return 0

        lax.fori_loop(1, n, run, 0)

    def start(copy):
        copy.start()

    def wait(copy):
        copy.wait()

    def sent(copy):
        copy.wait_send()

    first = remote(grads.at[pl.ds(al(other * HALF, HALF), HALF)], pair_in, core_sems, 0, place.core_id)
    first.start()

    def norm_body(n, _):
        at = pl.ds(al(n * 256, 256), 256)
        g_norm[:, at] = jnp.dot(w_in_ref[...], g_pre[:, at], preferred_element_type=F32)
        return 0

    lax.fori_loop(0, ROWS // 2, norm_body, 0)
    for r in range(ROWS):
        at = slice(PLACE[r] * COLS, (PLACE[r] + 1) * COLS)
        grad, x_hat = g_norm[:, at], x_hat_ref[:, at]
        mean = jnp.sum(grad, axis=0, keepdims=True) * (1.0 / C)
        proj = jnp.sum(grad * x_hat, axis=0, keepdims=True) * (1.0 / C)
        g_conv = inv_ref[pl.ds(r, 1), :] * (grad - mean - x_hat * proj)
        lay_row(r, g_conv.astype(BF16), ident, g_wide, g_rows, edge_f)
    lay_edges(edge_f, g_edges)
    g_copies = halo_copies(place, g_rows, g_edges, g_halo, g_rt, g_send, g_recv)

    first.wait()

    def add_pair(i, _):
        at = pl.ds(al(i * 256, 256), 256)
        own = grads[pl.ds(al(core * HALF + i * 256, 256), 256), :].astype(F32)
        mine[at, :] = (own + pair_in[at, :].astype(F32)).astype(BF16)
        return 0

    lax.fori_loop(0, HALF // 256, add_pair, 0)

    def y_copy(ahead, step):
        peer, device = place.y_peer(step)
        row = (peer * n_z + place.plane(ahead)) * rows_p
        return remote(mine.at[pl.ds(al(row, rows_p), rows_p)], y_in.at[ahead, step], y_sems, ahead * n_y + step, device)

    def plane_steps(ahead):
        return range(1 if ahead == 0 else 0, 4)

    for ahead in far:
        for step in range(1, n_y):
            y_copy(ahead, step).start()

    tap_sums(wide, g_wide, tap_acc)
    for h in range(2):
        gk[h] = tap_acc[h].reshape(64, COLS)
    first_k = remote(gk.at[other], gk_pair, gk_core, 0, place.core_id)
    first_k.start()

    def xz_copy(ahead, step):
        x, device = place.xz_peer(ahead, step)
        src = part.at[ahead, pl.ds(al(x * rows_x, rows_x), rows_x)]
        return remote(src, xz_in.at[ahead, step], xz_sems, ahead * 4 + step, device)

    for ahead in far:
        for step in range(1, n_y):
            y_copy(ahead, step).wait()
        own = pl.ds(al((place.yi * n_z + place.plane(ahead)) * rows_p, rows_p), rows_p)
        total = mine[own, :].astype(F32)
        for step in range(1, n_y):
            total = total + y_in[ahead, step].astype(F32)
        part[ahead] = total.astype(BF16)
        for step in plane_steps(ahead):
            xz_copy(ahead, step).start()
    halo_start(place, g_copies, g_edges, g_rt, g_recv)
    for k in range(3):
        row_start(place, g_copies, k)

    for h in range(2):
        conv_inner(g_wide, backward, conv_t, h)

    def branch_body(n, _):
        branch = jnp.dot(w_out_t[...], act[:, pl.ds(al(n * 256, 256), 256)], preferred_element_type=F32)
        for k, r in enumerate((3 - n, 4 + n)):
            ocean = mask_ref[pl.ds(r, 1), :].astype(F32)
            flat[pl.ds(r, C, stride=8), :] = ocean * branch[:, k * COLS : (k + 1) * COLS]
        return 0

    lax.fori_loop(0, ROWS // 2, branch_body, 0)

    first_k.wait()
    gk_mine[0] = (gk[core] + gk_pair[...]).astype(BF16)

    def gk_round(k, n, peer_of, slots, sems):
        def copy(step):
            return remote(gk_mine.at[k], slots.at[step], sems, step, peer_of(step))

        def finish():
            each(n, copy, wait)
            total = gk_mine[k].astype(F32)
            for step in range(1, n):
                total = total + slots[step].astype(F32)
            gk_mine[k + 1] = total.astype(BF16)

        each(n, copy, start)
        return finish

    gk_finish = gk_round(0, n_y, lambda step: place.y_peer(step)[1], gk_y, gk_y_sems)

    for ahead in near:
        for step in plane_steps(ahead):
            xz_copy(ahead, step).wait()
    total = part[0, pl.ds(al(place.xi * rows_x, rows_x), rows_x), :].astype(F32)
    for ahead in near:
        for step in plane_steps(ahead):
            total = total + xz_in[ahead, step].astype(F32)
    done[place.yi, place.zi, place.xi] = total.astype(BF16)

    def xzg_copy(ahead, step):
        _, device = place.xz_peer(ahead, step)
        own = done.at[place.yi, place.zi, place.xi]
        return remote(own, own, xzg_sems, ahead * 4 + step, device)

    for ahead in far:
        for step in plane_steps(ahead):
            xzg_copy(ahead, step).start()
    gk_finish()
    gk_finish = gk_round(1, 4, place.x_peer, gk_x, gk_x_sems)

    rim_wait(place, g_rt, g_recv)
    unpack_rim(place, g_rt, g_wide)
    conv_rim(g_wide, backward, conv_t)

    def behind(ahead):
        return lax.rem(place.zi + n_z - ahead, n_z)

    def yg_copy(ahead, step):
        _, device = place.y_peer(step)
        own = done.at[place.yi, behind(ahead)]
        return remote(own, own, yg_sems, ahead * n_y + step, device)

    def across(ahead, step, y):
        whole = done.at[y, behind(ahead)], sums.at[y, behind(ahead)]
        return remote(*whole, last_sems, ahead * n_y + step, place.core_id)

    for ahead in near:
        for step in plane_steps(ahead):
            x = lax.rem(place.xi + 4 - step, 4)
            wait_bytes(done.at[place.yi, behind(ahead), x], xzg_sems.at[1, ahead * 4 + step])
        for step in range(1, n_y):
            yg_copy(ahead, step).start()
        across(ahead, 0, place.yi).start()

    gk_finish()
    gk_finish = gk_round(2, n_z, place.z_peer, gk_z, gk_z_sems)
    for k in range(3):
        row_wait(place, k, g_halo, g_recv)
        unpack_row(place, k, g_halo, g_wide)
    conv_halo(g_wide, backward, conv_t, HALO_ROWS)
    for r in range(ROWS):
        at = slice(r * COLS, (r + 1) * COLS)
        flat2[pl.ds(r, C, stride=8), :] = jnp.concatenate([conv_t[0, at, :].T, conv_t[1, at, :].T], axis=0)

    def out_body(group, _):
        at = pl.ds(group * 32, 32)
        rows_at = pl.ds(al(group * 256, 256), 256)
        moved = flat[rows_at, :].reshape(32, ROWS, COLS)
        stepped_ref[at] = (x_ref[at].astype(F32) + moved).astype(BF16)
        moved = flat2[rows_at, :].reshape(32, ROWS, COLS)
        state_ref[at] = (cot_ref[at].astype(F32) + moved).astype(BF16)
        return 0

    lax.fori_loop(0, C // 32, out_body, 0)

    for ahead in near:
        for step in range(1, n_y):
            y = lax.rem(place.yi + n_y - step, n_y)
            wait_bytes(done.at[y, behind(ahead)], yg_sems.at[1, ahead * n_y + step])
            across(ahead, step, y).start()

    gk_finish()
    gk_all[core] = gk_mine[3]
    last_k = remote(gk_all.at[core], gk_all.at[core], gk_last_sems, 0, place.core_id)
    last_k.start()

    wait_bytes(gk_all.at[core], gk_last_sems.at[0, 0])
    wait_bytes(gk_all.at[other], gk_last_sems.at[1, 0])
    gk_out[...] = gk_all[...]
    sums_ref[core] = done[...]

    for ahead in near:
        for step in range(n_y):
            y = lax.rem(place.yi + n_y - step, n_y)
            wait_bytes(done.at[y, behind(ahead)], last_sems.at[0, ahead * n_y + step])
            wait_bytes(sums.at[y, behind(ahead)], last_sems.at[1, ahead * n_y + step])
    sums_ref[other] = sums[...]

    for ahead in near:
        for step in plane_steps(ahead):
            xzg_copy(ahead, step).wait_send()
        for step in range(1, n_y):
            yg_copy(ahead, step).wait_send()
    halo_sent(place, copies)
    halo_sent(place, g_copies)


def finish_kernel(stepped_in, state_in, sums_ref, gk_ref, stepped_ref, state_ref, gk_out, gin_ref, gout_ref):
    stepped_ref[...] = stepped_in[...]
    state_ref[...] = state_in[...]
    for b in range(2):
        gout_ref[:, b * COLS : (b + 1) * COLS] = sums_ref[0, b * 1024 : (b + 1) * 1024, :].astype(F32)
    for b in range(8):
        gin_ref[:, b * COLS : (b + 1) * COLS] = sums_ref[1, b * 256 : (b + 1) * 256, :].astype(F32)
    for h in range(2):
        total = gk_ref[h].astype(F32)
        for t in range(49):
            a, q = t // 7, t % 7
            gk_out[t : t + 1, h * COLS : (h + 1) * COLS] = total[8 * q + a : 8 * q + a + 1]


def halo_scratch():
    return [
        pltpu.VMEM((2, 2, 32, C), BF16),
        pltpu.VMEM((2, 3, COLS, C), BF16),
        pltpu.VMEM((2, 4, 32, C), BF16),
        pltpu.SemaphoreType.DMA((12,)),
        pltpu.SemaphoreType.DMA((12,)),
    ]


def per_device(n_lon, n_lat, ocean_state, land_mask, kernel, w_in, w_out, cotangent):
    n_y, n_z = n_lat // 2, n_lon // 4
    rows_p = HALF // n_y // n_z
    wide = pltpu.VMEM((2, 14, 144, COLS), F32)
    turned_rows = pltpu.VMEM((ROWS, COLS, C), BF16)
    table = pltpu.VMEM((2, 49, 8, COLS), F32)
    sems = lambda n: pltpu.SemaphoreType.DMA((2, n))
    summed = pltpu.VMEM((n_y, n_z, 4, rows_p // 4, COLS), BF16)
    flat = pltpu.VMEM((C * ROWS, COLS), F32)
    field = jax.ShapeDtypeStruct((C, ROWS, COLS), BF16)
    stepped, state, sums, gk = pl.pallas_call(
        functools.partial(whole_kernel, n_lon, n_lat),
        out_shape=(
            field,
            field,
            jax.ShapeDtypeStruct((2, n_y, n_z, 4, rows_p // 4, COLS), BF16),
            jax.ShapeDtypeStruct((2, 64, COLS), BF16),
        ),
        in_specs=[VSPEC] * 6,
        out_specs=(VSPEC,) * 4,
        scratch_shapes=[wide, turned_rows, pltpu.VMEM((2, 64, C), F32)]
        + halo_scratch()
        + [wide, turned_rows]
        + halo_scratch()
        + [
            table,
            table,
            pltpu.VMEM((HID, C), BF16),
            pltpu.VMEM((C, HID), BF16),
            flat,
            flat,
            pltpu.VMEM((2, CELLS, COLS), F32),
            pltpu.VMEM((C, CELLS), F32),
            pltpu.VMEM((C, CELLS), BF16),
            pltpu.VMEM((C, CELLS), BF16),
            pltpu.VMEM((HID, CELLS), BF16),
            pltpu.VMEM((HID, CELLS), BF16),
            pltpu.VMEM((C, CELLS), F32),
            pltpu.VMEM((ROWS, COLS), F32),
            pltpu.VMEM((2 * HALF, COLS), BF16),
            pltpu.VMEM((HALF, COLS), BF16),
            pltpu.VMEM((HALF, COLS), BF16),
            pltpu.VMEM((n_z, n_y, rows_p, COLS), BF16),
            pltpu.VMEM((n_z, rows_p, COLS), BF16),
            pltpu.VMEM((n_z, 4, rows_p // 4, COLS), BF16),
            summed,
            summed,
            pltpu.VMEM((2, 8, 8, COLS), F32),
            pltpu.VMEM((2, 64, COLS), F32),
            pltpu.VMEM((64, COLS), F32),
            pltpu.VMEM((4, 64, COLS), BF16),
            pltpu.VMEM((n_y, 64, COLS), BF16),
            pltpu.VMEM((4, 64, COLS), BF16),
            pltpu.VMEM((n_z, 64, COLS), BF16),
            pltpu.VMEM((2, 64, COLS), BF16),
            sems(1),
            sems(n_z * n_y),
            sems(n_z * 4),
            sems(n_z * 4),
            sems(n_z * n_y),
            sems(n_z * n_y),
            sems(1),
            sems(n_y),
            sems(4),
            sems(n_z),
            sems(1),
        ],
        compiler_params=pltpu.CompilerParams(
            collective_id=0, has_side_effects=True, vmem_limit_bytes=VMEM_LIMIT
        ),
        name="convnext",
    )(ocean_state, land_mask, kernel, w_in, w_out, cotangent)
    return pl.pallas_call(
        finish_kernel,
        out_shape=(
            field,
            field,
            jax.ShapeDtypeStruct((49, C), F32),
            jax.ShapeDtypeStruct((C, HID), F32),
            jax.ShapeDtypeStruct((HID, C), F32),
        ),
        in_specs=[VSPEC] * 4,
        out_specs=(VSPEC,) * 5,
        compiler_params=pltpu.CompilerParams(vmem_limit_bytes=VMEM_LIMIT),
        name="finish",
    )(stepped, state, sums.reshape(2, HALF, COLS), gk)


def solution(mesh):
    return jax.shard_map(
        functools.partial(per_device, mesh.shape["lon"], mesh.shape["lat"]),
        mesh=mesh,
        in_specs=(P(None, "lat", "lon"), P("lat", "lon"), P(), P(), P(), P(None, "lat", "lon")),
        out_specs=(P(None, "lat", "lon"), P(None, "lat", "lon"), P(), P(), P()),
        check_vma=False,
    )
```

```python
import functools

import jax
import jax.numpy as jnp
from jax import lax
from jax.experimental import pallas as pl
from jax.experimental.pallas import tpu as pltpu
from jax.sharding import PartitionSpec as P

F32 = jnp.float32
BF16 = jnp.bfloat16
MESH = pl.DeviceIdType.MESH
TANH_SLOPE = 0.7978845608028654
CUBIC = 0.044715
EPS = 1e-06
C = 256
HID = 1024
ROWS = 8
COLS = 128
CELLS = ROWS * COLS
HALF = 2048
VMEM_LIMIT = 56 * 1024 * 1024
VSPEC = pl.BlockSpec(memory_space=pltpu.VMEM)


def al(value, multiple):
    return pl.multiple_of(value, multiple)


def pick(flag, yes, no):
    return flag * yes + (1 - flag) * no


class Place:
    def __init__(self, n_lon, n_lat):
        self.n_lon, self.n_lat = n_lon, n_lat
        self.lon = lax.axis_index("lon")
        self.lat = lax.axis_index("lat")
        self.crown = (self.lat == n_lat - 1).astype(jnp.int32)
        self.floor = (self.lat == 0).astype(jnp.int32)
        east = lax.rem(self.lon + 1, n_lon)
        west = lax.rem(self.lon + n_lon - 1, n_lon)
        north = pick(self.crown, self.lat, self.lat + 1)
        south = lax.rem(self.lat + n_lat - 1, n_lat)
        mirror = n_lon - 1 - self.lon
        self.west_id = {"lon": west, "lat": self.lat}
        self.east_id = {"lon": east, "lat": self.lat}
        self.north_id = {"lon": pick(self.crown, mirror, self.lon), "lat": north}
        self.south_id = {"lon": self.lon, "lat": south}
        nw = pick(self.crown, lax.rem(n_lon - self.lon, n_lon), west)
        ne = pick(self.crown, lax.rem(2 * n_lon - 2 - self.lon, n_lon), east)
        self.nw_self = (self.crown == 1) & (nw == self.lon)
        self.ne_self = (self.crown == 1) & (ne == self.lon)
        self.nw_id = {"lon": nw, "lat": north}
        self.ne_id = {"lon": ne, "lat": north}
        self.sw_id = {"lon": west, "lat": south}
        self.se_id = {"lon": east, "lat": south}
        self.core = lax.rem(self.lon, 2)
        self.zi = self.lon // 4
        self.yi = self.lat // 2
        self.xi = lax.rem(self.lat, 2) * 2 + lax.rem(self.lon // 2, 2)
        self.n_y, self.n_z = n_lat // 2, n_lon // 4
        self.core_id = {"lon": self.lon + 1 - 2 * self.core, "lat": self.lat}

    def device(self, x, y, z):
        return {"lon": z * 4 + lax.rem(x, 2) * 2 + self.core, "lat": y * 2 + x // 2}

    def x_peer(self, step):
        return self.device(lax.rem(self.xi + step, 4), self.yi, self.zi)

    def z_peer(self, step):
        return self.device(self.xi, self.yi, lax.rem(self.zi + step, self.n_z))

    def y_peer(self, step):
        peer = lax.rem(self.yi + step, self.n_y)
        return peer, self.device(self.xi, peer, self.zi)

    def plane(self, ahead):
        return lax.rem(self.zi + ahead, self.n_z)

    def xz_peer(self, ahead, step):
        x = lax.rem(self.xi + step, 4)
        return x, self.device(x, self.yi, self.plane(ahead))


def signal(barrier, device):
    pl.semaphore_signal(barrier, inc=1, device_id=device, device_id_type=MESH)


def greet_halo(place, barrier):
    for device in (place.west_id, place.east_id, place.north_id):
        signal(barrier, device)

    @pl.when(jnp.logical_not(place.nw_self))
    def _():
        signal(barrier, place.nw_id)

    @pl.when(jnp.logical_not(place.ne_self))
    def _():
        signal(barrier, place.ne_id)

    @pl.when(place.floor == 0)
    def _():
        for device in (place.south_id, place.sw_id, place.se_id):
            signal(barrier, device)

    return (
        5
        - place.nw_self.astype(jnp.int32)
        - place.ne_self.astype(jnp.int32)
        + 3 * (1 - place.floor)
    )


def halo_copies(place, rows_ref, edges, halo_ref, rt_ref, send_sem, recv_sem):
    crown = place.crown

    def remote(src, dst, index, slot, device):
        return pltpu.make_async_remote_copy(
            src_ref=src,
            dst_ref=dst,
            send_sem=send_sem.at[index],
            recv_sem=recv_sem.at[slot],
            device_id=device,
            device_id_type=MESH,
        )

    return [
        remote(edges.at[0], rt_ref.at[1, pl.ds(1, 2)], 0, 0, place.west_id),
        remote(edges.at[1], rt_ref.at[0, pl.ds(1, 2)], 1, 1, place.east_id),
        remote(edges.at[0, 1], rt_ref.at[1 - crown, 3 * crown], 2, 2 + 3 * crown, place.nw_id),
        remote(edges.at[1, 1], rt_ref.at[crown, 3 * crown], 3, 3 + crown, place.ne_id),
        remote(edges.at[0, 0], rt_ref.at[1, 3], 4, 4, place.sw_id),
        remote(edges.at[1, 0], rt_ref.at[0, 3], 5, 5, place.se_id),
    ] + [
        remote(rows_ref.at[7 - k], halo_ref.at[crown, k], 6 + k, 6 + k + 3 * crown, place.north_id)
        for k in range(3)
    ] + [
        remote(rows_ref.at[k], halo_ref.at[1, k], 9 + k, 9 + k, place.south_id) for k in range(3)
    ]


def halo_start(place, copies, edges, rt_ref, recv_sem):
    copies[0].start()
    copies[1].start()
    for is_self, index, side, slot in ((place.nw_self, 2, 0, 5), (place.ne_self, 3, 1, 4)):

        @pl.when(is_self)
        def _(side=side, slot=slot):
            pltpu.make_async_copy(edges.at[side, 1], rt_ref.at[side, 3], recv_sem.at[slot]).start()

        @pl.when(jnp.logical_not(is_self))
        def _(index=index):
            copies[index].start()

    @pl.when(place.floor == 0)
    def _():
        copies[4].start()
        copies[5].start()


def row_start(place, copies, k):
    copies[6 + k].start()

    @pl.when(place.floor == 0)
    def _():
        copies[9 + k].start()


def wait_bytes(ref, sem):
    pltpu.make_async_copy(ref, ref, sem).wait()


def rim_wait(place, rt_ref, recv_sem):
    wait_bytes(rt_ref.at[1, pl.ds(1, 2)], recv_sem.at[0])
    wait_bytes(rt_ref.at[0, pl.ds(1, 2)], recv_sem.at[1])
    wait_bytes(rt_ref.at[1, 3], recv_sem.at[4])
    wait_bytes(rt_ref.at[0, 3], recv_sem.at[5])

    @pl.when(place.floor == 0)
    def _():
        wait_bytes(rt_ref.at[1, 0], recv_sem.at[2])
        wait_bytes(rt_ref.at[0, 0], recv_sem.at[3])


def row_wait(place, k, halo_ref, recv_sem):
    wait_bytes(halo_ref.at[1, k], recv_sem.at[9 + k])

    @pl.when(place.floor == 0)
    def _():
        wait_bytes(halo_ref.at[0, k], recv_sem.at[6 + k])


def halo_sent(place, copies):
    for index in (0, 1, 6, 7, 8):
        copies[index].wait_send()

    @pl.when(place.floor == 0)
    def _():
        for index in (4, 5, 9, 10, 11):
            copies[index].wait_send()

    for is_self, index in ((place.nw_self, 2), (place.ne_self, 3)):

        @pl.when(jnp.logical_not(is_self))
        def _(index=index):
            copies[index].wait_send()


NT = (((1,), (1,)), ((), ()))


def square(n, rule):
    source = lax.broadcasted_iota(jnp.int32, (n, n), 0)
    target = lax.broadcasted_iota(jnp.int32, (n, n), 1)
    return jnp.where(rule(source, target), 1.0, 0.0).astype(BF16)


def lay_row(i, row, ident, wide, rows_t, edge_f):
    turned = lax.dot_general(ident, row, NT, preferred_element_type=F32)
    wide[0, 3 + i, 8:136, :] = turned[:, :COLS]
    wide[1, 3 + i, 8:136, :] = turned[:, COLS:]
    rows_t[i] = turned.astype(BF16)
    edge_f[0, 8 * i : 8 * i + 8, :] = turned[:8]
    edge_f[1, 8 * i : 8 * i + 8, :] = turned[120:]


def lay_edges(edge_f, edges):
    for side in range(2):
        for b in range(2):
            edges[side, b] = edge_f[side, 32 * b : 32 * b + 32, :].astype(BF16)


def unpack_rim(place, rt_ref, wide):
    crown = place.crown == 1
    turn = square(32, lambda s, t: jnp.where(crown, 31 - s, s) == t)
    for side in range(2):
        at = slice(136 * side, 136 * side + 8)
        for b in range(4):
            if b == 3:
                block = jnp.dot(turn, rt_ref[side, b], preferred_element_type=F32)
            else:
                block = rt_ref[side, b].astype(F32)
            if b == 0:
                block = jnp.where(place.floor == 1, 0.0, block)
            for s in range(4):
                r = 4 * b + s - 1
                if 0 <= r < 14:
                    for h in range(2):
                        wide[h, r, at, :] = block[8 * s : 8 * s + 8, h * COLS : (h + 1) * COLS]


def unpack_row(place, k, halo_ref, wide):
    crown = place.crown == 1
    turn = square(COLS, lambda s, t: jnp.where(crown, COLS - 1 - s, s) == t)
    south = jnp.where(place.floor == 1, 0.0, halo_ref[0, k].astype(F32))
    north = jnp.dot(turn, halo_ref[1, k], preferred_element_type=F32)
    for h in range(2):
        wide[h, 2 - k, 8:136, :] = south[:, h * COLS : (h + 1) * COLS]
        wide[h, 11 + k, 8:136, :] = north[:, h * COLS : (h + 1) * COLS]


LOCAL_ROWS = tuple(range(3, 11))
PLACE = (6, 4, 2, 0, 1, 3, 5, 7)


def conv_block(wide, weight, out_ref, h, j, rows, add):
    at = [pl.ds(al(i * COLS + j * 8, 8), 8) for i in range(ROWS)]
    reached = [i for i in range(ROWS) if any(0 <= r - i < 7 for r in rows)]
    total = {i: out_ref[h, at[i], :] if add else None for i in reached}
    for q in range(7):
        for r in rows:
            moved = wide[h, r, pl.ds(j * 8 + (q + 5), 8), :]
            for a in range(7):
                i = r - a
                if 0 <= i < ROWS:
                    term = weight(h, a, q, r) * moved
                    total[i] = term if total[i] is None else total[i] + term
    for i in reached:
        out_ref[h, at[i], :] = total[i]


def conv_inner(wide, weight, out_ref, h):
    def body(n, _):
        conv_block(wide, weight, out_ref, h, n + 1, LOCAL_ROWS, False)
        return 0

    lax.fori_loop(0, 14, body, 0)


def conv_rim(wide, weight, out_ref):
    def body(n, _):
        conv_block(wide, weight, out_ref, n // 2, 15 * lax.rem(n, 2), LOCAL_ROWS, False)
        return 0

    lax.fori_loop(0, 4, body, 0)


def conv_halo(wide, weight, out_ref, rows):
    def body(j, _):
        for h in range(2):
            conv_block(wide, weight, out_ref, h, j, rows, True)
        return 0

    lax.fori_loop(0, 16, body, 0)


def tap_sums(wide, g_wide, out_ref):
    row_id = lax.broadcasted_iota(jnp.int32, (8, COLS), 0)

    def body(n, _):
        h, q = n // 7, lax.rem(n, 7)
        total = [None] * 7
        for j in range(16):
            grads = [g_wide[h, 3 + i, 8 + 8 * j : 16 + 8 * j, :] for i in range(ROWS)]
            for r in range(14):
                moved = wide[h, r, pl.ds(q + (8 * j + 5), 8), :]
                for a in range(7):
                    i = r - a
                    if 0 <= i < ROWS:
                        term = grads[i] * moved
                        total[a] = term if total[a] is None else total[a] + term
        tile = jnp.zeros((8, COLS), F32)
        for a in range(7):
            tile = jnp.where(row_id == a, jnp.sum(total[a], axis=0, keepdims=True), tile)
        out_ref[h, q] = tile
        return 0

    lax.fori_loop(0, 14, body, 0)
    for h in range(2):
        out_ref[h, 7] = jnp.zeros((8, COLS), F32)


def whole_kernel(
    n_lon, n_lat,
    x_ref, mask_ref, taps_ref, w_in_ref, w_out_ref, cot_ref,
    stepped_ref, state_ref, sums_ref, gk_out,
    wide, rows_t, edge_f, edges, halo, rt, send_sem, recv_sem,
    g_wide, g_rows, g_edges, g_halo, g_rt, g_send, g_recv,
    taps, taps_n, w_in_t, w_out_t, flat, flat2, conv_t, x_hat_ref, normed, gb, act, g_pre, g_norm, inv_ref,
    grads, pair_in, mine, y_in, part, xz_in, done, sums,
    tap_acc, gk, gk_pair, gk_mine, gk_y, gk_x, gk_z, gk_all,
    core_sems, y_sems, xz_sems, xzg_sems, yg_sems, last_sems, gk_core, gk_y_sems, gk_x_sems, gk_z_sems, gk_last_sems,
):
    place = Place(n_lon, n_lat)
    n_y, n_z = place.n_y, place.n_z
    rows_p = HALF // n_y // n_z
    rows_x = rows_p // 4
    near = sorted(range(n_z), key=lambda ahead: min(ahead, n_z - ahead))
    far = near[::-1]
    core, other = place.core, 1 - place.core

    barrier = pltpu.get_barrier_semaphore()
    def greet_y(step, _):
        signal(barrier, place.y_peer(step)[1])
        return 0

    def greet_xz(n, _):
        signal(barrier, place.xz_peer(n // 4, lax.rem(n, 4))[1])
        return 0

    lax.fori_loop(1, 4 * n_z, greet_xz, 0)
    lax.fori_loop(1, n_y, greet_y, 0)
    count = greet_halo(place, barrier)
    signal(barrier, place.core_id)

    ident = square(COLS, lambda s, t: s == t)
    flat[...] = x_ref[...].astype(F32).reshape(C * ROWS, COLS)
    for i in range(ROWS):
        lay_row(i, flat[pl.ds(i, C, stride=8), :].astype(BF16), ident, wide, rows_t, edge_f)
    lay_edges(edge_f, edges)
    w_in_t[...] = w_in_ref[...].astype(F32).T.astype(BF16)
    w_out_t[...] = w_out_ref[...].astype(F32).T.astype(BF16)
    pl.semaphore_wait(barrier, count + n_y + 4 * n_z - 1)
    copies = halo_copies(place, rows_t, edges, halo, rt, send_sem, recv_sem)
    halo_start(place, copies, edges, rt, recv_sem)
    row_start(place, copies, 0)

    crown = place.crown == 1
    table = taps_ref[...].astype(F32)
    for t in range(49):
        for h in range(2):
            taps[h, t] = jnp.broadcast_to(table[t : t + 1, h * COLS : (h + 1) * COLS], (8, COLS))
    for t in range(28, 49):
        for h in range(2):
            taps_n[h, t] = jnp.where(crown, taps[h, t], taps[h, 48 - t])

    def forward(h, a, q, r):
        return taps[h, 7 * a + q]

    def backward(h, a, q, r):
        return taps_n[h, 7 * a + q] if r >= 11 else taps[h, 48 - 7 * a - q]

    for h in range(2):
        conv_inner(wide, forward, conv_t, h)
        row_start(place, copies, 1 + h)
    flat[...] = cot_ref[...].astype(F32).reshape(C * ROWS, COLS)
    for r in range(ROWS):
        ocean = mask_ref[pl.ds(r, 1), :].astype(F32)
        gb[:, PLACE[r] * COLS : (PLACE[r] + 1) * COLS] = (ocean * flat[pl.ds(r, C, stride=8), :]).astype(BF16)

    rim_wait(place, rt, recv_sem)
    unpack_rim(place, rt, wide)
    conv_rim(wide, forward, conv_t)

    def cells_body(n, _):
        for k in range(3):

            @pl.when(n == k + 1)
            def _(k=k):
                row_wait(place, k, halo, recv_sem)
                unpack_row(place, k, halo, wide)
                conv_halo(wide, forward, conv_t, (2 - k, 11 + k))

        at = pl.ds(al(n * 256, 256), 256)
        pair = (3 - n, 4 + n)
        for k, r in enumerate(pair):
            row_at = pl.ds(al(r * COLS, COLS), COLS)
            value = jnp.concatenate([conv_t[0, row_at, :].T, conv_t[1, row_at, :].T], axis=0)
            centred = value - jnp.sum(value, axis=0, keepdims=True) * (1.0 / C)
            var = jnp.sum(centred * centred, axis=0, keepdims=True) * (1.0 / C)
            inv = lax.rsqrt(var + EPS)
            inv_ref[pl.ds(r, 1), :] = inv
            x_hat = centred * inv
            x_hat_ref[:, pl.ds(al(n * 256 + k * COLS, COLS), COLS)] = x_hat
            normed[:, pl.ds(al(n * 256 + k * COLS, COLS), COLS)] = x_hat.astype(BF16)
        hat = normed[:, at]
        grad = gb[:, at]
        for h in range(4):
            hs = slice(h * 256, (h + 1) * 256)
            u = jnp.dot(w_in_t[hs, :], hat, preferred_element_type=F32)
            uu = u * u
            t = jnp.tanh(TANH_SLOPE * (u + CUBIC * (uu * u)))
            gate = 0.5 * (1.0 + t)
            act[hs, at] = (u * gate).astype(BF16)
            slope = gate + (0.5 * TANH_SLOPE) * u * (1.0 - t * t) * (1.0 + (3.0 * CUBIC) * uu)
            g_act = jnp.dot(w_out_ref[hs, :], grad, preferred_element_type=F32)
            g_pre[hs, at] = (g_act * slope).astype(BF16)
        return 0

    lax.fori_loop(0, ROWS // 2, cells_body, 0)

    for h in range(4):
        hs = slice(h * 256, (h + 1) * 256)
        out = lax.dot_general(act[hs, :], gb[...], NT, preferred_element_type=F32).astype(BF16)
        grads[h * 256 : (h + 1) * 256, :] = out[:, :COLS]
        grads[1024 + h * 256 : 1024 + (h + 1) * 256, :] = out[:, COLS:]
    for h in range(4):
        hs = slice(h * 256, (h + 1) * 256)
        out = lax.dot_general(normed[...], g_pre[hs, :], NT, preferred_element_type=F32).astype(BF16)
        grads[HALF + h * 512 : HALF + h * 512 + 256, :] = out[:, :COLS]
        grads[HALF + h * 512 + 256 : HALF + (h + 1) * 512, :] = out[:, COLS:]

    def remote(src, dst, sems, index, device):
        return pltpu.make_async_remote_copy(
            src_ref=src, dst_ref=dst, send_sem=sems.at[0, index], recv_sem=sems.at[1, index],
            device_id=device, device_id_type=MESH,
        )

    def each(n, make, act):
        def run(step, _):
            act(make(step))
            return 0

        lax.fori_loop(1, n, run, 0)

    def start(copy):
        copy.start()

    def wait(copy):
        copy.wait()

    def sent(copy):
        copy.wait_send()

    first = remote(grads.at[pl.ds(al(other * HALF, HALF), HALF)], pair_in, core_sems, 0, place.core_id)
    first.start()

    def norm_body(n, _):
        at = pl.ds(al(n * 256, 256), 256)
        g_norm[:, at] = jnp.dot(w_in_ref[...], g_pre[:, at], preferred_element_type=F32)
        return 0

    lax.fori_loop(0, ROWS // 2, norm_body, 0)
    for r in range(ROWS):
        at = slice(PLACE[r] * COLS, (PLACE[r] + 1) * COLS)
        grad, x_hat = g_norm[:, at], x_hat_ref[:, at]
        mean = jnp.sum(grad, axis=0, keepdims=True) * (1.0 / C)
        proj = jnp.sum(grad * x_hat, axis=0, keepdims=True) * (1.0 / C)
        g_conv = inv_ref[pl.ds(r, 1), :] * (grad - mean - x_hat * proj)
        lay_row(r, g_conv.astype(BF16), ident, g_wide, g_rows, edge_f)
    lay_edges(edge_f, g_edges)
    g_copies = halo_copies(place, g_rows, g_edges, g_halo, g_rt, g_send, g_recv)

    first.wait()

    def add_pair(i, _):
        at = pl.ds(al(i * 256, 256), 256)
        own = grads[pl.ds(al(core * HALF + i * 256, 256), 256), :].astype(F32)
        mine[at, :] = (own + pair_in[at, :].astype(F32)).astype(BF16)
        return 0

    lax.fori_loop(0, HALF // 256, add_pair, 0)

    def y_copy(ahead, step):
        peer, device = place.y_peer(step)
        row = (peer * n_z + place.plane(ahead)) * rows_p
        return remote(mine.at[pl.ds(al(row, rows_p), rows_p)], y_in.at[ahead, step], y_sems, ahead * n_y + step, device)

    def plane_steps(ahead):
        return range(1 if ahead == 0 else 0, 4)

    for ahead in far:
        for step in range(1, n_y):
            y_copy(ahead, step).start()

    tap_sums(wide, g_wide, tap_acc)
    for h in range(2):
        gk[h] = tap_acc[h].reshape(64, COLS)
    first_k = remote(gk.at[other], gk_pair, gk_core, 0, place.core_id)
    first_k.start()

    halo_start(place, g_copies, g_edges, g_rt, g_recv)
    for k in range(3):
        row_start(place, g_copies, k)

    def xz_copy(ahead, step):
        x, device = place.xz_peer(ahead, step)
        src = part.at[ahead, pl.ds(al(x * rows_x, rows_x), rows_x)]
        return remote(src, xz_in.at[ahead, step], xz_sems, ahead * 4 + step, device)

    for ahead in far:
        for step in range(1, n_y):
            y_copy(ahead, step).wait()
        own = pl.ds(al((place.yi * n_z + place.plane(ahead)) * rows_p, rows_p), rows_p)
        total = mine[own, :].astype(F32)
        for step in range(1, n_y):
            total = total + y_in[ahead, step].astype(F32)
        part[ahead] = total.astype(BF16)
        for step in plane_steps(ahead):
            xz_copy(ahead, step).start()

    conv_inner(g_wide, backward, conv_t, 0)

    first_k.wait()
    gk_mine[0] = (gk[core] + gk_pair[...]).astype(BF16)

    def gk_round(k, n, peer_of, slots, sems):
        def copy(step):
            return remote(gk_mine.at[k], slots.at[step], sems, step, peer_of(step))

        def finish():
            each(n, copy, wait)
            total = gk_mine[k].astype(F32)
            for step in range(1, n):
                total = total + slots[step].astype(F32)
            gk_mine[k + 1] = total.astype(BF16)

        each(n, copy, start)
        return finish

    gk_finish = gk_round(0, n_y, lambda step: place.y_peer(step)[1], gk_y, gk_y_sems)

    for ahead in near:
        for step in plane_steps(ahead):
            xz_copy(ahead, step).wait()
    total = part[0, pl.ds(al(place.xi * rows_x, rows_x), rows_x), :].astype(F32)
    for ahead in near:
        for step in plane_steps(ahead):
            total = total + xz_in[ahead, step].astype(F32)
    done[place.yi, place.zi, place.xi] = total.astype(BF16)

    def xzg_copy(ahead, step):
        _, device = place.xz_peer(ahead, step)
        own = done.at[place.yi, place.zi, place.xi]
        return remote(own, own, xzg_sems, ahead * 4 + step, device)

    for ahead in far:
        for step in plane_steps(ahead):
            xzg_copy(ahead, step).start()
    gk_finish()
    gk_finish = gk_round(1, 4, place.x_peer, gk_x, gk_x_sems)

    conv_inner(g_wide, backward, conv_t, 1)

    def branch_body(n, _):
        branch = jnp.dot(w_out_t[...], act[:, pl.ds(al(n * 256, 256), 256)], preferred_element_type=F32)
        for k, r in enumerate((3 - n, 4 + n)):
            ocean = mask_ref[pl.ds(r, 1), :].astype(F32)
            flat[pl.ds(r, C, stride=8), :] = ocean * branch[:, k * COLS : (k + 1) * COLS]
        return 0

    lax.fori_loop(0, ROWS // 2, branch_body, 0)

    def stepped_body(group, _):
        at = pl.ds(group * 32, 32)
        moved = flat[pl.ds(al(group * 256, 256), 256), :].reshape(32, ROWS, COLS)
        stepped_ref[at] = (x_ref[at].astype(F32) + moved).astype(BF16)
        return 0

    lax.fori_loop(0, C // 32, stepped_body, 0)

    rim_wait(place, g_rt, g_recv)
    unpack_rim(place, g_rt, g_wide)
    conv_rim(g_wide, backward, conv_t)

    def halo_row(k):
        row_wait(place, k, g_halo, g_recv)
        unpack_row(place, k, g_halo, g_wide)
        conv_halo(g_wide, backward, conv_t, (2 - k, 11 + k))

    halo_row(0)
    halo_row(1)

    def behind(ahead):
        return lax.rem(place.zi + n_z - ahead, n_z)

    def yg_copy(ahead, step):
        _, device = place.y_peer(step)
        own = done.at[place.yi, behind(ahead)]
        return remote(own, own, yg_sems, ahead * n_y + step, device)

    def across(ahead, step, y):
        whole = done.at[y, behind(ahead)], sums.at[y, behind(ahead)]
        return remote(*whole, last_sems, ahead * n_y + step, place.core_id)

    for ahead in near:
        for step in plane_steps(ahead):
            x = lax.rem(place.xi + 4 - step, 4)
            wait_bytes(done.at[place.yi, behind(ahead), x], xzg_sems.at[1, ahead * 4 + step])
        for step in range(1, n_y):
            yg_copy(ahead, step).start()
        across(ahead, 0, place.yi).start()

    gk_finish()
    gk_finish = gk_round(2, n_z, place.z_peer, gk_z, gk_z_sems)
    halo_row(2)
    for r in range(ROWS):
        at = slice(r * COLS, (r + 1) * COLS)
        flat2[pl.ds(r, C, stride=8), :] = jnp.concatenate([conv_t[0, at, :].T, conv_t[1, at, :].T], axis=0)

    def state_body(group, _):
        at = pl.ds(group * 32, 32)
        rows_at = pl.ds(al(group * 256, 256), 256)
        moved = flat2[rows_at, :].reshape(32, ROWS, COLS)
        state_ref[at] = (cot_ref[at].astype(F32) + moved).astype(BF16)
        return 0

    lax.fori_loop(0, C // 32, state_body, 0)

    for ahead in near:
        for step in range(1, n_y):
            y = lax.rem(place.yi + n_y - step, n_y)
            wait_bytes(done.at[y, behind(ahead)], yg_sems.at[1, ahead * n_y + step])
            across(ahead, step, y).start()

    gk_finish()
    gk_all[core] = gk_mine[3]
    last_k = remote(gk_all.at[core], gk_all.at[core], gk_last_sems, 0, place.core_id)
    last_k.start()

    wait_bytes(gk_all.at[core], gk_last_sems.at[0, 0])
    wait_bytes(gk_all.at[other], gk_last_sems.at[1, 0])
    gk_out[...] = gk_all[...]
    sums_ref[core] = done[...]

    for ahead in near:
        for step in range(n_y):
            y = lax.rem(place.yi + n_y - step, n_y)
            wait_bytes(done.at[y, behind(ahead)], last_sems.at[0, ahead * n_y + step])
            wait_bytes(sums.at[y, behind(ahead)], last_sems.at[1, ahead * n_y + step])
    sums_ref[other] = sums[...]

    for ahead in near:
        for step in plane_steps(ahead):
            xzg_copy(ahead, step).wait_send()
        for step in range(1, n_y):
            yg_copy(ahead, step).wait_send()
    halo_sent(place, copies)
    halo_sent(place, g_copies)


def finish_kernel(stepped_in, state_in, sums_ref, gk_ref, stepped_ref, state_ref, gk_out, gin_ref, gout_ref):
    stepped_ref[...] = stepped_in[...]
    state_ref[...] = state_in[...]
    for b in range(2):
        gout_ref[:, b * COLS : (b + 1) * COLS] = sums_ref[0, b * 1024 : (b + 1) * 1024, :].astype(F32)
    for b in range(8):
        gin_ref[:, b * COLS : (b + 1) * COLS] = sums_ref[1, b * 256 : (b + 1) * 256, :].astype(F32)
    for h in range(2):
        total = gk_ref[h].astype(F32)
        for t in range(49):
            a, q = t // 7, t % 7
            gk_out[t : t + 1, h * COLS : (h + 1) * COLS] = total[8 * q + a : 8 * q + a + 1]


def halo_scratch():
    return [
        pltpu.VMEM((2, 2, 32, C), BF16),
        pltpu.VMEM((2, 3, COLS, C), BF16),
        pltpu.VMEM((2, 4, 32, C), BF16),
        pltpu.SemaphoreType.DMA((12,)),
        pltpu.SemaphoreType.DMA((12,)),
    ]


def per_device(n_lon, n_lat, ocean_state, land_mask, kernel, w_in, w_out, cotangent):
    n_y, n_z = n_lat // 2, n_lon // 4
    rows_p = HALF // n_y // n_z
    wide = pltpu.VMEM((2, 14, 144, COLS), F32)
    turned_rows = pltpu.VMEM((ROWS, COLS, C), BF16)
    table = pltpu.VMEM((2, 49, 8, COLS), F32)
    sems = lambda n: pltpu.SemaphoreType.DMA((2, n))
    summed = pltpu.VMEM((n_y, n_z, 4, rows_p // 4, COLS), BF16)
    flat = pltpu.VMEM((C * ROWS, COLS), F32)
    field = jax.ShapeDtypeStruct((C, ROWS, COLS), BF16)
    stepped, state, sums, gk = pl.pallas_call(
        functools.partial(whole_kernel, n_lon, n_lat),
        out_shape=(
            field,
            field,
            jax.ShapeDtypeStruct((2, n_y, n_z, 4, rows_p // 4, COLS), BF16),
            jax.ShapeDtypeStruct((2, 64, COLS), BF16),
        ),
        in_specs=[VSPEC] * 6,
        out_specs=(VSPEC,) * 4,
        scratch_shapes=[wide, turned_rows, pltpu.VMEM((2, 64, C), F32)]
        + halo_scratch()
        + [wide, turned_rows]
        + halo_scratch()
        + [
            table,
            table,
            pltpu.VMEM((HID, C), BF16),
            pltpu.VMEM((C, HID), BF16),
            flat,
            flat,
            pltpu.VMEM((2, CELLS, COLS), F32),
            pltpu.VMEM((C, CELLS), F32),
            pltpu.VMEM((C, CELLS), BF16),
            pltpu.VMEM((C, CELLS), BF16),
            pltpu.VMEM((HID, CELLS), BF16),
            pltpu.VMEM((HID, CELLS), BF16),
            pltpu.VMEM((C, CELLS), F32),
            pltpu.VMEM((ROWS, COLS), F32),
            pltpu.VMEM((2 * HALF, COLS), BF16),
            pltpu.VMEM((HALF, COLS), BF16),
            pltpu.VMEM((HALF, COLS), BF16),
            pltpu.VMEM((n_z, n_y, rows_p, COLS), BF16),
            pltpu.VMEM((n_z, rows_p, COLS), BF16),
            pltpu.VMEM((n_z, 4, rows_p // 4, COLS), BF16),
            summed,
            summed,
            pltpu.VMEM((2, 8, 8, COLS), F32),
            pltpu.VMEM((2, 64, COLS), F32),
            pltpu.VMEM((64, COLS), F32),
            pltpu.VMEM((4, 64, COLS), BF16),
            pltpu.VMEM((n_y, 64, COLS), BF16),
            pltpu.VMEM((4, 64, COLS), BF16),
            pltpu.VMEM((n_z, 64, COLS), BF16),
            pltpu.VMEM((2, 64, COLS), BF16),
            sems(1),
            sems(n_z * n_y),
            sems(n_z * 4),
            sems(n_z * 4),
            sems(n_z * n_y),
            sems(n_z * n_y),
            sems(1),
            sems(n_y),
            sems(4),
            sems(n_z),
            sems(1),
        ],
        compiler_params=pltpu.CompilerParams(
            collective_id=0, has_side_effects=True, vmem_limit_bytes=VMEM_LIMIT
        ),
        name="convnext",
    )(ocean_state, land_mask, kernel, w_in, w_out, cotangent)
    return pl.pallas_call(
        finish_kernel,
        out_shape=(
            field,
            field,
            jax.ShapeDtypeStruct((49, C), F32),
            jax.ShapeDtypeStruct((C, HID), F32),
            jax.ShapeDtypeStruct((HID, C), F32),
        ),
        in_specs=[VSPEC] * 4,
        out_specs=(VSPEC,) * 5,
        compiler_params=pltpu.CompilerParams(vmem_limit_bytes=VMEM_LIMIT),
        name="finish",
    )(stepped, state, sums.reshape(2, HALF, COLS), gk)


def solution(mesh):
    return jax.shard_map(
        functools.partial(per_device, mesh.shape["lon"], mesh.shape["lat"]),
        mesh=mesh,
        in_specs=(P(None, "lat", "lon"), P("lat", "lon"), P(), P(), P(), P(None, "lat", "lon")),
        out_specs=(P(None, "lat", "lon"), P(None, "lat", "lon"), P(), P(), P()),
        check_vma=False,
    )
```

```python
import functools

import jax
import jax.numpy as jnp
from jax import lax
from jax.experimental import pallas as pl
from jax.experimental.pallas import tpu as pltpu
from jax.sharding import PartitionSpec as P

F32 = jnp.float32
BF16 = jnp.bfloat16
MESH = pl.DeviceIdType.MESH
TANH_SLOPE = 0.7978845608028654
CUBIC = 0.044715
EPS = 1e-06
C = 256
HID = 1024
ROWS = 8
COLS = 128
CELLS = ROWS * COLS
HALF = 2048
VMEM_LIMIT = 56 * 1024 * 1024
VSPEC = pl.BlockSpec(memory_space=pltpu.VMEM)


def al(value, multiple):
    return pl.multiple_of(value, multiple)


def pick(flag, yes, no):
    return flag * yes + (1 - flag) * no


class Place:
    def __init__(self, n_lon, n_lat):
        self.n_lon, self.n_lat = n_lon, n_lat
        self.lon = lax.axis_index("lon")
        self.lat = lax.axis_index("lat")
        self.crown = (self.lat == n_lat - 1).astype(jnp.int32)
        self.floor = (self.lat == 0).astype(jnp.int32)
        east = lax.rem(self.lon + 1, n_lon)
        west = lax.rem(self.lon + n_lon - 1, n_lon)
        north = pick(self.crown, self.lat, self.lat + 1)
        south = lax.rem(self.lat + n_lat - 1, n_lat)
        mirror = n_lon - 1 - self.lon
        self.west_id = {"lon": west, "lat": self.lat}
        self.east_id = {"lon": east, "lat": self.lat}
        self.north_id = {"lon": pick(self.crown, mirror, self.lon), "lat": north}
        self.south_id = {"lon": self.lon, "lat": south}
        nw = pick(self.crown, lax.rem(n_lon - self.lon, n_lon), west)
        ne = pick(self.crown, lax.rem(2 * n_lon - 2 - self.lon, n_lon), east)
        self.nw_self = (self.crown == 1) & (nw == self.lon)
        self.ne_self = (self.crown == 1) & (ne == self.lon)
        self.nw_id = {"lon": nw, "lat": north}
        self.ne_id = {"lon": ne, "lat": north}
        self.sw_id = {"lon": west, "lat": south}
        self.se_id = {"lon": east, "lat": south}
        self.core = lax.rem(self.lon, 2)
        self.zi = self.lon // 4
        self.yi = self.lat // 2
        self.xi = lax.rem(self.lat, 2) * 2 + lax.rem(self.lon // 2, 2)
        self.n_y, self.n_z = n_lat // 2, n_lon // 4
        self.core_id = {"lon": self.lon + 1 - 2 * self.core, "lat": self.lat}

    def device(self, x, y, z):
        return {"lon": z * 4 + lax.rem(x, 2) * 2 + self.core, "lat": y * 2 + x // 2}

    def x_peer(self, step):
        return self.device(lax.rem(self.xi + step, 4), self.yi, self.zi)

    def z_peer(self, step):
        return self.device(self.xi, self.yi, lax.rem(self.zi + step, self.n_z))

    def y_peer(self, step):
        peer = lax.rem(self.yi + step, self.n_y)
        return peer, self.device(self.xi, peer, self.zi)

    def plane(self, ahead):
        return lax.rem(self.zi + ahead, self.n_z)

    def xz_peer(self, ahead, step):
        x = lax.rem(self.xi + step, 4)
        return x, self.device(x, self.yi, self.plane(ahead))


def signal(barrier, device):
    pl.semaphore_signal(barrier, inc=1, device_id=device, device_id_type=MESH)


def greet_halo(place, barrier):
    for device in (place.west_id, place.east_id, place.north_id):
        signal(barrier, device)

    @pl.when(jnp.logical_not(place.nw_self))
    def _():
        signal(barrier, place.nw_id)

    @pl.when(jnp.logical_not(place.ne_self))
    def _():
        signal(barrier, place.ne_id)

    @pl.when(place.floor == 0)
    def _():
        for device in (place.south_id, place.sw_id, place.se_id):
            signal(barrier, device)

    return (
        5
        - place.nw_self.astype(jnp.int32)
        - place.ne_self.astype(jnp.int32)
        + 3 * (1 - place.floor)
    )


def halo_copies(place, rows_ref, edges, halo_ref, rt_ref, send_sem, recv_sem):
    crown = place.crown

    def remote(src, dst, index, slot, device):
        return pltpu.make_async_remote_copy(
            src_ref=src,
            dst_ref=dst,
            send_sem=send_sem.at[index],
            recv_sem=recv_sem.at[slot],
            device_id=device,
            device_id_type=MESH,
        )

    return [
        remote(edges.at[0], rt_ref.at[1, pl.ds(1, 2)], 0, 0, place.west_id),
        remote(edges.at[1], rt_ref.at[0, pl.ds(1, 2)], 1, 1, place.east_id),
        remote(edges.at[0, 1], rt_ref.at[1 - crown, 3 * crown], 2, 2 + 3 * crown, place.nw_id),
        remote(edges.at[1, 1], rt_ref.at[crown, 3 * crown], 3, 3 + crown, place.ne_id),
        remote(edges.at[0, 0], rt_ref.at[1, 3], 4, 4, place.sw_id),
        remote(edges.at[1, 0], rt_ref.at[0, 3], 5, 5, place.se_id),
    ] + [
        remote(rows_ref.at[7 - k], halo_ref.at[crown, k], 6 + k, 6 + k + 3 * crown, place.north_id)
        for k in range(3)
    ] + [
        remote(rows_ref.at[k], halo_ref.at[1, k], 9 + k, 9 + k, place.south_id) for k in range(3)
    ]


def halo_start(place, copies, edges, rt_ref, recv_sem):
    copies[0].start()
    copies[1].start()
    for is_self, index, side, slot in ((place.nw_self, 2, 0, 5), (place.ne_self, 3, 1, 4)):

        @pl.when(is_self)
        def _(side=side, slot=slot):
            pltpu.make_async_copy(edges.at[side, 1], rt_ref.at[side, 3], recv_sem.at[slot]).start()

        @pl.when(jnp.logical_not(is_self))
        def _(index=index):
            copies[index].start()

    @pl.when(place.floor == 0)
    def _():
        copies[4].start()
        copies[5].start()


def row_start(place, copies, k):
    copies[6 + k].start()

    @pl.when(place.floor == 0)
    def _():
        copies[9 + k].start()


def wait_bytes(ref, sem):
    pltpu.make_async_copy(ref, ref, sem).wait()


def rim_wait(place, rt_ref, recv_sem):
    wait_bytes(rt_ref.at[1, pl.ds(1, 2)], recv_sem.at[0])
    wait_bytes(rt_ref.at[0, pl.ds(1, 2)], recv_sem.at[1])
    wait_bytes(rt_ref.at[1, 3], recv_sem.at[4])
    wait_bytes(rt_ref.at[0, 3], recv_sem.at[5])

    @pl.when(place.floor == 0)
    def _():
        wait_bytes(rt_ref.at[1, 0], recv_sem.at[2])
        wait_bytes(rt_ref.at[0, 0], recv_sem.at[3])


def row_wait(place, k, halo_ref, recv_sem):
    wait_bytes(halo_ref.at[1, k], recv_sem.at[9 + k])

    @pl.when(place.floor == 0)
    def _():
        wait_bytes(halo_ref.at[0, k], recv_sem.at[6 + k])


def halo_sent(place, copies):
    for index in (0, 1, 6, 7, 8):
        copies[index].wait_send()

    @pl.when(place.floor == 0)
    def _():
        for index in (4, 5, 9, 10, 11):
            copies[index].wait_send()

    for is_self, index in ((place.nw_self, 2), (place.ne_self, 3)):

        @pl.when(jnp.logical_not(is_self))
        def _(index=index):
            copies[index].wait_send()


NT = (((1,), (1,)), ((), ()))


def square(n, rule):
    source = lax.broadcasted_iota(jnp.int32, (n, n), 0)
    target = lax.broadcasted_iota(jnp.int32, (n, n), 1)
    return jnp.where(rule(source, target), 1.0, 0.0).astype(BF16)


def lay_row(i, row, ident, wide, rows_t, edge_f):
    turned = lax.dot_general(ident, row, NT, preferred_element_type=F32)
    wide[0, 3 + i, 8:136, :] = turned[:, :COLS]
    wide[1, 3 + i, 8:136, :] = turned[:, COLS:]
    rows_t[i] = turned.astype(BF16)
    edge_f[0, 8 * i : 8 * i + 8, :] = turned[:8]
    edge_f[1, 8 * i : 8 * i + 8, :] = turned[120:]


def lay_edges(edge_f, edges):
    for side in range(2):
        for b in range(2):
            edges[side, b] = edge_f[side, 32 * b : 32 * b + 32, :].astype(BF16)


def unpack_rim(place, rt_ref, wide):
    crown = place.crown == 1
    turn = square(32, lambda s, t: jnp.where(crown, 31 - s, s) == t)
    for side in range(2):
        at = slice(136 * side, 136 * side + 8)
        for b in range(4):
            if b == 3:
                block = jnp.dot(turn, rt_ref[side, b], preferred_element_type=F32)
            else:
                block = rt_ref[side, b].astype(F32)
            if b == 0:
                block = jnp.where(place.floor == 1, 0.0, block)
            for s in range(4):
                r = 4 * b + s - 1
                if 0 <= r < 14:
                    for h in range(2):
                        wide[h, r, at, :] = block[8 * s : 8 * s + 8, h * COLS : (h + 1) * COLS]


def unpack_row(place, k, halo_ref, wide):
    crown = place.crown == 1
    turn = square(COLS, lambda s, t: jnp.where(crown, COLS - 1 - s, s) == t)
    south = jnp.where(place.floor == 1, 0.0, halo_ref[0, k].astype(F32))
    north = jnp.dot(turn, halo_ref[1, k], preferred_element_type=F32)
    for h in range(2):
        wide[h, 2 - k, 8:136, :] = south[:, h * COLS : (h + 1) * COLS]
        wide[h, 11 + k, 8:136, :] = north[:, h * COLS : (h + 1) * COLS]


LOCAL_ROWS = tuple(range(3, 11))
HALO_ROWS = (0, 1, 2, 11, 12, 13)
PLACE = (6, 4, 2, 0, 1, 3, 5, 7)


def conv_block(wide, weight, out_ref, h, j, rows, add):
    at = [pl.ds(al(i * COLS + j * 8, 8), 8) for i in range(ROWS)]
    reached = [i for i in range(ROWS) if any(0 <= r - i < 7 for r in rows)]
    total = {i: out_ref[h, at[i], :] if add else None for i in reached}
    for q in range(7):
        for r in rows:
            moved = wide[h, r, pl.ds(j * 8 + (q + 5), 8), :]
            for a in range(7):
                i = r - a
                if 0 <= i < ROWS:
                    term = weight(h, a, q, r) * moved
                    total[i] = term if total[i] is None else total[i] + term
    for i in reached:
        out_ref[h, at[i], :] = total[i]


def conv_inner(wide, weight, out_ref, h):
    def body(n, _):
        conv_block(wide, weight, out_ref, h, n + 1, LOCAL_ROWS, False)
        return 0

    lax.fori_loop(0, 14, body, 0)


def conv_rim(wide, weight, out_ref):
    def body(n, _):
        conv_block(wide, weight, out_ref, n // 2, 15 * lax.rem(n, 2), LOCAL_ROWS, False)
        return 0

    lax.fori_loop(0, 4, body, 0)


def conv_halo(wide, weight, out_ref, rows):
    def body(j, _):
        for h in range(2):
            conv_block(wide, weight, out_ref, h, j, rows, True)
        return 0

    lax.fori_loop(0, 16, body, 0)


def tap_sums(wide, g_wide, out_ref):
    row_id = lax.broadcasted_iota(jnp.int32, (8, COLS), 0)

    def body(n, _):
        h, q = n // 7, lax.rem(n, 7)
        total = [None] * 7
        for j in range(16):
            grads = [g_wide[h, 3 + i, 8 + 8 * j : 16 + 8 * j, :] for i in range(ROWS)]
            for r in range(14):
                moved = wide[h, r, pl.ds(q + (8 * j + 5), 8), :]
                for a in range(7):
                    i = r - a
                    if 0 <= i < ROWS:
                        term = grads[i] * moved
                        total[a] = term if total[a] is None else total[a] + term
        tile = jnp.zeros((8, COLS), F32)
        for a in range(7):
            tile = jnp.where(row_id == a, jnp.sum(total[a], axis=0, keepdims=True), tile)
        out_ref[h, q] = tile
        return 0

    lax.fori_loop(0, 14, body, 0)
    for h in range(2):
        out_ref[h, 7] = jnp.zeros((8, COLS), F32)


def whole_kernel(
    n_lon, n_lat,
    x_ref, mask_ref, taps_ref, w_in_ref, w_out_ref, cot_ref,
    stepped_ref, state_ref, sums_ref, gk_out,
    wide, rows_t, edge_f, edges, halo, rt, send_sem, recv_sem,
    g_wide, g_rows, g_edges, g_halo, g_rt, g_send, g_recv,
    taps, taps_n, w_in_t, w_out_t, flat, flat2, conv_t, x_hat_ref, normed, gb, act, g_pre, g_norm, inv_ref,
    grads, pair_in, mine, y_in, part, xz_in, done, sums,
    tap_acc, gk, gk_pair, gk_mine, gk_y, gk_x, gk_z, gk_all,
    core_sems, y_sems, xz_sems, xzg_sems, yg_sems, last_sems, gk_core, gk_y_sems, gk_x_sems, gk_z_sems, gk_last_sems,
):
    place = Place(n_lon, n_lat)
    n_y, n_z = place.n_y, place.n_z
    rows_p = HALF // n_y // n_z
    rows_x = rows_p // 4
    near = sorted(range(n_z), key=lambda ahead: min(ahead, n_z - ahead))
    far = near[::-1]
    core, other = place.core, 1 - place.core

    barrier = pltpu.get_barrier_semaphore()
    def greet_y(step, _):
        signal(barrier, place.y_peer(step)[1])
        return 0

    def greet_xz(n, _):
        signal(barrier, place.xz_peer(n // 4, lax.rem(n, 4))[1])
        return 0

    lax.fori_loop(1, 4 * n_z, greet_xz, 0)
    lax.fori_loop(1, n_y, greet_y, 0)
    count = greet_halo(place, barrier)
    signal(barrier, place.core_id)

    ident = square(COLS, lambda s, t: s == t)
    flat[...] = x_ref[...].astype(F32).reshape(C * ROWS, COLS)
    for i in range(ROWS):
        lay_row(i, flat[pl.ds(i, C, stride=8), :].astype(BF16), ident, wide, rows_t, edge_f)
    lay_edges(edge_f, edges)
    w_in_t[...] = w_in_ref[...].astype(F32).T.astype(BF16)
    w_out_t[...] = w_out_ref[...].astype(F32).T.astype(BF16)
    pl.semaphore_wait(barrier, count + n_y + 4 * n_z - 1)
    copies = halo_copies(place, rows_t, edges, halo, rt, send_sem, recv_sem)
    halo_start(place, copies, edges, rt, recv_sem)
    row_start(place, copies, 0)

    crown = place.crown == 1
    table = taps_ref[...].astype(F32)
    for t in range(49):
        for h in range(2):
            taps[h, t] = jnp.broadcast_to(table[t : t + 1, h * COLS : (h + 1) * COLS], (8, COLS))
    for t in range(28, 49):
        for h in range(2):
            taps_n[h, t] = jnp.where(crown, taps[h, t], taps[h, 48 - t])

    def forward(h, a, q, r):
        return taps[h, 7 * a + q]

    def backward(h, a, q, r):
        return taps_n[h, 7 * a + q] if r >= 11 else taps[h, 48 - 7 * a - q]

    for h in range(2):
        conv_inner(wide, forward, conv_t, h)
        row_start(place, copies, 1 + h)
    flat[...] = cot_ref[...].astype(F32).reshape(C * ROWS, COLS)
    for r in range(ROWS):
        ocean = mask_ref[pl.ds(r, 1), :].astype(F32)
        gb[:, PLACE[r] * COLS : (PLACE[r] + 1) * COLS] = (ocean * flat[pl.ds(r, C, stride=8), :]).astype(BF16)

    rim_wait(place, rt, recv_sem)
    unpack_rim(place, rt, wide)
    conv_rim(wide, forward, conv_t)

    def cells_body(n, _):
        for k in range(3):

            @pl.when(n == k + 1)
            def _(k=k):
                row_wait(place, k, halo, recv_sem)
                unpack_row(place, k, halo, wide)
                conv_halo(wide, forward, conv_t, (2 - k, 11 + k))

        at = pl.ds(al(n * 256, 256), 256)
        pair = (3 - n, 4 + n)
        for k, r in enumerate(pair):
            row_at = pl.ds(al(r * COLS, COLS), COLS)
            value = jnp.concatenate([conv_t[0, row_at, :].T, conv_t[1, row_at, :].T], axis=0)
            centred = value - jnp.sum(value, axis=0, keepdims=True) * (1.0 / C)
            var = jnp.sum(centred * centred, axis=0, keepdims=True) * (1.0 / C)
            inv = lax.rsqrt(var + EPS)
            inv_ref[pl.ds(r, 1), :] = inv
            x_hat = centred * inv
            x_hat_ref[:, pl.ds(al(n * 256 + k * COLS, COLS), COLS)] = x_hat
            normed[:, pl.ds(al(n * 256 + k * COLS, COLS), COLS)] = x_hat.astype(BF16)
        hat = normed[:, at]
        grad = gb[:, at]
        for h in range(4):
            hs = slice(h * 256, (h + 1) * 256)
            u = jnp.dot(w_in_t[hs, :], hat, preferred_element_type=F32)
            uu = u * u
            t = jnp.tanh(TANH_SLOPE * (u + CUBIC * (uu * u)))
            gate = 0.5 * (1.0 + t)
            act[hs, at] = (u * gate).astype(BF16)
            slope = gate + (0.5 * TANH_SLOPE) * u * (1.0 - t * t) * (1.0 + (3.0 * CUBIC) * uu)
            g_act = jnp.dot(w_out_ref[hs, :], grad, preferred_element_type=F32)
            g_pre[hs, at] = (g_act * slope).astype(BF16)
        return 0

    lax.fori_loop(0, ROWS // 2, cells_body, 0)

    for h in range(4):
        hs = slice(h * 256, (h + 1) * 256)
        out = lax.dot_general(act[hs, :], gb[...], NT, preferred_element_type=F32).astype(BF16)
        grads[h * 256 : (h + 1) * 256, :] = out[:, :COLS]
        grads[1024 + h * 256 : 1024 + (h + 1) * 256, :] = out[:, COLS:]
    for h in range(4):
        hs = slice(h * 256, (h + 1) * 256)
        out = lax.dot_general(normed[...], g_pre[hs, :], NT, preferred_element_type=F32).astype(BF16)
        grads[HALF + h * 512 : HALF + h * 512 + 256, :] = out[:, :COLS]
        grads[HALF + h * 512 + 256 : HALF + (h + 1) * 512, :] = out[:, COLS:]

    def remote(src, dst, sems, index, device):
        return pltpu.make_async_remote_copy(
            src_ref=src, dst_ref=dst, send_sem=sems.at[0, index], recv_sem=sems.at[1, index],
            device_id=device, device_id_type=MESH,
        )

    def each(n, make, act):
        def run(step, _):
            act(make(step))
            return 0

        lax.fori_loop(1, n, run, 0)

    def start(copy):
        copy.start()

    def wait(copy):
        copy.wait()

    def sent(copy):
        copy.wait_send()

    first = remote(grads.at[pl.ds(al(other * HALF, HALF), HALF)], pair_in, core_sems, 0, place.core_id)
    first.start()

    def norm_body(n, _):
        at = pl.ds(al(n * 256, 256), 256)
        g_norm[:, at] = jnp.dot(w_in_ref[...], g_pre[:, at], preferred_element_type=F32)
        return 0

    lax.fori_loop(0, ROWS // 2, norm_body, 0)
    for r in range(ROWS):
        at = slice(PLACE[r] * COLS, (PLACE[r] + 1) * COLS)
        grad, x_hat = g_norm[:, at], x_hat_ref[:, at]
        mean = jnp.sum(grad, axis=0, keepdims=True) * (1.0 / C)
        proj = jnp.sum(grad * x_hat, axis=0, keepdims=True) * (1.0 / C)
        g_conv = inv_ref[pl.ds(r, 1), :] * (grad - mean - x_hat * proj)
        lay_row(r, g_conv.astype(BF16), ident, g_wide, g_rows, edge_f)
    lay_edges(edge_f, g_edges)
    g_copies = halo_copies(place, g_rows, g_edges, g_halo, g_rt, g_send, g_recv)

    first.wait()

    def add_pair(i, _):
        at = pl.ds(al(i * 256, 256), 256)
        own = grads[pl.ds(al(core * HALF + i * 256, 256), 256), :].astype(F32)
        mine[at, :] = (own + pair_in[at, :].astype(F32)).astype(BF16)
        return 0

    lax.fori_loop(0, HALF // 256, add_pair, 0)

    def y_copy(ahead, step):
        peer, device = place.y_peer(step)
        row = (peer * n_z + place.plane(ahead)) * rows_p
        return remote(mine.at[pl.ds(al(row, rows_p), rows_p)], y_in.at[ahead, step], y_sems, ahead * n_y + step, device)

    def plane_steps(ahead):
        return range(1 if ahead == 0 else 0, 4)

    for ahead in far:
        for step in range(1, n_y):
            y_copy(ahead, step).start()

    halo_start(place, g_copies, g_edges, g_rt, g_recv)
    for k in range(3):
        row_start(place, g_copies, k)

    tap_sums(wide, g_wide, tap_acc)
    for h in range(2):
        gk[h] = tap_acc[h].reshape(64, COLS)
    first_k = remote(gk.at[other], gk_pair, gk_core, 0, place.core_id)
    first_k.start()

    def xz_copy(ahead, step):
        x, device = place.xz_peer(ahead, step)
        src = part.at[ahead, pl.ds(al(x * rows_x, rows_x), rows_x)]
        return remote(src, xz_in.at[ahead, step], xz_sems, ahead * 4 + step, device)

    for ahead in far:
        for step in range(1, n_y):
            y_copy(ahead, step).wait()
        own = pl.ds(al((place.yi * n_z + place.plane(ahead)) * rows_p, rows_p), rows_p)
        total = mine[own, :].astype(F32)
        for step in range(1, n_y):
            total = total + y_in[ahead, step].astype(F32)
        part[ahead] = total.astype(BF16)
        for step in plane_steps(ahead):
            xz_copy(ahead, step).start()

    conv_inner(g_wide, backward, conv_t, 0)

    first_k.wait()
    gk_mine[0] = (gk[core] + gk_pair[...]).astype(BF16)

    def gk_round(k, n, peer_of, slots, sems):
        def copy(step):
            return remote(gk_mine.at[k], slots.at[step], sems, step, peer_of(step))

        def finish():
            each(n, copy, wait)
            total = gk_mine[k].astype(F32)
            for step in range(1, n):
                total = total + slots[step].astype(F32)
            gk_mine[k + 1] = total.astype(BF16)

        each(n, copy, start)
        return finish

    gk_finish = gk_round(0, n_y, lambda step: place.y_peer(step)[1], gk_y, gk_y_sems)

    for ahead in near:
        for step in plane_steps(ahead):
            xz_copy(ahead, step).wait()
    total = part[0, pl.ds(al(place.xi * rows_x, rows_x), rows_x), :].astype(F32)
    for ahead in near:
        for step in plane_steps(ahead):
            total = total + xz_in[ahead, step].astype(F32)
    done[place.yi, place.zi, place.xi] = total.astype(BF16)

    def xzg_copy(ahead, step):
        _, device = place.xz_peer(ahead, step)
        own = done.at[place.yi, place.zi, place.xi]
        return remote(own, own, xzg_sems, ahead * 4 + step, device)

    for ahead in far:
        for step in plane_steps(ahead):
            xzg_copy(ahead, step).start()
    gk_finish()
    gk_finish = gk_round(1, 4, place.x_peer, gk_x, gk_x_sems)

    conv_inner(g_wide, backward, conv_t, 1)

    def branch_body(n, _):
        branch = jnp.dot(w_out_t[...], act[:, pl.ds(al(n * 256, 256), 256)], preferred_element_type=F32)
        for k, r in enumerate((3 - n, 4 + n)):
            ocean = mask_ref[pl.ds(r, 1), :].astype(F32)
            flat[pl.ds(r, C, stride=8), :] = ocean * branch[:, k * COLS : (k + 1) * COLS]
        return 0

    lax.fori_loop(0, ROWS // 2, branch_body, 0)

    rim_wait(place, g_rt, g_recv)
    unpack_rim(place, g_rt, g_wide)
    conv_rim(g_wide, backward, conv_t)

    def behind(ahead):
        return lax.rem(place.zi + n_z - ahead, n_z)

    def yg_copy(ahead, step):
        _, device = place.y_peer(step)
        own = done.at[place.yi, behind(ahead)]
        return remote(own, own, yg_sems, ahead * n_y + step, device)

    def across(ahead, step, y):
        whole = done.at[y, behind(ahead)], sums.at[y, behind(ahead)]
        return remote(*whole, last_sems, ahead * n_y + step, place.core_id)

    for ahead in near:
        for step in plane_steps(ahead):
            x = lax.rem(place.xi + 4 - step, 4)
            wait_bytes(done.at[place.yi, behind(ahead), x], xzg_sems.at[1, ahead * 4 + step])
        for step in range(1, n_y):
            yg_copy(ahead, step).start()
        across(ahead, 0, place.yi).start()

    gk_finish()
    gk_finish = gk_round(2, n_z, place.z_peer, gk_z, gk_z_sems)
    for k in range(3):
        row_wait(place, k, g_halo, g_recv)
        unpack_row(place, k, g_halo, g_wide)
    conv_halo(g_wide, backward, conv_t, HALO_ROWS)
    for r in range(ROWS):
        at = slice(r * COLS, (r + 1) * COLS)
        flat2[pl.ds(r, C, stride=8), :] = jnp.concatenate([conv_t[0, at, :].T, conv_t[1, at, :].T], axis=0)

    def out_body(group, _):
        at = pl.ds(group * 32, 32)
        rows_at = pl.ds(al(group * 256, 256), 256)
        moved = flat[rows_at, :].reshape(32, ROWS, COLS)
        stepped_ref[at] = (x_ref[at].astype(F32) + moved).astype(BF16)
        moved = flat2[rows_at, :].reshape(32, ROWS, COLS)
        state_ref[at] = (cot_ref[at].astype(F32) + moved).astype(BF16)
        return 0

    lax.fori_loop(0, C // 32, out_body, 0)

    for ahead in near:
        for step in range(1, n_y):
            y = lax.rem(place.yi + n_y - step, n_y)
            wait_bytes(done.at[y, behind(ahead)], yg_sems.at[1, ahead * n_y + step])
            across(ahead, step, y).start()

    gk_finish()
    gk_all[core] = gk_mine[3]
    last_k = remote(gk_all.at[core], gk_all.at[core], gk_last_sems, 0, place.core_id)
    last_k.start()

    wait_bytes(gk_all.at[core], gk_last_sems.at[0, 0])
    wait_bytes(gk_all.at[other], gk_last_sems.at[1, 0])
    gk_out[...] = gk_all[...]
    sums_ref[core] = done[...]

    for ahead in near:
        for step in range(n_y):
            y = lax.rem(place.yi + n_y - step, n_y)
            wait_bytes(done.at[y, behind(ahead)], last_sems.at[0, ahead * n_y + step])
            wait_bytes(sums.at[y, behind(ahead)], last_sems.at[1, ahead * n_y + step])
    sums_ref[other] = sums[...]

    for ahead in near:
        for step in plane_steps(ahead):
            xzg_copy(ahead, step).wait_send()
        for step in range(1, n_y):
            yg_copy(ahead, step).wait_send()
    halo_sent(place, copies)
    halo_sent(place, g_copies)


def finish_kernel(stepped_in, state_in, sums_ref, gk_ref, stepped_ref, state_ref, gk_out, gin_ref, gout_ref):
    stepped_ref[...] = stepped_in[...]
    state_ref[...] = state_in[...]
    for b in range(2):
        gout_ref[:, b * COLS : (b + 1) * COLS] = sums_ref[0, b * 1024 : (b + 1) * 1024, :].astype(F32)
    for b in range(8):
        gin_ref[:, b * COLS : (b + 1) * COLS] = sums_ref[1, b * 256 : (b + 1) * 256, :].astype(F32)
    for h in range(2):
        total = gk_ref[h].astype(F32)
        for t in range(49):
            a, q = t // 7, t % 7
            gk_out[t : t + 1, h * COLS : (h + 1) * COLS] = total[8 * q + a : 8 * q + a + 1]


def halo_scratch():
    return [
        pltpu.VMEM((2, 2, 32, C), BF16),
        pltpu.VMEM((2, 3, COLS, C), BF16),
        pltpu.VMEM((2, 4, 32, C), BF16),
        pltpu.SemaphoreType.DMA((12,)),
        pltpu.SemaphoreType.DMA((12,)),
    ]


def per_device(n_lon, n_lat, ocean_state, land_mask, kernel, w_in, w_out, cotangent):
    n_y, n_z = n_lat // 2, n_lon // 4
    rows_p = HALF // n_y // n_z
    wide = pltpu.VMEM((2, 14, 144, COLS), F32)
    turned_rows = pltpu.VMEM((ROWS, COLS, C), BF16)
    table = pltpu.VMEM((2, 49, 8, COLS), F32)
    sems = lambda n: pltpu.SemaphoreType.DMA((2, n))
    summed = pltpu.VMEM((n_y, n_z, 4, rows_p // 4, COLS), BF16)
    flat = pltpu.VMEM((C * ROWS, COLS), F32)
    field = jax.ShapeDtypeStruct((C, ROWS, COLS), BF16)
    stepped, state, sums, gk = pl.pallas_call(
        functools.partial(whole_kernel, n_lon, n_lat),
        out_shape=(
            field,
            field,
            jax.ShapeDtypeStruct((2, n_y, n_z, 4, rows_p // 4, COLS), BF16),
            jax.ShapeDtypeStruct((2, 64, COLS), BF16),
        ),
        in_specs=[VSPEC] * 6,
        out_specs=(VSPEC,) * 4,
        scratch_shapes=[wide, turned_rows, pltpu.VMEM((2, 64, C), F32)]
        + halo_scratch()
        + [wide, turned_rows]
        + halo_scratch()
        + [
            table,
            table,
            pltpu.VMEM((HID, C), BF16),
            pltpu.VMEM((C, HID), BF16),
            flat,
            flat,
            pltpu.VMEM((2, CELLS, COLS), F32),
            pltpu.VMEM((C, CELLS), F32),
            pltpu.VMEM((C, CELLS), BF16),
            pltpu.VMEM((C, CELLS), BF16),
            pltpu.VMEM((HID, CELLS), BF16),
            pltpu.VMEM((HID, CELLS), BF16),
            pltpu.VMEM((C, CELLS), F32),
            pltpu.VMEM((ROWS, COLS), F32),
            pltpu.VMEM((2 * HALF, COLS), BF16),
            pltpu.VMEM((HALF, COLS), BF16),
            pltpu.VMEM((HALF, COLS), BF16),
            pltpu.VMEM((n_z, n_y, rows_p, COLS), BF16),
            pltpu.VMEM((n_z, rows_p, COLS), BF16),
            pltpu.VMEM((n_z, 4, rows_p // 4, COLS), BF16),
            summed,
            summed,
            pltpu.VMEM((2, 8, 8, COLS), F32),
            pltpu.VMEM((2, 64, COLS), F32),
            pltpu.VMEM((64, COLS), F32),
            pltpu.VMEM((4, 64, COLS), BF16),
            pltpu.VMEM((n_y, 64, COLS), BF16),
            pltpu.VMEM((4, 64, COLS), BF16),
            pltpu.VMEM((n_z, 64, COLS), BF16),
            pltpu.VMEM((2, 64, COLS), BF16),
            sems(1),
            sems(n_z * n_y),
            sems(n_z * 4),
            sems(n_z * 4),
            sems(n_z * n_y),
            sems(n_z * n_y),
            sems(1),
            sems(n_y),
            sems(4),
            sems(n_z),
            sems(1),
        ],
        compiler_params=pltpu.CompilerParams(
            collective_id=0, has_side_effects=True, vmem_limit_bytes=VMEM_LIMIT
        ),
        name="convnext",
    )(ocean_state, land_mask, kernel, w_in, w_out, cotangent)
    return pl.pallas_call(
        finish_kernel,
        out_shape=(
            field,
            field,
            jax.ShapeDtypeStruct((49, C), F32),
            jax.ShapeDtypeStruct((C, HID), F32),
            jax.ShapeDtypeStruct((HID, C), F32),
        ),
        in_specs=[VSPEC] * 4,
        out_specs=(VSPEC,) * 5,
        compiler_params=pltpu.CompilerParams(vmem_limit_bytes=VMEM_LIMIT),
        name="finish",
    )(stepped, state, sums.reshape(2, HALF, COLS), gk)


def solution(mesh):
    return jax.shard_map(
        functools.partial(per_device, mesh.shape["lon"], mesh.shape["lat"]),
        mesh=mesh,
        in_specs=(P(None, "lat", "lon"), P("lat", "lon"), P(), P(), P(), P(None, "lat", "lon")),
        out_specs=(P(None, "lat", "lon"), P(None, "lat", "lon"), P(), P(), P()),
        check_vma=False,
    )
```
